32 devices in a mesh: src: 4 (over y, core), tgt: 8 (over z, x).
Axes of the slice: x: 2, y: 2, z: 4, core: 2. Of those that a mesh axis runs over, the one named last changes fastest.
Arguments:
- source: bfloat16 [8192, 128], P('src'), may hold values from -6 to 6
- target: bfloat16 [8192, 128], P('tgt'), may hold values from -5 to 5
- start_map: float32 [128, 128], replicated, may hold values from -1 to 1
- warm_potential: float32 [8192], P('tgt'), may hold values from -60 to 24
Outputs:
- row_potential: float32 [8192], P('src')
- col_potential: float32 [8192], P('tgt')
- new_map: float32 [128, 128], replicated
The draws below stay inside these ranges and needn't reach their ends.
All inputs are finite; a program needn't handle non-finite values.
Results may differ from the reference program's by a relative error of at most 0.0078.
Values sent between devices are 32-bit elements; how exact they have to be, the bound alone decides.
No kernel may reach another device: no remote copies, remote signals or barrier semaphores. Data moves between devices by JAX's collectives and lax.ppermute only.
A program may use at most 64 MiB of HBM per device.

```python
import math
import jax
import jax.numpy as jnp
from jax import lax

D = 128
ROUNDS = 3
NEWTON = 10
NS = 8192
NT = 8192


def butterfly(key):
    matrix = jnp.eye(D, dtype=jnp.float32)
    stride = 1
    section_index = 0
    while stride < D:
        angles = jax.random.uniform(jax.random.fold_in(key, section_index), (D // (2 * stride), stride, 1), jnp.float32, -math.pi, math.pi)
        cosine = jnp.cos(angles)
        sine_vals = jnp.sin(angles)
        shaped = matrix.reshape(D // (2 * stride), 2, stride, D)
        upper_rows = shaped[:, 0]
        lower_rows = shaped[:, 1]
        new_upper = cosine * upper_rows - sine_vals * lower_rows
        new_lower = sine_vals * upper_rows + cosine * lower_rows
        matrix = jnp.stack([new_upper, new_lower], axis=1).reshape(D, D)
        stride = stride * 2
        section_index = section_index + 1
    row_order = jax.random.permutation(jax.random.fold_in(key, 99), D)
    return matrix[row_order]


def faint_rows(key):
    spacing = NT // 16
    offsets = jax.random.randint(jax.random.fold_in(key, 21), (16,), 2, spacing)
    return jnp.arange(16, dtype=jnp.int32) * spacing + offsets


def joint(key):
    rotation = butterfly(jax.random.fold_in(key, 11))
    source_key = jax.random.fold_in(key, 12)
    target_key = jax.random.fold_in(key, 13)
    source = jnp.clip(jax.random.normal(source_key, (NS, D), jnp.float32), -5.0, 5.0)
    target = jnp.clip(jax.random.normal(target_key, (NT, D), jnp.float32), -5.0, 5.0)
    faint = faint_rows(key)
    target = target.at[faint].multiply(0.02)
    return (source, target, rotation)


def draw_source(key, part):
    return joint(key)[0].astype(jnp.bfloat16)


def draw_target(key, part):
    return joint(key)[1].astype(jnp.bfloat16)


def draw_start_map(key, part):
    return joint(key)[2]


def draw_warm_potential(key, part):
    faint = faint_rows(key)
    key = jax.random.fold_in(key, 5)
    values = jnp.clip(4.0 * jax.random.normal(key, (NT,), jnp.float32), -24.0, 24.0)
    return values.at[faint].set(-60.0)


def setup_inputs(seed: int = 0) -> dict:
    key_list = jax.random.split(jax.random.key(seed), 5)
    return {
        "source": draw_source(jax.random.fold_in(key_list[4], 71), 0),
        "target": draw_target(jax.random.fold_in(key_list[4], 71), 0),
        "start_map": draw_start_map(jax.random.fold_in(key_list[4], 71), 0),
        "warm_potential": draw_warm_potential(jax.random.fold_in(key_list[4], 71), 0),
    }


EPS = 0.05

def row_lse_all(rotated, target, col_pot, score_scale):
    row_count = rotated.shape[0]
    block_rows = math.gcd(row_count, 512)
    blocks = rotated.reshape(row_count // block_rows, block_rows, rotated.shape[1])

    def one_block(row_block):
        scores = jnp.dot(row_block, target.T, preferred_element_type=jnp.float32) * score_scale + col_pot[None, :]
        return jax.nn.logsumexp(scores, axis=1)
    return lax.map(one_block, blocks).reshape(row_count)

def col_lse_all(rotated, target, row_pot, score_scale):
    row_count = rotated.shape[0]
    block_rows = math.gcd(row_count, 512)
    blocks = rotated.reshape(row_count // block_rows, block_rows, rotated.shape[1])
    pots = row_pot.reshape(row_count // block_rows, block_rows)

    def one_block(inputs):
        row_block, pot_block = inputs
        scores = jnp.dot(row_block, target.T, preferred_element_type=jnp.float32) * score_scale + pot_block[:, None]
        return jax.nn.logsumexp(scores, axis=0)
    return jax.nn.logsumexp(lax.map(one_block, (blocks, pots)), axis=0)

def covariance(source, rotated, target, col_pot, row_lse, score_scale):
    row_count = rotated.shape[0]
    block_rows = math.gcd(row_count, 512)
    nblocks = row_count // block_rows
    width = rotated.shape[1]

    def one_block(inputs):
        source_block, row_block, lse_block = inputs
        scores = jnp.dot(row_block, target.T, preferred_element_type=jnp.float32) * score_scale + col_pot[None, :] - lse_block[:, None]
        weights = jnp.exp(scores).astype(jnp.bfloat16)
        bary = jnp.dot(weights, target, preferred_element_type=jnp.float32)
        return jnp.dot(source_block.astype(jnp.float32).T, bary, precision=lax.Precision.HIGHEST)
    parts_sum = lax.map(one_block, (source.reshape(nblocks, block_rows, width), rotated.reshape(nblocks, block_rows, width), row_lse.reshape(nblocks, block_rows)))
    return lax.optimization_barrier(jnp.sum(parts_sum, axis=0))

def polar(matrix):
    iterate = matrix / jnp.sqrt(jnp.sum(matrix * matrix) + 1e-06)
    for newton_index in range(NEWTON):
        gram_matrix = jnp.dot(iterate.T, iterate, precision=lax.Precision.HIGHEST)
        iterate = 1.5 * iterate - 0.5 * jnp.dot(iterate, gram_matrix, precision=lax.Precision.HIGHEST)
    return iterate

def reference(source, target, start_map, warm_potential):
    score_scale = 1.0 / (math.sqrt(D) * EPS)
    rotated = jnp.dot(source, start_map.astype(jnp.bfloat16), preferred_element_type=jnp.float32).astype(jnp.bfloat16)
    col_pot = warm_potential
    for round_index in range(ROUNDS):
        row_pot = -math.log(NS) - row_lse_all(rotated, target, col_pot, score_scale)
        col_pot = -math.log(NT) - col_lse_all(rotated, target, row_pot, score_scale)
    row_lse = row_lse_all(rotated, target, col_pot, score_scale)
    row_pot = -math.log(NS) - row_lse
    new_map = polar(covariance(source, rotated, target, col_pot, row_lse, score_scale))
    return (EPS * row_pot, EPS * col_pot, new_map)
```

```python
import functools
import math

import jax
import jax.numpy as jnp
from jax import lax
from jax.experimental import pallas as pl
from jax.experimental.pallas import tpu as pltpu
from jax.sharding import PartitionSpec as P

NEWTON = 10
EPS = 0.05
LANES = 128
VMEM_LIMIT = 40 * 1024 * 1024

F32 = jnp.float32
BF16 = jnp.bfloat16


def call(body, name, out_shape, scratch=(), flops=0):
    space = pl.BlockSpec(memory_space=pltpu.VMEM)
    return lambda *args: pl.pallas_call(
        body,
        name=name,
        out_shape=out_shape,
        in_specs=[space] * len(args),
        out_specs=jax.tree.map(lambda _: space, out_shape),
        scratch_shapes=scratch,
        compiler_params=pltpu.CompilerParams(vmem_limit_bytes=VMEM_LIMIT),
        cost_estimate=pl.CostEstimate(flops=flops, bytes_accessed=8 << 20, transcendentals=0),
    )(*args)


def eye_mask():
    shape = (LANES, LANES)
    return lax.broadcasted_iota(jnp.int32, shape, 0) == lax.broadcasted_iota(jnp.int32, shape, 1)


def to_lanes(column):
    wide = jnp.broadcast_to(column, (LANES, LANES))
    return jnp.sum(jnp.where(eye_mask(), wide, 0.0), axis=0, keepdims=True)


def to_column(row):
    wide = jnp.broadcast_to(row, (LANES, LANES))
    return jnp.sum(jnp.where(eye_mask(), wide, 0.0), axis=1, keepdims=True)


def split(x):
    high = x.astype(BF16)
    return high, (x - high.astype(F32)).astype(BF16)


def tree(combine, values):
    values = list(values)
    while len(values) > 1:
        values = [combine(a, b) for a, b in zip(values[::2], values[1::2])]
    return values[0]


def tree_sum(refs):
    return tree(jnp.add, [ref[...] for ref in refs])


def tree_lse(refs):
    parts = [ref[...] for ref in refs]
    peak = tree(jnp.maximum, parts)
    return peak + jnp.log(tree(jnp.add, [jnp.exp(part - peak) for part in parts]))


def dot_t(a, b):
    return lax.dot_general(a, b, (((1,), (1,)), ((), ())), preferred_element_type=F32)


def row_first(scale, rows, source, start_map, target, pot, scores_out, lse_out):
    weights = start_map[...].astype(BF16)
    pots = pot[...]

    @pl.loop(0, source.shape[0] // rows)
    def _(step):
        start = pl.multiple_of(step * rows, rows)
        rotated = jnp.dot(source[pl.ds(start, rows), :], weights, preferred_element_type=F32).astype(BF16)
        scores = dot_t(rotated, target[...]) * scale
        scores_out[pl.ds(start, rows), :] = scores
        shifted = scores + pots
        peak = jnp.max(shifted, axis=1, keepdims=True)
        lse = peak + jnp.log(jnp.sum(jnp.exp(shifted - peak), axis=1, keepdims=True))
        for part in range(rows // LANES):
            lse_out[pl.ds(step * (rows // LANES) + part, 1), :] = to_lanes(lse[part * LANES : (part + 1) * LANES])


def col_first(group, log_rows, scores, *refs):
    parts, (block_out, pot_out, peak_out, lse_out, work) = refs[:group], refs[group:]
    row_pot = -log_rows - tree_lse(parts)
    pot_out[...] = row_pot
    count, width = scores.shape
    blocks = count // LANES

    def peaks(step, peak):
        start = pl.multiple_of(step * LANES, LANES)
        shifted = scores[pl.ds(start, LANES), :] + to_column(pot_out[pl.ds(step, 1), :])
        work[pl.ds(start, LANES), :] = shifted
        return jnp.maximum(peak, jnp.max(shifted.reshape(LANES // 8, 8, width), axis=0))

    peak = lax.fori_loop(0, blocks, peaks, jnp.full((8, width), -jnp.inf, F32))
    peak = jnp.max(peak, axis=0, keepdims=True)

    def sums(step, total):
        start = pl.multiple_of(step * LANES, LANES)
        value = jnp.exp(work[pl.ds(start, LANES), :] - peak)
        block_out[pl.ds(start, LANES), :] = value.astype(BF16)
        return total + jnp.sum(value.reshape(LANES // 8, 8, width), axis=0)

    total = lax.fori_loop(0, blocks, sums, jnp.zeros((8, width), F32))
    peak_out[...] = peak
    lse_out[...] = peak + jnp.log(jnp.sum(total, axis=0, keepdims=True))


def wide_columns(row):
    pieces = []
    for part in range(row.shape[1] // LANES):
        pieces.append(jnp.broadcast_to(to_column(row[:, part * LANES : (part + 1) * LANES]), (LANES, LANES)))
    high, low = split(jnp.concatenate(pieces, axis=0))
    return jnp.concatenate([high, low], axis=1)


def row_sums(block, weights, sums_out):
    rows = 256
    for step in range(block.shape[0] // rows):
        wide = jnp.dot(block[step * rows : (step + 1) * rows, :], weights, preferred_element_type=F32)
        sums = wide[:, :LANES] + wide[:, LANES:]
        for part in range(rows // LANES):
            at = step * (rows // LANES) + part
            sums_out[at : at + 1, :] = to_lanes(sums[part * LANES : (part + 1) * LANES])


def row_second(group, log_cols, block, peak, *refs):
    parts, (pot_out, scale_out, sums_out) = refs[:group], refs[group:]
    lse = tree_lse(parts)
    pot_out[...] = -log_cols - lse
    scale = jnp.exp(peak[...] - lse)
    scale_out[...] = scale
    row_sums(block, wide_columns(scale), sums_out)


def col_later(group, ratio, block, scale, *refs):
    parts, (sums_out, factor) = refs[:group], refs[group:]
    factor[...] = ratio / tree_sum(parts)
    count, width = block.shape

    def sums(step, total):
        start = pl.multiple_of(step * LANES, LANES)
        value = block[pl.ds(start, LANES), :].astype(F32) * to_column(factor[pl.ds(step, 1), :])
        return total + jnp.sum(value.reshape(LANES // 8, 8, width), axis=0)

    total = lax.fori_loop(0, count // LANES, sums, jnp.zeros((8, width), F32))
    sums_out[...] = scale[...] * jnp.sum(total, axis=0, keepdims=True)


def row_later(group, block, scale, *refs):
    parts, (sums_out,) = refs[:group], refs[group:]
    row_sums(block, wide_columns(scale[...] / tree_sum(parts)), sums_out)


def row_last(group, block, scale, pot, target, *refs):
    parts, (col_out, sums_out, bary_out) = refs[:group], refs[group:]
    totals = tree_sum(parts)
    col_out[...] = EPS * (pot[...] - jnp.log(totals))
    row = scale[...] / totals
    weights = wide_columns(row)
    row_sums(block, weights, sums_out)
    factors = weights[:, :LANES].astype(F32) + weights[:, LANES:].astype(F32)
    high, low = split(target[...].astype(F32) * factors)
    both = jnp.concatenate([high, low], axis=1)
    rows = 256
    for step in range(block.shape[0] // rows):
        wide = jnp.dot(block[step * rows : (step + 1) * rows, :], both, preferred_element_type=F32)
        bary_out[step * rows : (step + 1) * rows, :] = wide[:, :LANES] + wide[:, LANES:]


def cross_local(group, ratio, source, bary, pot, *refs):
    parts, (row_out, cross_out) = refs[:group], refs[group:]
    totals = tree_sum(parts)
    row_out[...] = EPS * (pot[...] + jnp.log(ratio / totals))
    inverse = 1.0 / totals
    pieces = []
    for part in range(totals.shape[0]):
        piece = bary[part * LANES : (part + 1) * LANES, :] * to_column(inverse[part : part + 1, :])
        pieces.append(jnp.concatenate(split(piece), axis=1))
    both = jnp.concatenate(pieces, axis=0)
    cross = lax.dot_general(source[...], both, (((0,), (0,)), ((), ())), preferred_element_type=F32)
    width = source.shape[1]
    cross_out[...] = cross[:, :width] + cross[:, width:]


def precise(a, b, left):
    ah, al = split(a)
    bh, bl = split(b)
    axis = 0 if left else 1
    return lax.dot_general(
        jnp.concatenate([ah, ah, al], axis=axis),
        jnp.concatenate([bh, bl, bh], axis=0),
        (((axis,), (0,)), ((), ())),
        preferred_element_type=F32,
    )


def polar(group, *refs):
    parts, (out,) = refs[:group], refs[group:]
    cross = tree_sum(parts)
    iterate = cross / jnp.sqrt(jnp.sum(cross * cross) + 1e-06)
    for _ in range(NEWTON):
        gram = precise(iterate, iterate, True)
        iterate = 1.5 * iterate - 0.5 * precise(iterate, gram, False)
    out[...] = iterate


def exchange(x, axis):
    size = lax.axis_size(axis)
    return [x] + [lax.ppermute(x, axis, [(me, me ^ k) for me in range(size)]) for k in range(1, size)]


def shards(source, target, start_map, warm_potential):
    rows, width = source.shape
    cols = target.shape[0]
    n_src, n_tgt = lax.axis_size("src"), lax.axis_size("tgt")
    log_rows, log_cols = math.log(rows * n_src), math.log(cols * n_tgt)
    ratio = (cols * n_tgt) / (rows * n_src)
    scale = 1.0 / (math.sqrt(width) * EPS)
    row_vec = jax.ShapeDtypeStruct((rows // LANES, LANES), F32)
    col_vec = jax.ShapeDtypeStruct((1, cols), F32)
    pot = warm_potential.reshape(1, cols)
    mac = rows * cols * width

    scores, lse = call(
        functools.partial(row_first, scale, 256),
        "row_first",
        (jax.ShapeDtypeStruct((rows, cols), F32), row_vec),
        flops=4 * mac,
    )(source, start_map, target, pot)
    block, row_pot, peak, lse = call(
        functools.partial(col_first, n_tgt, log_rows),
        "col_first",
        (jax.ShapeDtypeStruct((rows, cols), BF16), row_vec, col_vec, col_vec),
        scratch=[pltpu.VMEM((rows, cols), F32)],
        flops=4 * mac,
    )(scores, *exchange(lse, "tgt"))
    col_pot, col_scale, sums = call(
        functools.partial(row_second, n_src, log_cols), "row_second", (col_vec, col_vec, row_vec), flops=2 * mac
    )(block, peak, *exchange(lse, "src"))
    col_later_call = call(
        functools.partial(col_later, n_tgt, ratio),
        "col_later",
        col_vec,
        scratch=[pltpu.VMEM(row_vec.shape, F32)],
        flops=2 * mac,
    )
    sums = col_later_call(block, col_scale, *exchange(sums, "tgt"))
    sums = call(functools.partial(row_later, n_src), "row_later", row_vec, flops=2 * mac)(
        block, col_scale, *exchange(sums, "src")
    )
    sums = col_later_call(block, col_scale, *exchange(sums, "tgt"))
    col_out, sums, bary = call(
        functools.partial(row_last, n_src),
        "row_last",
        (col_vec, row_vec, jax.ShapeDtypeStruct((rows, width), F32)),
        flops=4 * mac,
    )(block, col_scale, col_pot, target, *exchange(sums, "src"))
    square = jax.ShapeDtypeStruct((width, width), F32)
    row_out, cross = call(
        functools.partial(cross_local, n_tgt, ratio), "cross_local", (row_vec, square), flops=2 * rows * width * width
    )(source, bary, row_pot, *exchange(sums, "tgt"))
    cross = tree(jnp.add, exchange(cross, "src"))
    new_map = call(functools.partial(polar, n_tgt), "polar", square, flops=1 << 27)(*exchange(cross, "tgt"))
    return row_out.reshape(rows), col_out.reshape(cols), new_map


def solution(mesh):
    placed = (P("src", None), P("tgt", None), P(), P("tgt"))
    return jax.shard_map(
        shards, mesh=mesh, in_specs=placed, out_specs=(P("src"), P("tgt"), P()), check_vma=False
    )
```

```python
import functools
import math

import jax
import jax.numpy as jnp
from jax import lax
from jax.experimental import pallas as pl
from jax.experimental.pallas import tpu as pltpu
from jax.sharding import PartitionSpec as P

NEWTON = 10
EPS = 0.05
LANES = 128
VMEM_LIMIT = 40 * 1024 * 1024

F32 = jnp.float32
BF16 = jnp.bfloat16


def call(body, name, out_shape, scratch=(), flops=0):
    space = pl.BlockSpec(memory_space=pltpu.VMEM)
    return lambda *args: pl.pallas_call(
        body,
        name=name,
        out_shape=out_shape,
        in_specs=[space] * len(args),
        out_specs=jax.tree.map(lambda _: space, out_shape),
        scratch_shapes=scratch,
        compiler_params=pltpu.CompilerParams(vmem_limit_bytes=VMEM_LIMIT),
        cost_estimate=pl.CostEstimate(flops=flops, bytes_accessed=8 << 20, transcendentals=0),
    )(*args)


def eye_mask():
    shape = (LANES, LANES)
    return lax.broadcasted_iota(jnp.int32, shape, 0) == lax.broadcasted_iota(jnp.int32, shape, 1)


def to_lanes(column):
    wide = jnp.broadcast_to(column, (LANES, LANES))
    return jnp.sum(jnp.where(eye_mask(), wide, 0.0), axis=0, keepdims=True)


def to_column(row):
    wide = jnp.broadcast_to(row, (LANES, LANES))
    return jnp.sum(jnp.where(eye_mask(), wide, 0.0), axis=1, keepdims=True)


def split(x):
    high = x.astype(BF16)
    return high, (x - high.astype(F32)).astype(BF16)


def tree(combine, values):
    values = list(values)
    while len(values) > 1:
        values = [combine(a, b) for a, b in zip(values[::2], values[1::2])]
    return values[0]


def tree_sum(parts):
    return tree(jnp.add, parts)


def tree_lse(parts):
    peak = tree(jnp.maximum, parts)
    return peak + jnp.log(tree(jnp.add, [jnp.exp(part - peak) for part in parts]))


def received(refs, group):
    if len(refs[0].shape) == 3:
        return [refs[0][k] for k in range(group)], refs[1:]
    return [ref[...] for ref in refs[:group]], refs[group:]


def dot_t(a, b):
    return lax.dot_general(a, b, (((1,), (1,)), ((), ())), preferred_element_type=F32)


def row_first(scale, rows, source, start_map, target, pot, scores_out, lse_out):
    weights = start_map[...].astype(BF16)
    pots = pot[...]

    @pl.loop(0, source.shape[0] // rows)
    def _(step):
        start = pl.multiple_of(step * rows, rows)
        rotated = jnp.dot(source[pl.ds(start, rows), :], weights, preferred_element_type=F32).astype(BF16)
        scores = dot_t(rotated, target[...]) * scale
        scores_out[pl.ds(start, rows), :] = scores
        shifted = scores + pots
        peak = jnp.max(shifted, axis=1, keepdims=True)
        lse = peak + jnp.log(jnp.sum(jnp.exp(shifted - peak), axis=1, keepdims=True))
        for part in range(rows // LANES):
            lse_out[pl.ds(step * (rows // LANES) + part, 1), :] = to_lanes(lse[part * LANES : (part + 1) * LANES])


def col_first(group, log_rows, scores, *refs):
    parts, (block_out, pot_out, peak_out, lse_out, work) = received(refs, group)
    row_pot = -log_rows - tree_lse(parts)
    pot_out[...] = row_pot
    count, width = scores.shape
    blocks = count // LANES

    def peaks(step, peak):
        start = pl.multiple_of(step * LANES, LANES)
        shifted = scores[pl.ds(start, LANES), :] + to_column(pot_out[pl.ds(step, 1), :])
        work[pl.ds(start, LANES), :] = shifted
        return jnp.maximum(peak, jnp.max(shifted.reshape(LANES // 8, 8, width), axis=0))

    peak = lax.fori_loop(0, blocks, peaks, jnp.full((8, width), -jnp.inf, F32))
    peak = jnp.max(peak, axis=0, keepdims=True)

    def sums(step, total):
        start = pl.multiple_of(step * LANES, LANES)
        value = jnp.exp(work[pl.ds(start, LANES), :] - peak)
        block_out[pl.ds(start, LANES), :] = value.astype(BF16)
        return total + jnp.sum(value.reshape(LANES // 8, 8, width), axis=0)

    total = lax.fori_loop(0, blocks, sums, jnp.zeros((8, width), F32))
    peak_out[...] = peak
    lse_out[...] = peak + jnp.log(jnp.sum(total, axis=0, keepdims=True))


def wide_columns(row):
    pieces = []
    for part in range(row.shape[1] // LANES):
        pieces.append(jnp.broadcast_to(to_column(row[:, part * LANES : (part + 1) * LANES]), (LANES, LANES)))
    high, low = split(jnp.concatenate(pieces, axis=0))
    return jnp.concatenate([high, low], axis=1)


def row_sums(block, weights, sums_out):
    rows = 256
    for step in range(block.shape[0] // rows):
        wide = jnp.dot(block[step * rows : (step + 1) * rows, :], weights, preferred_element_type=F32)
        sums = wide[:, :LANES] + wide[:, LANES:]
        for part in range(rows // LANES):
            at = step * (rows // LANES) + part
            sums_out[at : at + 1, :] = to_lanes(sums[part * LANES : (part + 1) * LANES])


def row_second(group, log_cols, block, peak, *refs):
    parts, (pot_out, scale_out, sums_out) = received(refs, group)
    lse = tree_lse(parts)
    pot_out[...] = -log_cols - lse
    scale = jnp.exp(peak[...] - lse)
    scale_out[...] = scale
    row_sums(block, wide_columns(scale), sums_out)


def col_later(group, ratio, block, scale, *refs):
    parts, (sums_out, factor) = received(refs, group)
    factor[...] = ratio / tree_sum(parts)
    count, width = block.shape

    def sums(step, total):
        start = pl.multiple_of(step * LANES, LANES)
        value = block[pl.ds(start, LANES), :].astype(F32) * to_column(factor[pl.ds(step, 1), :])
        return total + jnp.sum(value.reshape(LANES // 8, 8, width), axis=0)

    total = lax.fori_loop(0, count // LANES, sums, jnp.zeros((8, width), F32))
    sums_out[...] = scale[...] * jnp.sum(total, axis=0, keepdims=True)


def row_later(group, block, scale, *refs):
    parts, (sums_out,) = received(refs, group)
    row_sums(block, wide_columns(scale[...] / tree_sum(parts)), sums_out)


def row_last(group, block, scale, pot, target, *refs):
    parts, (col_out, sums_out, bary_out) = received(refs, group)
    totals = tree_sum(parts)
    col_out[...] = EPS * (pot[...] - jnp.log(totals))
    row = scale[...] / totals
    weights = wide_columns(row)
    row_sums(block, weights, sums_out)
    factors = weights[:, :LANES].astype(F32) + weights[:, LANES:].astype(F32)
    high, low = split(target[...].astype(F32) * factors)
    both = jnp.concatenate([high, low], axis=1)
    rows = 256
    for step in range(block.shape[0] // rows):
        wide = jnp.dot(block[step * rows : (step + 1) * rows, :], both, preferred_element_type=F32)
        bary_out[step * rows : (step + 1) * rows, :] = wide[:, :LANES] + wide[:, LANES:]


def cross_local(group, ratio, source, bary, pot, *refs):
    parts, (row_out, cross_out) = received(refs, group)
    totals = tree_sum(parts)
    row_out[...] = EPS * (pot[...] + jnp.log(ratio / totals))
    inverse = 1.0 / totals
    pieces = []
    for part in range(totals.shape[0]):
        piece = bary[part * LANES : (part + 1) * LANES, :] * to_column(inverse[part : part + 1, :])
        pieces.append(jnp.concatenate(split(piece), axis=1))
    both = jnp.concatenate(pieces, axis=0)
    cross = lax.dot_general(source[...], both, (((0,), (0,)), ((), ())), preferred_element_type=F32)
    width = source.shape[1]
    cross_out[...] = cross[:, :width] + cross[:, width:]


def precise(a, b, left):
    ah, al = split(a)
    bh, bl = split(b)
    axis = 0 if left else 1
    return lax.dot_general(
        jnp.concatenate([ah, ah, al], axis=axis),
        jnp.concatenate([bh, bl, bh], axis=0),
        (((axis,), (0,)), ((), ())),
        preferred_element_type=F32,
    )


def polar(cross_ref, out):
    cross = cross_ref[...]
    iterate = cross / jnp.sqrt(jnp.sum(cross * cross) + 1e-06)
    for _ in range(NEWTON):
        gram = precise(iterate, iterate, True)
        iterate = 1.5 * iterate - 0.5 * precise(iterate, gram, False)
    out[...] = iterate


def exchange(x, axis):
    size = lax.axis_size(axis)
    if axis == "tgt":
        return [lax.all_to_all(jnp.broadcast_to(x, (size,) + x.shape), axis, 0, 0)]
    return [x] + [lax.ppermute(x, axis, [(me, me ^ k) for me in range(size)]) for k in range(1, size)]


def shards(source, target, start_map, warm_potential):
    rows, width = source.shape
    cols = target.shape[0]
    n_src, n_tgt = lax.axis_size("src"), lax.axis_size("tgt")
    log_rows, log_cols = math.log(rows * n_src), math.log(cols * n_tgt)
    ratio = (cols * n_tgt) / (rows * n_src)
    scale = 1.0 / (math.sqrt(width) * EPS)
    row_vec = jax.ShapeDtypeStruct((rows // LANES, LANES), F32)
    col_vec = jax.ShapeDtypeStruct((1, cols), F32)
    pot = warm_potential.reshape(1, cols)
    mac = rows * cols * width

    scores, lse = call(
        functools.partial(row_first, scale, 256),
        "row_first",
        (jax.ShapeDtypeStruct((rows, cols), F32), row_vec),
        flops=4 * mac,
    )(source, start_map, target, pot)
    block, row_pot, peak, lse = call(
        functools.partial(col_first, n_tgt, log_rows),
        "col_first",
        (jax.ShapeDtypeStruct((rows, cols), BF16), row_vec, col_vec, col_vec),
        scratch=[pltpu.VMEM((rows, cols), F32)],
        flops=4 * mac,
    )(scores, *exchange(lse, "tgt"))
    col_pot, col_scale, sums = call(
        functools.partial(row_second, n_src, log_cols), "row_second", (col_vec, col_vec, row_vec), flops=2 * mac
    )(block, peak, *exchange(lse, "src"))
    col_later_call = call(
        functools.partial(col_later, n_tgt, ratio),
        "col_later",
        col_vec,
        scratch=[pltpu.VMEM(row_vec.shape, F32)],
        flops=2 * mac,
    )
    sums = col_later_call(block, col_scale, *exchange(sums, "tgt"))
    sums = call(functools.partial(row_later, n_src), "row_later", row_vec, flops=2 * mac)(
        block, col_scale, *exchange(sums, "src")
    )
    sums = col_later_call(block, col_scale, *exchange(sums, "tgt"))
    col_out, sums, bary = call(
        functools.partial(row_last, n_src),
        "row_last",
        (col_vec, row_vec, jax.ShapeDtypeStruct((rows, width), F32)),
        flops=4 * mac,
    )(block, col_scale, col_pot, target, *exchange(sums, "src"))
    square = jax.ShapeDtypeStruct((width, width), F32)
    row_out, cross = call(
        functools.partial(cross_local, n_tgt, ratio), "cross_local", (row_vec, square), flops=2 * rows * width * width
    )(source, bary, row_pot, *exchange(sums, "tgt"))
    shares = lax.all_to_all(cross.reshape(n_tgt, width // n_tgt, width), "tgt", 0, 0)
    share = tree(jnp.add, exchange(jnp.sum(shares, axis=0), "src"))
    new_map = call(polar, "polar", square, flops=1 << 27)(exchange(share, "tgt")[0].reshape(width, width))
    return row_out.reshape(rows), col_out.reshape(cols), new_map


def solution(mesh):
    placed = (P("src", None), P("tgt", None), P(), P("tgt"))
    return jax.shard_map(
        shards, mesh=mesh, in_specs=placed, out_specs=(P("src"), P("tgt"), P()), check_vma=False
    )
```

```python
import functools
import math

import jax
import jax.numpy as jnp
from jax import lax
from jax.experimental import pallas as pl
from jax.experimental.pallas import tpu as pltpu
from jax.sharding import PartitionSpec as P

NEWTON = 10
EPS = 0.05
LANES = 128
VMEM_LIMIT = 40 * 1024 * 1024

F32 = jnp.float32
BF16 = jnp.bfloat16


def call(body, name, out_shape, scratch=(), flops=0):
    space = pl.BlockSpec(memory_space=pltpu.VMEM)
    return lambda *args: pl.pallas_call(
        body,
        name=name,
        out_shape=out_shape,
        in_specs=[space] * len(args),
        out_specs=jax.tree.map(lambda _: space, out_shape),
        scratch_shapes=scratch,
        compiler_params=pltpu.CompilerParams(vmem_limit_bytes=VMEM_LIMIT),
        cost_estimate=pl.CostEstimate(flops=flops, bytes_accessed=8 << 20, transcendentals=0),
    )(*args)


def eye_mask():
    shape = (LANES, LANES)
    return lax.broadcasted_iota(jnp.int32, shape, 0) == lax.broadcasted_iota(jnp.int32, shape, 1)


def to_lanes(column):
    wide = jnp.broadcast_to(column, (LANES, LANES))
    return jnp.sum(jnp.where(eye_mask(), wide, 0.0), axis=0, keepdims=True)


def to_column(row):
    wide = jnp.broadcast_to(row, (LANES, LANES))
    return jnp.sum(jnp.where(eye_mask(), wide, 0.0), axis=1, keepdims=True)


def split(x):
    high = x.astype(BF16)
    return high, (x - high.astype(F32)).astype(BF16)


def tree(combine, values):
    values = list(values)
    while len(values) > 1:
        values = [combine(a, b) for a, b in zip(values[::2], values[1::2])]
    return values[0]


def tree_sum(parts):
    return tree(jnp.add, parts)


def tree_lse(parts):
    peak = tree(jnp.maximum, parts)
    return peak + jnp.log(tree(jnp.add, [jnp.exp(part - peak) for part in parts]))


def received(refs, group):
    if len(refs[0].shape) == 3:
        return [refs[0][k] for k in range(group)], refs[1:]
    return [ref[...] for ref in refs[:group]], refs[group:]


def dot_t(a, b):
    return lax.dot_general(a, b, (((1,), (1,)), ((), ())), preferred_element_type=F32)


def row_first(scale, rows, source, start_map, target, pot, scores_out, lse_out):
    weights = start_map[...].astype(BF16)
    pots = pot[...]

    @pl.loop(0, source.shape[0] // rows)
    def _(step):
        start = pl.multiple_of(step * rows, rows)
        rotated = jnp.dot(source[pl.ds(start, rows), :], weights, preferred_element_type=F32).astype(BF16)
        scores = dot_t(rotated, target[...]) * scale
        scores_out[pl.ds(start, rows), :] = scores
        shifted = scores + pots
        peak = jnp.max(shifted, axis=1, keepdims=True)
        lse = peak + jnp.log(jnp.sum(jnp.exp(shifted - peak), axis=1, keepdims=True))
        for part in range(rows // LANES):
            lse_out[pl.ds(step * (rows // LANES) + part, 1), :] = to_lanes(lse[part * LANES : (part + 1) * LANES])


def col_first(group, log_rows, scores, *refs):
    parts, (block_out, pot_out, peak_out, lse_out, work) = received(refs, group)
    row_pot = -log_rows - tree_lse(parts)
    pot_out[...] = row_pot
    count, width = scores.shape
    blocks = count // LANES

    def peaks(step, peak):
        start = pl.multiple_of(step * LANES, LANES)
        shifted = scores[pl.ds(start, LANES), :] + to_column(pot_out[pl.ds(step, 1), :])
        work[pl.ds(start, LANES), :] = shifted
        return jnp.maximum(peak, jnp.max(shifted.reshape(LANES // 8, 8, width), axis=0))

    peak = lax.fori_loop(0, blocks, peaks, jnp.full((8, width), -jnp.inf, F32))
    peak = jnp.max(peak, axis=0, keepdims=True)

    def sums(step, total):
        start = pl.multiple_of(step * LANES, LANES)
        value = jnp.exp(work[pl.ds(start, LANES), :] - peak)
        block_out[pl.ds(start, LANES), :] = value.astype(BF16)
        return total + jnp.sum(value.reshape(LANES // 8, 8, width), axis=0)

    total = lax.fori_loop(0, blocks, sums, jnp.zeros((8, width), F32))
    peak_out[...] = peak
    lse_out[...] = peak + jnp.log(jnp.sum(total, axis=0, keepdims=True))


def wide_columns(row):
    pieces = []
    for part in range(row.shape[1] // LANES):
        pieces.append(jnp.broadcast_to(to_column(row[:, part * LANES : (part + 1) * LANES]), (LANES, LANES)))
    high, low = split(jnp.concatenate(pieces, axis=0))
    return jnp.concatenate([high, low], axis=1)


def row_sums(block, weights, sums_out):
    rows = 256
    for step in range(block.shape[0] // rows):
        wide = jnp.dot(block[step * rows : (step + 1) * rows, :], weights, preferred_element_type=F32)
        sums = wide[:, :LANES] + wide[:, LANES:]
        for part in range(rows // LANES):
            at = step * (rows // LANES) + part
            sums_out[at : at + 1, :] = to_lanes(sums[part * LANES : (part + 1) * LANES])


def row_second(group, log_cols, block, peak, *refs):
    parts, (pot_out, scale_out, sums_out) = received(refs, group)
    lse = tree_lse(parts)
    pot_out[...] = -log_cols - lse
    scale = jnp.exp(peak[...] - lse)
    scale_out[...] = scale
    row_sums(block, wide_columns(scale), sums_out)


def col_later(group, ratio, block, scale, *refs):
    parts, (sums_out, factor) = received(refs, group)
    factor[...] = ratio / tree_sum(parts)
    count, width = block.shape

    def sums(step, total):
        start = pl.multiple_of(step * LANES, LANES)
        value = block[pl.ds(start, LANES), :].astype(F32) * to_column(factor[pl.ds(step, 1), :])
        return total + jnp.sum(value.reshape(LANES // 8, 8, width), axis=0)

    total = lax.fori_loop(0, count // LANES, sums, jnp.zeros((8, width), F32))
    sums_out[...] = scale[...] * jnp.sum(total, axis=0, keepdims=True)


def row_later(group, block, scale, *refs):
    parts, (sums_out,) = received(refs, group)
    row_sums(block, wide_columns(scale[...] / tree_sum(parts)), sums_out)


def row_last(group, block, scale, pot, target, *refs):
    parts, (col_out, sums_out, bary_out) = received(refs, group)
    totals = tree_sum(parts)
    col_out[...] = EPS * (pot[...] - jnp.log(totals))
    row = scale[...] / totals
    weights = wide_columns(row)
    row_sums(block, weights, sums_out)
    factors = weights[:, :LANES].astype(F32) + weights[:, LANES:].astype(F32)
    high, low = split(target[...].astype(F32) * factors)
    both = jnp.concatenate([high, low], axis=1)
    rows = 256
    for step in range(block.shape[0] // rows):
        wide = jnp.dot(block[step * rows : (step + 1) * rows, :], both, preferred_element_type=F32)
        bary_out[step * rows : (step + 1) * rows, :] = wide[:, :LANES] + wide[:, LANES:]


def cross_local(group, ratio, source, bary, pot, *refs):
    parts, (row_out, cross_out) = received(refs, group)
    totals = tree_sum(parts)
    row_out[...] = EPS * (pot[...] + jnp.log(ratio / totals))
    inverse = 1.0 / totals
    pieces = []
    for part in range(totals.shape[0]):
        piece = bary[part * LANES : (part + 1) * LANES, :] * to_column(inverse[part : part + 1, :])
        pieces.append(jnp.concatenate(split(piece), axis=1))
    both = jnp.concatenate(pieces, axis=0)
    cross = lax.dot_general(source[...], both, (((0,), (0,)), ((), ())), preferred_element_type=F32)
    width = source.shape[1]
    cross_out[...] = cross[:, :width] + cross[:, width:]


def precise(a, b, left):
    ah, al = split(a)
    bh, bl = split(b)
    axis = 0 if left else 1
    return lax.dot_general(
        jnp.concatenate([ah, ah, al], axis=axis),
        jnp.concatenate([bh, bl, bh], axis=0),
        (((axis,), (0,)), ((), ())),
        preferred_element_type=F32,
    )


def polar(cross_ref, out):
    cross = cross_ref[...]
    iterate = cross / jnp.sqrt(jnp.sum(cross * cross) + 1e-06)
    for _ in range(NEWTON):
        gram = precise(iterate, iterate, True)
        iterate = 1.5 * iterate - 0.5 * precise(iterate, gram, False)
    out[...] = iterate


def exchange(x, axis):
    size = lax.axis_size(axis)
    if axis == "tgt":
        return [lax.all_gather(x, axis)]
    return [x] + [lax.ppermute(x, axis, [(me, me ^ k) for me in range(size)]) for k in range(1, size)]


def scatter(x, axis):
    size = lax.axis_size(axis)
    index = lax.axis_index(axis)
    pairs = lambda k: [(me, me ^ k) for me in range(size)]
    own = [lax.dynamic_index_in_dim(x, index ^ k, keepdims=False) for k in range(size)]
    return own[:1] + [lax.ppermute(own[k], axis, pairs(k)) for k in range(1, size)]


def gather(x, axis):
    index = lax.axis_index(axis)
    stacked = jnp.zeros((lax.axis_size(axis),) + x.shape, x.dtype)
    for k, part in enumerate(exchange(x, axis)):
        stacked = lax.dynamic_update_index_in_dim(stacked, part, index ^ k, 0)
    return stacked


def shards(source, target, start_map, warm_potential):
    rows, width = source.shape
    cols = target.shape[0]
    n_src, n_tgt = lax.axis_size("src"), lax.axis_size("tgt")
    log_rows, log_cols = math.log(rows * n_src), math.log(cols * n_tgt)
    ratio = (cols * n_tgt) / (rows * n_src)
    scale = 1.0 / (math.sqrt(width) * EPS)
    row_vec = jax.ShapeDtypeStruct((rows // LANES, LANES), F32)
    col_vec = jax.ShapeDtypeStruct((1, cols), F32)
    pot = warm_potential.reshape(1, cols)
    mac = rows * cols * width

    scores, lse = call(
        functools.partial(row_first, scale, 256),
        "row_first",
        (jax.ShapeDtypeStruct((rows, cols), F32), row_vec),
        flops=4 * mac,
    )(source, start_map, target, pot)
    block, row_pot, peak, lse = call(
        functools.partial(col_first, n_tgt, log_rows),
        "col_first",
        (jax.ShapeDtypeStruct((rows, cols), BF16), row_vec, col_vec, col_vec),
        scratch=[pltpu.VMEM((rows, cols), F32)],
        flops=4 * mac,
    )(scores, *exchange(lse, "tgt"))
    col_pot, col_scale, sums = call(
        functools.partial(row_second, n_src, log_cols), "row_second", (col_vec, col_vec, row_vec), flops=2 * mac
    )(block, peak, *exchange(lse, "src"))
    col_later_call = call(
        functools.partial(col_later, n_tgt, ratio),
        "col_later",
        col_vec,
        scratch=[pltpu.VMEM(row_vec.shape, F32)],
        flops=2 * mac,
    )
    sums = col_later_call(block, col_scale, *exchange(sums, "tgt"))
    sums = call(functools.partial(row_later, n_src), "row_later", row_vec, flops=2 * mac)(
        block, col_scale, *exchange(sums, "src")
    )
    sums = col_later_call(block, col_scale, *exchange(sums, "tgt"))
    col_out, sums, bary = call(
        functools.partial(row_last, n_src),
        "row_last",
        (col_vec, row_vec, jax.ShapeDtypeStruct((rows, width), F32)),
        flops=4 * mac,
    )(block, col_scale, col_pot, target, *exchange(sums, "src"))
    square = jax.ShapeDtypeStruct((width, width), F32)
    row_out, cross = call(
        functools.partial(cross_local, n_tgt, ratio), "cross_local", (row_vec, square), flops=2 * rows * width * width
    )(source, bary, row_pot, *exchange(sums, "tgt"))
    share = tree(jnp.add, scatter(cross.reshape(n_src, width // n_src, width), "src"))
    share = tree_sum(exchange(share, "tgt")[0])
    cross = gather(share, "src").reshape(width, width)
    new_map = call(polar, "polar", square, flops=1 << 27)(cross)
    return row_out.reshape(rows), col_out.reshape(cols), new_map


def solution(mesh):
    placed = (P("src", None), P("tgt", None), P(), P("tgt"))
    return jax.shard_map(
        shards, mesh=mesh, in_specs=placed, out_specs=(P("src"), P("tgt"), P()), check_vma=False
    )
```

```python
import functools
import math

import jax
import jax.numpy as jnp
from jax import lax
from jax.experimental import pallas as pl
from jax.experimental.pallas import tpu as pltpu
from jax.sharding import PartitionSpec as P

NEWTON = 10
EPS = 0.05
LANES = 128
CHUNK = 256
VMEM_LIMIT = 40 * 1024 * 1024

F32 = jnp.float32
BF16 = jnp.bfloat16


def call(body, name, out_shape, scratch=(), flops=0, space=pltpu.VMEM):
    return lambda *args: pl.pallas_call(
        body,
        name=name,
        out_shape=out_shape,
        in_specs=[pl.BlockSpec(memory_space=space)] * len(args),
        out_specs=jax.tree.map(lambda _: pl.BlockSpec(memory_space=pltpu.VMEM), out_shape),
        scratch_shapes=scratch,
        compiler_params=pltpu.CompilerParams(vmem_limit_bytes=VMEM_LIMIT),
        cost_estimate=pl.CostEstimate(flops=flops, bytes_accessed=8 << 20, transcendentals=0),
    )(*args)


def eye_mask():
    shape = (LANES, LANES)
    return lax.broadcasted_iota(jnp.int32, shape, 0) == lax.broadcasted_iota(jnp.int32, shape, 1)


def to_lanes(column):
    wide = jnp.broadcast_to(column, (LANES, LANES))
    return jnp.sum(jnp.where(eye_mask(), wide, 0.0), axis=0, keepdims=True)


def to_column(row):
    wide = jnp.broadcast_to(row, (LANES, LANES))
    return jnp.broadcast_to(jnp.sum(jnp.where(eye_mask(), wide, 0.0), axis=1, keepdims=True), (LANES, LANES))


def split(x):
    high = x.astype(BF16)
    return high, (x - high.astype(F32)).astype(BF16)


def lane_parts(wide, first, fill):
    lane = lax.broadcasted_iota(jnp.int32, wide.shape, 1)
    out = jnp.where((lane >= fill) & (lane < fill + 3), 1.0, 0.0)
    rest = wide
    for k in range(3):
        part = rest.astype(BF16).astype(F32)
        out = jnp.where(lane == first + k, part, out)
        rest = rest - part
    return out.astype(BF16)


def tree(combine, values):
    values = list(values)
    while len(values) > 1:
        values = [combine(a, b) for a, b in zip(values[::2], values[1::2])]
    return values[0]


def tree_sum(parts):
    return tree(jnp.add, parts)


def tree_lse(unit, parts):
    peak = tree(jnp.maximum, parts)
    total = tree(jnp.add, [jnp.exp2(unit * (part - peak)) for part in parts])
    return peak + jnp.log(total) * (1.0 / (unit * math.log(2.0)))


def received(refs, group):
    return [ref[...] for ref in refs[:group]], refs[group:]


def dot_t(a, b):
    return lax.dot_general(a, b, (((1,), (1,)), ((), ())), preferred_element_type=F32)


def row_first(
    unit, scale, source_hbm, map_hbm, target_hbm, pot_hbm, left_out, right_out, lse_out, source, start_map, target, pot, work, sems
):
    copies = [
        pltpu.make_async_copy(src, dst, sems.at[k])
        for k, (src, dst) in enumerate(
            [(source_hbm, source), (map_hbm, start_map), (target_hbm, target), (pot_hbm, pot)]
        )
    ]
    for copy in copies:
        copy.start()
    for copy in copies:
        copy.wait()
    width = source.shape[1]
    rows = source.shape[0]
    for part in range(target.shape[0] // LANES):
        at = pl.ds(part * LANES, LANES)
        right_out[at, :width] = target[at, :]
        right_out[at, width:] = lane_parts(to_column(pot[:, at] * (1.0 / scale)), 0, 3)
    left_out[...] = jnp.dot(source[...], start_map[...].astype(BF16), preferred_element_type=F32).astype(BF16)
    lane = lax.broadcasted_iota(jnp.int32, (CHUNK, LANES), 1)
    ones = jnp.where(lane < 3, 1.0, 0.0).astype(BF16)
    group = 32
    for start in range(0, rows, CHUNK):
        left = jnp.concatenate([left_out[start : start + CHUNK, :], ones], axis=1)
        work[start : start + CHUNK, :] = dot_t(left, right_out[...])
        peaks, sums = [], []
        for at in range(start, start + CHUNK, group):
            peak = jnp.max(work[at : at + group, :], axis=1, keepdims=True)
            value = jnp.exp2((work[at : at + group, :] - peak) * unit)
            peaks.append(peak)
            sums.append(jnp.sum(value, axis=1, keepdims=True))
        peak = jnp.concatenate(peaks, axis=0)
        total = jnp.concatenate(sums, axis=0)
        for part in range(CHUNK // LANES):
            here = slice(part * LANES, (part + 1) * LANES)
            at = start // LANES + part
            lse_out[at : at + 1, :] = to_lanes(peak[here]) + jnp.log(to_lanes(total[here])) * (
                1.0 / (unit * math.log(2.0))
            )


def col_first(group, unit, log_rows, left_in, right, *refs):
    parts, (block_out, pot_out, peak_out, lse_out, left, work) = received(refs, group)
    row_pot = -log_rows - tree_lse(unit, parts)
    pot_out[...] = row_pot
    rows, width = left_in.shape
    cols = right.shape[0]
    left[:, :width] = left_in[...]
    for part in range(rows // LANES):
        left[part * LANES : (part + 1) * LANES, width:] = lane_parts(to_column(row_pot[part : part + 1, :]), 3, 0)
    peak = None
    for start in range(0, rows, CHUNK):
        value = dot_t(left[start : start + CHUNK, :], right[...])
        work[start : start + CHUNK, :] = value
        top = jnp.max(value.reshape(CHUNK // 8, 8, cols), axis=0)
        peak = top if peak is None else jnp.maximum(peak, top)
    peak = jnp.max(peak, axis=0, keepdims=True)
    group_rows = 16

    def sums(step, total):
        for k in range(0, LANES, group_rows):
            at = pl.ds(pl.multiple_of(step * LANES + k, group_rows), group_rows)
            value = jnp.exp2((work[at, :] - peak) * unit)
            block_out[at, :] = value.astype(BF16)
            total = total + value[:8] + value[8:]
        return total

    total = lax.fori_loop(0, rows // LANES, sums, jnp.zeros((8, cols), F32))
    peak_out[...] = peak
    lse_out[...] = peak + jnp.log(jnp.sum(total, axis=0, keepdims=True)) * (1.0 / (unit * math.log(2.0)))


def column_factors(row):
    pieces = [to_column(row[:, at : at + LANES]) for at in range(0, row.shape[1], LANES)]
    return jnp.concatenate(pieces, axis=0)


def row_sums(block, row, sums_out):
    weights = jnp.concatenate(split(column_factors(row)), axis=1)
    for start in range(0, block.shape[0], CHUNK):
        wide = jnp.dot(block[start : start + CHUNK, :], weights, preferred_element_type=F32)
        sums = wide[:, :LANES] + wide[:, LANES:]
        for part in range(CHUNK // LANES):
            at = start // LANES + part
            sums_out[at : at + 1, :] = to_lanes(sums[part * LANES : (part + 1) * LANES])


def row_second(group, unit, log_cols, block, peak, pot, *refs):
    parts, (pot_out, scale_out, sums_out) = received(refs, group)
    lse = tree_lse(unit, parts)
    pot_out[...] = pot[...] - log_cols - lse
    scale = jnp.exp2(unit * (peak[...] - lse))
    scale_out[...] = scale
    row_sums(block, scale, sums_out)


def col_later(group, ratio, block, scale, *refs):
    parts, (sums_out, factor) = received(refs, group)
    factors = ratio / tree_sum(parts)
    rows, cols = block.shape
    for part in range(rows // LANES):
        factor[part * LANES : (part + 1) * LANES, :] = to_column(factors[part : part + 1, :])
    group_rows = 16

    def sums(step, total):
        for k in range(0, LANES, group_rows):
            at = pl.ds(pl.multiple_of(step * LANES + k, group_rows), group_rows)
            value = block[at, :].astype(F32) * jnp.concatenate([factor[at, :]] * (cols // LANES), axis=1)
            total = total + value[:8] + value[8:]
        return total

    total = lax.fori_loop(0, rows // LANES, sums, jnp.zeros((8, cols), F32))
    sums_out[...] = scale[...] * jnp.sum(total, axis=0, keepdims=True)


def row_later(group, block, scale, *refs):
    parts, (sums_out,) = received(refs, group)
    row_sums(block, scale[...] / tree_sum(parts), sums_out)


def row_last(group, unit, block, scale, pot, target, *refs):
    parts, (col_out, sums_out, bary_out) = received(refs, group)
    totals = tree_sum(parts)
    col_out[...] = (EPS * math.log(2.0)) * (unit * pot[...] - jnp.log(totals) * (1.0 / math.log(2.0)))
    factors = column_factors(scale[...] / totals)
    high, low = split(factors)
    lane = lax.broadcasted_iota(jnp.int32, factors.shape, 1)
    sides = jnp.where(lane < LANES // 2, high.astype(F32), low.astype(F32)).astype(BF16)
    scaled = (target[:, : factors.shape[1]].astype(F32) * factors).astype(BF16)
    weights = jnp.concatenate([scaled, sides], axis=1)
    for start in range(0, block.shape[0], CHUNK):
        wide = jnp.dot(block[start : start + CHUNK, :], weights, preferred_element_type=F32)
        bary_out[start : start + CHUNK, :] = wide[:, :LANES]
        sums = wide[:, LANES:] + pltpu.roll(wide[:, LANES:], LANES // 2, 1)
        for part in range(CHUNK // LANES):
            at = start // LANES + part
            sums_out[at : at + 1, :] = to_lanes(sums[part * LANES : (part + 1) * LANES])


def cross_local(group, unit, ratio, source, bary, pot, *refs):
    parts, (row_out, cross_out) = received(refs, group)
    totals = tree_sum(parts)
    row_out[...] = (EPS * math.log(2.0)) * (unit * pot[...] + jnp.log(ratio / totals) * (1.0 / math.log(2.0)))
    inverse = 1.0 / totals
    pieces = []
    for part in range(totals.shape[0]):
        piece = bary[part * LANES : (part + 1) * LANES, :] * to_column(inverse[part : part + 1, :])
        pieces.append(jnp.concatenate(split(piece), axis=1))
    both = jnp.concatenate(pieces, axis=0)
    cross = lax.dot_general(source[...], both, (((0,), (0,)), ((), ())), preferred_element_type=F32)
    width = source.shape[1]
    cross_out[...] = cross[:, :width] + cross[:, width:]


def precise(a, b, axis):
    ah, al = split(a)
    bh, bl = split(b)
    return lax.dot_general(
        jnp.concatenate([ah, ah, al], axis=axis),
        jnp.concatenate([bh, bl, bh], axis=0),
        (((axis,), (0,)), ((), ())),
        preferred_element_type=F32,
    )


def polar(cross_ref, out):
    cross = cross_ref[...]
    iterate = cross / jnp.sqrt(jnp.sum(cross * cross) + 1e-06)
    gram = precise(iterate, iterate, 0)
    for step in range(NEWTON):
        factor = jnp.where(eye_mask(), 1.5, 0.0) - 0.5 * gram
        if step < NEWTON - 1:
            gram = precise(precise(factor, gram, 1), factor, 1)
        iterate = precise(iterate, factor, 1)
    out[...] = iterate


def partners(x, axis, ks):
    size = lax.axis_size(axis)
    return [x] + [lax.ppermute(x, axis, [(me, me ^ k) for me in range(size)]) for k in ks]


def exchange(x, axis, combine):
    size = lax.axis_size(axis)
    if axis == "src":
        return partners(x, axis, range(1, size))
    return partners(combine(partners(x, axis, [1])), axis, range(2, size, 2))


def scatter(x, axis):
    size = lax.axis_size(axis)
    index = lax.axis_index(axis)
    pairs = lambda k: [(me, me ^ k) for me in range(size)]
    own = [lax.dynamic_index_in_dim(x, index ^ k, keepdims=False) for k in range(size)]
    return own[:1] + [lax.ppermute(own[k], axis, pairs(k)) for k in range(1, size)]


def gather(x, axis):
    size = lax.axis_size(axis)
    index = lax.axis_index(axis)
    stacked = jnp.zeros((size,) + x.shape, x.dtype)
    for k, part in enumerate(partners(x, axis, range(1, size))):
        stacked = lax.dynamic_update_index_in_dim(stacked, part, index ^ k, 0)
    return stacked


def shards(source, target, start_map, warm_potential):
    rows, width = source.shape
    cols = target.shape[0]
    n_src, n_tgt = lax.axis_size("src"), lax.axis_size("tgt")
    ratio = (cols * n_tgt) / (rows * n_src)
    scale = 1.0 / (math.sqrt(width) * EPS)
    unit = scale / math.log(2.0)
    log_rows, log_cols = math.log(rows * n_src) / scale, math.log(cols * n_tgt) / scale
    row_vec = jax.ShapeDtypeStruct((rows // LANES, LANES), F32)
    col_vec = jax.ShapeDtypeStruct((1, cols), F32)
    pot = warm_potential.reshape(1, cols)
    mac = rows * cols * width
    lse_of = functools.partial(tree_lse, unit)
    n_rows = len(jax.eval_shape(lambda x: exchange(x, "tgt", tree_sum), row_vec))

    left, right, lse = call(
        functools.partial(row_first, unit, scale),
        "row_first",
        (
            jax.ShapeDtypeStruct((rows, width), BF16),
            jax.ShapeDtypeStruct((cols, width + LANES), BF16),
            row_vec,
        ),
        scratch=[
            pltpu.VMEM((rows, width), BF16),
            pltpu.VMEM((width, width), F32),
            pltpu.VMEM((cols, width), BF16),
            pltpu.VMEM((1, cols), F32),
            pltpu.VMEM((rows, cols), F32),
            pltpu.SemaphoreType.DMA((4,)),
        ],
        flops=4 * mac,
        space=pl.ANY,
    )(source, start_map, target, pot)
    block, row_pot, peak, lse = call(
        functools.partial(col_first, n_rows, unit, log_rows),
        "col_first",
        (jax.ShapeDtypeStruct((rows, cols), BF16), row_vec, col_vec, col_vec),
        scratch=[pltpu.VMEM((rows, width + LANES), BF16), pltpu.VMEM((rows, cols), F32)],
        flops=4 * mac,
    )(left, right, *exchange(lse, "tgt", lse_of))
    col_pot, col_scale, sums = call(
        functools.partial(row_second, n_src, unit, log_cols), "row_second", (col_vec, col_vec, row_vec), flops=2 * mac
    )(block, peak, pot * (1.0 / scale), *exchange(lse, "src", lse_of))
    col_later_call = call(
        functools.partial(col_later, n_rows, ratio),
        "col_later",
        col_vec,
        scratch=[pltpu.VMEM((rows, LANES), F32)],
        flops=2 * mac,
    )
    sums = col_later_call(block, col_scale, *exchange(sums, "tgt", tree_sum))
    sums = call(functools.partial(row_later, n_src), "row_later", row_vec, flops=2 * mac)(
        block, col_scale, *exchange(sums, "src", tree_sum)
    )
    sums = col_later_call(block, col_scale, *exchange(sums, "tgt", tree_sum))
    col_out, sums, bary = call(
        functools.partial(row_last, n_src, unit),
        "row_last",
        (col_vec, row_vec, jax.ShapeDtypeStruct((rows, width), F32)),
        flops=4 * mac,
    )(block, col_scale, col_pot, right, *exchange(sums, "src", tree_sum))
    square = jax.ShapeDtypeStruct((width, width), F32)
    row_out, cross = call(
        functools.partial(cross_local, n_rows, unit, ratio),
        "cross_local",
        (row_vec, square),
        flops=2 * rows * width * width,
    )(source, bary, row_pot, *exchange(sums, "tgt", tree_sum))
    share = tree_sum(scatter(cross.reshape(n_src, width // n_src, width), "src"))
    share = tree_sum(exchange(share, "tgt", tree_sum))
    new_map = call(polar, "polar", square, flops=1 << 27)(gather(share, "src").reshape(width, width))
    return row_out.reshape(rows), col_out.reshape(cols), new_map


def solution(mesh):
    placed = (P("src", None), P("tgt", None), P(), P("tgt"))
    return jax.shard_map(
        shards, mesh=mesh, in_specs=placed, out_specs=(P("src"), P("tgt"), P()), check_vma=False
    )
```

```python
import functools
import math

import jax
import jax.numpy as jnp
from jax import lax
from jax.experimental import pallas as pl
from jax.experimental.pallas import tpu as pltpu
from jax.sharding import PartitionSpec as P

NEWTON = 10
EPS = 0.05
LANES = 128
CHUNK = 256
VMEM_LIMIT = 40 * 1024 * 1024

F32 = jnp.float32
BF16 = jnp.bfloat16


def call(body, name, out_shape, scratch=(), flops=0, space=pltpu.VMEM):
    return lambda *args: pl.pallas_call(
        body,
        name=name,
        out_shape=out_shape,
        in_specs=[pl.BlockSpec(memory_space=space)] * len(args),
        out_specs=jax.tree.map(lambda _: pl.BlockSpec(memory_space=pltpu.VMEM), out_shape),
        scratch_shapes=scratch,
        compiler_params=pltpu.CompilerParams(vmem_limit_bytes=VMEM_LIMIT),
        cost_estimate=pl.CostEstimate(flops=flops, bytes_accessed=8 << 20, transcendentals=0),
    )(*args)


def eye_mask():
    shape = (LANES, LANES)
    return lax.broadcasted_iota(jnp.int32, shape, 0) == lax.broadcasted_iota(jnp.int32, shape, 1)


def to_lanes(column):
    wide = jnp.broadcast_to(column, (LANES, LANES))
    return jnp.sum(jnp.where(eye_mask(), wide, 0.0), axis=0, keepdims=True)


def to_column(row):
    wide = jnp.broadcast_to(row, (LANES, LANES))
    return jnp.broadcast_to(jnp.sum(jnp.where(eye_mask(), wide, 0.0), axis=1, keepdims=True), (LANES, LANES))


def split(x):
    high = x.astype(BF16)
    return high, (x - high.astype(F32)).astype(BF16)


def lane_parts(wide, first, fill):
    lane = lax.broadcasted_iota(jnp.int32, wide.shape, 1)
    out = jnp.where((lane >= fill) & (lane < fill + 3), 1.0, 0.0)
    rest = wide
    for k in range(3):
        part = rest.astype(BF16).astype(F32)
        out = jnp.where(lane == first + k, part, out)
        rest = rest - part
    return out.astype(BF16)


def tree(combine, values):
    values = list(values)
    while len(values) > 1:
        values = [combine(a, b) for a, b in zip(values[::2], values[1::2])]
    return values[0]


def tree_sum(parts):
    return tree(jnp.add, parts)


def tree_lse(unit, parts):
    peak = tree(jnp.maximum, parts)
    total = tree(jnp.add, [jnp.exp2(unit * (part - peak)) for part in parts])
    return peak + jnp.log(total) * (1.0 / (unit * math.log(2.0)))


def received(refs, group):
    if len(refs[0].shape) == 3:
        return [refs[0][k] for k in range(group)], refs[1:]
    return [ref[...] for ref in refs[:group][::-1]], refs[group:]


def dot_t(a, b):
    return lax.dot_general(a, b, (((1,), (1,)), ((), ())), preferred_element_type=F32)


def row_first(
    unit, scale, source_hbm, map_hbm, target_hbm, pot_hbm, left_out, right_out, lse_out,
    source, start_map, target, pot, work, peaks, totals, sums, sems,
):
    copies = [
        pltpu.make_async_copy(src, dst, sems.at[k])
        for k, (src, dst) in enumerate(
            [(source_hbm, source), (map_hbm, start_map), (target_hbm, target), (pot_hbm, pot)]
        )
    ]
    for copy in copies:
        copy.start()
    for copy in copies:
        copy.wait()
    width = source.shape[1]
    rows = source.shape[0]
    for part in range(target.shape[0] // LANES):
        at = pl.ds(part * LANES, LANES)
        right_out[at, :width] = target[at, :]
        right_out[at, width:] = lane_parts(to_column(pot[:, at] * (1.0 / scale)), 0, 3)
    left_out[...] = jnp.dot(source[...], start_map[...].astype(BF16), preferred_element_type=F32).astype(BF16)
    lane = lax.broadcasted_iota(jnp.int32, (CHUNK, LANES), 1)
    ones = jnp.where(lane < 3, 1.0, 0.0).astype(BF16)
    group = 16
    for start in range(0, rows, CHUNK):
        left = jnp.concatenate([left_out[start : start + CHUNK, :], ones], axis=1)
        work[start : start + CHUNK, :] = dot_t(left, right_out[...])
        for at in range(start, start + CHUNK, group):
            tiles = [work[at : at + group, k : k + LANES] for k in range(0, work.shape[1], LANES)]
            peak = functools.reduce(jnp.maximum, tiles)
            peaks[at : at + group, :] = peak
            totals[at : at + group, :] = functools.reduce(jnp.add, [jnp.exp2((tile - peak) * unit) for tile in tiles])
    for part in range(rows // LANES):
        here = slice(part * LANES, (part + 1) * LANES)
        lane_peak = peaks[here, :]
        peak = jnp.max(lane_peak, axis=1, keepdims=True)
        total = jnp.sum(totals[here, :] * jnp.exp2((lane_peak - peak) * unit), axis=1, keepdims=True)
        lse_out[part : part + 1, :] = to_lanes(peak)
        sums[part : part + 1, :] = to_lanes(total)
    lse_out[...] = lse_out[...] + jnp.log(sums[...]) * (1.0 / (unit * math.log(2.0)))


def col_first(group, unit, log_rows, left_in, right, *refs):
    parts, (block_out, pot_out, peak_out, lse_out, left, work) = received(refs, group)
    row_pot = -log_rows - tree_lse(unit, parts)
    pot_out[...] = row_pot
    rows, width = left_in.shape
    cols = right.shape[0]
    left[:, :width] = left_in[...]
    for part in range(rows // LANES):
        left[part * LANES : (part + 1) * LANES, width:] = lane_parts(to_column(row_pot[part : part + 1, :]), 3, 0)
    peak = None
    for start in range(0, rows, CHUNK):
        value = dot_t(left[start : start + CHUNK, :], right[...])
        work[start : start + CHUNK, :] = value
        top = jnp.max(value.reshape(CHUNK // 8, 8, cols), axis=0)
        peak = top if peak is None else jnp.maximum(peak, top)
    peak = jnp.max(peak, axis=0, keepdims=True)
    group_rows = 16

    def sums(step, total):
        for k in range(0, LANES, group_rows):
            at = pl.ds(pl.multiple_of(step * LANES + k, group_rows), group_rows)
            value = jnp.exp2((work[at, :] - peak) * unit)
            block_out[at, :] = value.astype(BF16)
            total = total + value[:8] + value[8:]
        return total

    total = lax.fori_loop(0, rows // LANES, sums, jnp.zeros((8, cols), F32))
    peak_out[...] = peak
    lse_out[...] = peak + jnp.log(jnp.sum(total, axis=0, keepdims=True)) * (1.0 / (unit * math.log(2.0)))


def column_factors(row):
    pieces = [to_column(row[:, at : at + LANES]) for at in range(0, row.shape[1], LANES)]
    return jnp.concatenate(pieces, axis=0)


def row_sums(block, row, sums_out):
    weights = jnp.concatenate(split(column_factors(row)), axis=1)
    for start in range(0, block.shape[0], CHUNK):
        wide = jnp.dot(block[start : start + CHUNK, :], weights, preferred_element_type=F32)
        sums = wide[:, :LANES] + wide[:, LANES:]
        for part in range(CHUNK // LANES):
            at = start // LANES + part
            sums_out[at : at + 1, :] = to_lanes(sums[part * LANES : (part + 1) * LANES])


def row_second(group, unit, log_cols, block, peak, pot, *refs):
    parts, (pot_out, scale_out, sums_out) = received(refs, group)
    lse = tree_lse(unit, parts)
    pot_out[...] = pot[...] - log_cols - lse
    scale = jnp.exp2(unit * (peak[...] - lse))
    scale_out[...] = scale
    row_sums(block, scale, sums_out)


def col_later(group, ratio, block, scale, *refs):
    parts, (sums_out, factor) = received(refs, group)
    factors = ratio / tree_sum(parts)
    rows, cols = block.shape
    for part in range(rows // LANES):
        factor[part * LANES : (part + 1) * LANES, :] = to_column(factors[part : part + 1, :])
    group_rows = 16

    def sums(step, total):
        for k in range(0, LANES, group_rows):
            at = pl.ds(pl.multiple_of(step * LANES + k, group_rows), group_rows)
            value = block[at, :].astype(F32) * jnp.concatenate([factor[at, :]] * (cols // LANES), axis=1)
            total = total + value[:8] + value[8:]
        return total

    total = lax.fori_loop(0, rows // LANES, sums, jnp.zeros((8, cols), F32))
    sums_out[...] = scale[...] * jnp.sum(total, axis=0, keepdims=True)


def row_later(group, block, scale, *refs):
    parts, (sums_out,) = received(refs, group)
    row_sums(block, scale[...] / tree_sum(parts), sums_out)


def row_last(group, unit, block, scale, pot, target, *refs):
    parts, (col_out, sums_out, bary_out) = received(refs, group)
    totals = tree_sum(parts)
    col_out[...] = (EPS * math.log(2.0)) * (unit * pot[...] - jnp.log(totals) * (1.0 / math.log(2.0)))
    factors = column_factors(scale[...] / totals)
    high, low = split(factors)
    lane = lax.broadcasted_iota(jnp.int32, factors.shape, 1)
    sides = jnp.where(lane < LANES // 2, high.astype(F32), low.astype(F32)).astype(BF16)
    scaled = (target[:, : factors.shape[1]].astype(F32) * factors).astype(BF16)
    weights = jnp.concatenate([scaled, sides], axis=1)
    for start in range(0, block.shape[0], CHUNK):
        wide = jnp.dot(block[start : start + CHUNK, :], weights, preferred_element_type=F32)
        bary_out[start : start + CHUNK, :] = wide[:, :LANES]
        sums = wide[:, LANES:] + pltpu.roll(wide[:, LANES:], LANES // 2, 1)
        for part in range(CHUNK // LANES):
            at = start // LANES + part
            sums_out[at : at + 1, :] = to_lanes(sums[part * LANES : (part + 1) * LANES])


def cross_local(group, unit, ratio, source, bary, pot, *refs):
    parts, (row_out, cross_out) = received(refs, group)
    totals = tree_sum(parts)
    row_out[...] = (EPS * math.log(2.0)) * (unit * pot[...] + jnp.log(ratio / totals) * (1.0 / math.log(2.0)))
    inverse = 1.0 / totals
    pieces = []
    for part in range(totals.shape[0]):
        piece = bary[part * LANES : (part + 1) * LANES, :] * to_column(inverse[part : part + 1, :])
        pieces.append(jnp.concatenate(split(piece), axis=1))
    both = jnp.concatenate(pieces, axis=0)
    cross = lax.dot_general(source[...], both, (((0,), (0,)), ((), ())), preferred_element_type=F32)
    width = source.shape[1]
    cross_out[...] = cross[:, :width] + cross[:, width:]


def precise(a, b, axis=1):
    size = a.shape[0]
    both = lax.dot_general(
        jnp.concatenate(split(a), axis=1 - axis),
        jnp.concatenate(split(b), axis=1),
        (((axis,), (0,)), ((), ())),
        preferred_element_type=F32,
    )
    return both[:size, :size] + (both[:size, size:] + both[size:, :size])


def polar(cross_ref, out):
    cross = cross_ref[...]
    iterate = cross / jnp.sqrt(jnp.sum(cross * cross) + 1e-06)
    gram = precise(iterate, iterate, 0)
    for step in range(NEWTON):
        factor = jnp.where(eye_mask(), 1.5, 0.0) - 0.5 * gram
        if step < NEWTON - 1:
            gram = precise(precise(factor, gram), factor)
        iterate = precise(iterate, factor)
    out[...] = iterate


def partners(values, axis):
    size = lax.axis_size(axis)
    got = [lax.ppermute(values[k], axis, [(me, me ^ k) for me in range(size)]) for k in range(size - 1, 0, -1)]
    return got + [values[0]]


def exchange(x, axis):
    size = lax.axis_size(axis)
    if axis == "src":
        return partners([x] * size, axis)
    return [lax.all_to_all(jnp.broadcast_to(x, (size,) + x.shape), axis, 0, 0)]


def scatter(x, axis):
    index = lax.axis_index(axis)
    return partners([lax.dynamic_index_in_dim(x, index ^ k, keepdims=False) for k in range(lax.axis_size(axis))], axis)


def gather(x, axis):
    size = lax.axis_size(axis)
    index = lax.axis_index(axis)
    stacked = jnp.zeros((size,) + x.shape, x.dtype)
    for k, part in zip(range(size - 1, -1, -1), partners([x] * size, axis)):
        stacked = lax.dynamic_update_index_in_dim(stacked, part, index ^ k, 0)
    return stacked


def shards(source, target, start_map, warm_potential):
    rows, width = source.shape
    cols = target.shape[0]
    n_src, n_tgt = lax.axis_size("src"), lax.axis_size("tgt")
    ratio = (cols * n_tgt) / (rows * n_src)
    scale = 1.0 / (math.sqrt(width) * EPS)
    unit = scale / math.log(2.0)
    log_rows, log_cols = math.log(rows * n_src) / scale, math.log(cols * n_tgt) / scale
    row_vec = jax.ShapeDtypeStruct((rows // LANES, LANES), F32)
    col_vec = jax.ShapeDtypeStruct((1, cols), F32)
    pot = warm_potential.reshape(1, cols)
    mac = rows * cols * width

    left, right, lse = call(
        functools.partial(row_first, unit, scale),
        "row_first",
        (
            jax.ShapeDtypeStruct((rows, width), BF16),
            jax.ShapeDtypeStruct((cols, width + LANES), BF16),
            row_vec,
        ),
        scratch=[
            pltpu.VMEM((rows, width), BF16),
            pltpu.VMEM((width, width), F32),
            pltpu.VMEM((cols, width), BF16),
            pltpu.VMEM((1, cols), F32),
            pltpu.VMEM((rows, cols), F32),
            pltpu.VMEM((rows, LANES), F32),
            pltpu.VMEM((rows, LANES), F32),
            pltpu.VMEM(row_vec.shape, F32),
            pltpu.SemaphoreType.DMA((4,)),
        ],
        flops=4 * mac,
        space=pltpu.HBM,
    )(*[pltpu.with_memory_space_constraint(x, pltpu.HBM) for x in (source, start_map, target, pot)])
    block, row_pot, peak, lse = call(
        functools.partial(col_first, n_tgt, unit, log_rows),
        "col_first",
        (jax.ShapeDtypeStruct((rows, cols), BF16), row_vec, col_vec, col_vec),
        scratch=[pltpu.VMEM((rows, width + LANES), BF16), pltpu.VMEM((rows, cols), F32)],
        flops=4 * mac,
    )(left, right, *exchange(lse, "tgt"))
    col_pot, col_scale, sums = call(
        functools.partial(row_second, n_src, unit, log_cols), "row_second", (col_vec, col_vec, row_vec), flops=2 * mac
    )(block, peak, pot * (1.0 / scale), *exchange(lse, "src"))
    col_later_call = call(
        functools.partial(col_later, n_tgt, ratio),
        "col_later",
        col_vec,
        scratch=[pltpu.VMEM((rows, LANES), F32)],
        flops=2 * mac,
    )
    sums = col_later_call(block, col_scale, *exchange(sums, "tgt"))
    sums = call(functools.partial(row_later, n_src), "row_later", row_vec, flops=2 * mac)(
        block, col_scale, *exchange(sums, "src")
    )
    sums = col_later_call(block, col_scale, *exchange(sums, "tgt"))
    col_out, sums, bary = call(
        functools.partial(row_last, n_src, unit),
        "row_last",
        (col_vec, row_vec, jax.ShapeDtypeStruct((rows, width), F32)),
        flops=4 * mac,
    )(block, col_scale, col_pot, right, *exchange(sums, "src"))
    square = jax.ShapeDtypeStruct((width, width), F32)
    row_out, cross = call(
        functools.partial(cross_local, n_tgt, unit, ratio),
        "cross_local",
        (row_vec, square),
        flops=2 * rows * width * width,
    )(source, bary, row_pot, *exchange(sums, "tgt"))
    share = tree_sum(scatter(cross.reshape(n_src, width // n_src, width), "src"))
    share = jnp.sum(exchange(share, "tgt")[0], axis=0)
    new_map = call(polar, "polar", square, flops=1 << 27)(gather(share, "src").reshape(width, width))
    return row_out.reshape(rows), col_out.reshape(cols), new_map


def solution(mesh):
    placed = (P("src", None), P("tgt", None), P(), P("tgt"))
    return jax.shard_map(
        shards, mesh=mesh, in_specs=placed, out_specs=(P("src"), P("tgt"), P()), check_vma=False
    )
```

```python
import functools
import math

import jax
import jax.numpy as jnp
from jax import lax
from jax.experimental import pallas as pl
from jax.experimental.pallas import tpu as pltpu
from jax.sharding import PartitionSpec as P

NEWTON = 10
EPS = 0.05
LANES = 128
CHUNK = 256
VMEM_LIMIT = 40 * 1024 * 1024

F32 = jnp.float32
BF16 = jnp.bfloat16


def call(body, name, out_shape, scratch=(), flops=0, space=pltpu.VMEM):
    return lambda *args: pl.pallas_call(
        body,
        name=name,
        out_shape=out_shape,
        in_specs=[pl.BlockSpec(memory_space=space)] * len(args),
        out_specs=jax.tree.map(lambda _: pl.BlockSpec(memory_space=pltpu.VMEM), out_shape),
        scratch_shapes=scratch,
        compiler_params=pltpu.CompilerParams(vmem_limit_bytes=VMEM_LIMIT),
        cost_estimate=pl.CostEstimate(flops=flops, bytes_accessed=8 << 20, transcendentals=0),
    )(*args)


def eye_mask(shift=0):
    shape = (LANES, LANES)
    row, lane = (lax.broadcasted_iota(jnp.int32, shape, k) for k in range(2))
    return (row + shift) % LANES == lane if shift else row == lane


def to_lanes(column, shift=0):
    wide = jnp.broadcast_to(column, (LANES, LANES))
    return jnp.sum(jnp.where(eye_mask(shift), wide, 0.0), axis=0, keepdims=True)


def to_column(row):
    wide = jnp.broadcast_to(row, (LANES, LANES))
    return jnp.broadcast_to(jnp.sum(jnp.where(eye_mask(), wide, 0.0), axis=1, keepdims=True), (LANES, LANES))


def split(x):
    high = x.astype(BF16)
    return high, (x - high.astype(F32)).astype(BF16)


def lane_parts(wide, first, fill):
    lane = lax.broadcasted_iota(jnp.int32, wide.shape, 1)
    out = jnp.where((lane >= fill) & (lane < fill + 3), 1.0, 0.0)
    rest = wide
    for k in range(3):
        part = rest.astype(BF16).astype(F32)
        out = jnp.where(lane == first + k, part, out)
        rest = rest - part
    return out.astype(BF16)


def tree(combine, values):
    values = list(values)
    while len(values) > 1:
        values = [combine(a, b) for a, b in zip(values[::2], values[1::2])]
    return values[0]


def tree_sum(parts):
    return tree(jnp.add, parts)


def tree_lse(unit, parts):
    peak = tree(jnp.maximum, parts)
    total = tree(jnp.add, [jnp.exp2(unit * (part - peak)) for part in parts])
    return peak + jnp.log(total) * (1.0 / (unit * math.log(2.0)))


def received(refs, group):
    if len(refs[0].shape) == 3:
        return [refs[0][k] for k in range(group)], refs[1:]
    return [ref[...] for ref in refs[:group]], refs[group:]


def dot_t(a, b):
    return lax.dot_general(a, b, (((1,), (1,)), ((), ())), preferred_element_type=F32)


def row_first(
    unit, scale, source_hbm, map_hbm, target_hbm, pot_hbm, left_out, right_out, lse_out, turned_out,
    source, start_map, target, pot, work, peaks, totals, sums, sems,
):
    copies = [
        pltpu.make_async_copy(src, dst, sems.at[k])
        for k, (src, dst) in enumerate(
            [(source_hbm, source), (map_hbm, start_map), (target_hbm, target), (pot_hbm, pot)]
        )
    ]
    for copy in copies:
        copy.start()
    for copy in copies:
        copy.wait()
    width = source.shape[1]
    rows = source.shape[0]
    for part in range(target.shape[0] // LANES):
        at = pl.ds(part * LANES, LANES)
        right_out[at, :width] = target[at, :]
        right_out[at, width:] = lane_parts(to_column(pot[:, at] * (1.0 / scale)), 0, 3)
    left_out[...] = jnp.dot(source[...], start_map[...].astype(BF16), preferred_element_type=F32).astype(BF16)
    for part in range(rows // LANES):
        here = slice(part * LANES, (part + 1) * LANES)
        turned_out[:, here] = source[here, :].T
    lane = lax.broadcasted_iota(jnp.int32, (CHUNK, LANES), 1)
    ones = jnp.where(lane < 3, 1.0, 0.0).astype(BF16)
    group = 16
    for start in range(0, rows, CHUNK):
        left = jnp.concatenate([left_out[start : start + CHUNK, :], ones], axis=1)
        work[start : start + CHUNK, :] = dot_t(left, right_out[...])
        for at in range(start, start + CHUNK, group):
            tiles = [work[at : at + group, k : k + LANES] for k in range(0, work.shape[1], LANES)]
            peak = functools.reduce(jnp.maximum, tiles)
            peaks[at : at + group, :] = peak
            totals[at : at + group, :] = functools.reduce(jnp.add, [jnp.exp2((tile - peak) * unit) for tile in tiles])
    for part in range(rows // LANES):
        here = slice(part * LANES, (part + 1) * LANES)
        lane_peak = peaks[here, :]
        peak = jnp.max(lane_peak, axis=1, keepdims=True)
        total = jnp.sum(totals[here, :] * jnp.exp2((lane_peak - peak) * unit), axis=1, keepdims=True)
        lse_out[part : part + 1, :] = to_lanes(peak)
        sums[part : part + 1, :] = to_lanes(total)
    lse_out[...] = lse_out[...] + jnp.log(sums[...]) * (1.0 / (unit * math.log(2.0)))


def col_first(group, unit, log_rows, left_in, right, *refs):
    parts, (block_out, pot_out, peak_out, lse_out, left, work) = received(refs, group)
    row_pot = -log_rows - tree_lse(unit, parts)
    pot_out[...] = row_pot
    rows, width = left_in.shape
    cols = right.shape[0]
    left[:, :width] = left_in[...]
    for part in range(rows // LANES):
        left[part * LANES : (part + 1) * LANES, width:] = lane_parts(to_column(row_pot[part : part + 1, :]), 3, 0)
    peak = None
    for start in range(0, rows, CHUNK):
        value = dot_t(left[start : start + CHUNK, :], right[...])
        work[start : start + CHUNK, :] = value
        top = jnp.max(value.reshape(CHUNK // 8, 8, cols), axis=0)
        peak = top if peak is None else jnp.maximum(peak, top)
    peak = jnp.max(peak, axis=0, keepdims=True)
    group_rows = 16

    def sums(step, total):
        for k in range(0, LANES, group_rows):
            at = pl.ds(pl.multiple_of(step * LANES + k, group_rows), group_rows)
            value = jnp.exp2((work[at, :] - peak) * unit)
            block_out[at, :] = value.astype(BF16)
            total = total + value[:8] + value[8:]
        return total

    total = lax.fori_loop(0, rows // LANES, sums, jnp.zeros((8, cols), F32))
    peak_out[...] = peak
    lse_out[...] = peak + jnp.log(jnp.sum(total, axis=0, keepdims=True)) * (1.0 / (unit * math.log(2.0)))


def column_factors(row):
    pieces = [to_column(row[:, at : at + LANES]) for at in range(0, row.shape[1], LANES)]
    return jnp.concatenate(pieces, axis=0)


def row_sums(block, row, sums_out):
    weights = jnp.concatenate(split(column_factors(row)), axis=1)
    for start in range(0, block.shape[0], CHUNK):
        wide = jnp.dot(block[start : start + CHUNK, :], weights, preferred_element_type=F32)
        sums = wide[:, :LANES] + wide[:, LANES:]
        for part in range(CHUNK // LANES):
            at = start // LANES + part
            sums_out[at : at + 1, :] = to_lanes(sums[part * LANES : (part + 1) * LANES])


def row_second(group, unit, log_cols, block, peak, pot, *refs):
    parts, (pot_out, scale_out, sums_out) = received(refs, group)
    lse = tree_lse(unit, parts)
    pot_out[...] = pot[...] - log_cols - lse
    scale = jnp.exp2(unit * (peak[...] - lse))
    scale_out[...] = scale
    row_sums(block, scale, sums_out)


def col_later(group, ratio, block, scale, *refs):
    parts, (sums_out, factor) = received(refs, group)
    factors = ratio / tree_sum(parts)
    rows, cols = block.shape
    for part in range(rows // LANES):
        factor[part * LANES : (part + 1) * LANES, :] = to_column(factors[part : part + 1, :])
    group_rows = 16

    def sums(step, total):
        for k in range(0, LANES, group_rows):
            at = pl.ds(pl.multiple_of(step * LANES + k, group_rows), group_rows)
            value = block[at, :].astype(F32) * jnp.concatenate([factor[at, :]] * (cols // LANES), axis=1)
            total = total + value[:8] + value[8:]
        return total

    total = lax.fori_loop(0, rows // LANES, sums, jnp.zeros((8, cols), F32))
    sums_out[...] = scale[...] * jnp.sum(total, axis=0, keepdims=True)


def row_later(group, block, scale, *refs):
    parts, (sums_out,) = received(refs, group)
    row_sums(block, scale[...] / tree_sum(parts), sums_out)


def row_last(group, unit, block, scale, pot, target, *refs):
    parts, (col_out, sums_out, bary_out, other) = received(refs, group)
    totals = tree_sum(parts)
    col_out[...] = (EPS * math.log(2.0)) * (unit * pot[...] - jnp.log(totals) * (1.0 / math.log(2.0)))
    factors = column_factors(scale[...] / totals)
    high, low = split(factors)
    lane = lax.broadcasted_iota(jnp.int32, factors.shape, 1)
    sides = jnp.where(lane < LANES // 2, high.astype(F32), low.astype(F32)).astype(BF16)
    scaled = (target[:, : factors.shape[1]].astype(F32) * factors).astype(BF16)
    weights = jnp.concatenate([scaled, sides], axis=1)
    for start in range(0, block.shape[0], CHUNK):
        wide = jnp.dot(block[start : start + CHUNK, :], weights, preferred_element_type=F32)
        bary_out[start : start + CHUNK, :] = wide[:, :LANES]
        for part in range(CHUNK // LANES):
            at = start // LANES + part
            sides = wide[part * LANES : (part + 1) * LANES, LANES:]
            sums_out[at : at + 1, :] = to_lanes(sides)
            other[at : at + 1, :] = to_lanes(sides, LANES // 2)
    sums_out[...] += pltpu.roll(other[...], LANES // 2, 1)


def cross_local(group, unit, ratio, turned, bary, pot, *refs):
    parts, (row_out, *share_outs, square) = received(refs, group)
    totals = tree_sum(parts)
    row_out[...] = (EPS * math.log(2.0)) * (unit * pot[...] + jnp.log(ratio / totals) * (1.0 / math.log(2.0)))
    inverse = 1.0 / totals
    pieces = []
    for part in range(totals.shape[0]):
        piece = bary[part * LANES : (part + 1) * LANES, :] * to_column(inverse[part : part + 1, :])
        pieces.append(jnp.concatenate(split(piece), axis=1))
    cross = jnp.dot(turned[...], jnp.concatenate(pieces, axis=0), preferred_element_type=F32)
    width = square.shape[0]
    square[...] = cross[:, :width] + cross[:, width:]
    index = lax.axis_index("src")
    count = len(share_outs)
    height = width // count
    for k, out in zip(range(count - 1, -1, -1), share_outs):
        out[...] = square[pl.ds(pl.multiple_of((index ^ k) * height, height), height), :]


def share_sum(*refs):
    total = tree_sum([ref[...] for ref in refs[:-1]])
    for k in range(refs[-1].shape[0]):
        refs[-1][k] = total


def precise(a, b, axis=1):
    ah, al = split(a)
    bh, bl = split(b)
    return lax.dot_general(
        jnp.concatenate([ah, ah, al], axis=axis),
        jnp.concatenate([bh, bl, bh], axis=0),
        (((axis,), (0,)), ((), ())),
        preferred_element_type=F32,
    )


def polar(*refs):
    shares, (out, square) = refs[:-2], refs[-2:]
    index = lax.axis_index("src")
    height = shares[0].shape[0]
    for k, share in enumerate(shares):
        square[pl.ds(pl.multiple_of((index ^ k) * height, height), height), :] = share[...]
    cross = square[...]
    iterate = cross / jnp.sqrt(jnp.sum(cross * cross) + 1e-06)
    gram = precise(iterate, iterate, 0)
    for step in range(NEWTON):
        factor = jnp.where(eye_mask(), 1.5, 0.0) - 0.5 * gram
        if step < NEWTON - 1:
            gram = precise(precise(factor, gram), factor)
        iterate = precise(iterate, factor)
    out[...] = iterate


def partners(values, axis, order):
    size = lax.axis_size(axis)
    return [lax.ppermute(values[k], axis, [(me, me ^ k) for me in range(size)]) if k else values[0] for k in order]


def exchange(x, axis):
    size = lax.axis_size(axis)
    if axis == "src":
        return partners([x] * size, axis, range(size))
    return [lax.all_to_all(jnp.broadcast_to(x, (size,) + x.shape), axis, 0, 0)]


def shards(source, target, start_map, warm_potential):
    rows, width = source.shape
    cols = target.shape[0]
    n_src, n_tgt = lax.axis_size("src"), lax.axis_size("tgt")
    ratio = (cols * n_tgt) / (rows * n_src)
    scale = 1.0 / (math.sqrt(width) * EPS)
    unit = scale / math.log(2.0)
    log_rows, log_cols = math.log(rows * n_src) / scale, math.log(cols * n_tgt) / scale
    row_vec = jax.ShapeDtypeStruct((rows // LANES, LANES), F32)
    col_vec = jax.ShapeDtypeStruct((1, cols), F32)
    pot = warm_potential.reshape(1, cols)
    mac = rows * cols * width

    left, right, lse, turned = call(
        functools.partial(row_first, unit, scale),
        "row_first",
        (
            jax.ShapeDtypeStruct((rows, width), BF16),
            jax.ShapeDtypeStruct((cols, width + LANES), BF16),
            row_vec,
            jax.ShapeDtypeStruct((width, rows), BF16),
        ),
        scratch=[
            pltpu.VMEM((rows, width), BF16),
            pltpu.VMEM((width, width), F32),
            pltpu.VMEM((cols, width), BF16),
            pltpu.VMEM((1, cols), F32),
            pltpu.VMEM((rows, cols), F32),
            pltpu.VMEM((rows, LANES), F32),
            pltpu.VMEM((rows, LANES), F32),
            pltpu.VMEM(row_vec.shape, F32),
            pltpu.SemaphoreType.DMA((4,)),
        ],
        flops=4 * mac,
        space=pltpu.HBM,
    )(*[pltpu.with_memory_space_constraint(x, pltpu.HBM) for x in (source, start_map, target, pot)])
    block, row_pot, peak, lse = call(
        functools.partial(col_first, n_tgt, unit, log_rows),
        "col_first",
        (jax.ShapeDtypeStruct((rows, cols), BF16), row_vec, col_vec, col_vec),
        scratch=[pltpu.VMEM((rows, width + LANES), BF16), pltpu.VMEM((rows, cols), F32)],
        flops=4 * mac,
    )(left, right, *exchange(lse, "tgt"))
    col_pot, col_scale, sums = call(
        functools.partial(row_second, n_src, unit, log_cols), "row_second", (col_vec, col_vec, row_vec), flops=2 * mac
    )(block, peak, pot * (1.0 / scale), *exchange(lse, "src"))
    col_later_call = call(
        functools.partial(col_later, n_tgt, ratio),
        "col_later",
        col_vec,
        scratch=[pltpu.VMEM((rows, LANES), F32)],
        flops=2 * mac,
    )
    sums = col_later_call(block, col_scale, *exchange(sums, "tgt"))
    sums = call(functools.partial(row_later, n_src), "row_later", row_vec, flops=2 * mac)(
        block, col_scale, *exchange(sums, "src")
    )
    sums = col_later_call(block, col_scale, *exchange(sums, "tgt"))
    col_out, sums, bary = call(
        functools.partial(row_last, n_src, unit),
        "row_last",
        (col_vec, row_vec, jax.ShapeDtypeStruct((rows, width), F32)),
        scratch=[pltpu.VMEM(row_vec.shape, F32)],
        flops=4 * mac,
    )(block, col_scale, col_pot, right, *exchange(sums, "src"))
    square = jax.ShapeDtypeStruct((width, width), F32)
    share_shape = (width // n_src, width)
    row_out, *shares = call(
        functools.partial(cross_local, n_tgt, unit, ratio),
        "cross_local",
        (row_vec,) + (jax.ShapeDtypeStruct(share_shape, F32),) * n_src,
        scratch=[pltpu.VMEM((width, width), F32)],
        flops=2 * rows * width * width,
    )(turned, bary, row_pot, *exchange(sums, "tgt"))
    share = call(share_sum, "share_sum", jax.ShapeDtypeStruct((n_tgt,) + share_shape, F32))(
        *partners(shares[::-1], "src", range(n_src - 1, -1, -1))
    )
    share = jnp.sum(lax.all_to_all(share, "tgt", 0, 0), axis=0)
    new_map = call(polar, "polar", square, scratch=[pltpu.VMEM((width, width), F32)], flops=1 << 27)(
        *exchange(share, "src")
    )
    return row_out.reshape(rows), col_out.reshape(cols), new_map


def solution(mesh):
    placed = (P("src", None), P("tgt", None), P(), P("tgt"))
    return jax.shard_map(
        shards, mesh=mesh, in_specs=placed, out_specs=(P("src"), P("tgt"), P()), check_vma=False
    )
```

```python
import functools
import math

import jax
import jax.numpy as jnp
from jax import lax
from jax.experimental import pallas as pl
from jax.experimental.pallas import tpu as pltpu
from jax.sharding import PartitionSpec as P

NEWTON = 10
EPS = 0.05
LANES = 128
CHUNK = 256
VMEM_LIMIT = 40 * 1024 * 1024

F32 = jnp.float32
BF16 = jnp.bfloat16


def call(body, name, out_shape, scratch=(), flops=0, space=pltpu.VMEM):
    return lambda *args: pl.pallas_call(
        body,
        name=name,
        out_shape=out_shape,
        in_specs=[pl.BlockSpec(memory_space=space)] * len(args),
        out_specs=jax.tree.map(lambda _: pl.BlockSpec(memory_space=pltpu.VMEM), out_shape),
        scratch_shapes=scratch,
        compiler_params=pltpu.CompilerParams(vmem_limit_bytes=VMEM_LIMIT),
        cost_estimate=pl.CostEstimate(flops=flops, bytes_accessed=8 << 20, transcendentals=0),
    )(*args)


def eye_mask(shift=0):
    shape = (LANES, LANES)
    row, lane = (lax.broadcasted_iota(jnp.int32, shape, k) for k in range(2))
    return (row + shift) % LANES == lane if shift else row == lane


def to_lanes(column, shift=0):
    wide = jnp.broadcast_to(column, (LANES, LANES))
    return jnp.sum(jnp.where(eye_mask(shift), wide, 0.0), axis=0, keepdims=True)


def to_column(row):
    wide = jnp.broadcast_to(row, (LANES, LANES))
    return jnp.broadcast_to(jnp.sum(jnp.where(eye_mask(), wide, 0.0), axis=1, keepdims=True), (LANES, LANES))


def split(x):
    high = x.astype(BF16)
    return high, (x - high.astype(F32)).astype(BF16)


def lane_parts(wide, first, fill):
    lane = lax.broadcasted_iota(jnp.int32, wide.shape, 1)
    out = jnp.where((lane >= fill) & (lane < fill + 3), 1.0, 0.0)
    rest = wide
    for k in range(3):
        part = rest.astype(BF16).astype(F32)
        out = jnp.where(lane == first + k, part, out)
        rest = rest - part
    return out.astype(BF16)


def tree(combine, values):
    values = list(values)
    while len(values) > 1:
        values = [combine(a, b) for a, b in zip(values[::2], values[1::2])]
    return values[0]


def tree_sum(parts):
    return tree(jnp.add, parts)


def tree_lse(unit, parts):
    peak = tree(jnp.maximum, parts)
    total = tree(jnp.add, [jnp.exp2(unit * (part - peak)) for part in parts])
    return peak + jnp.log(total) * (1.0 / (unit * math.log(2.0)))


def received(refs, group):
    return [refs[0][k] for k in range(group)], refs[1:]


def dot_t(a, b):
    return lax.dot_general(a, b, (((1,), (1,)), ((), ())), preferred_element_type=F32)


def row_first(
    unit, scale, source_hbm, map_hbm, target_hbm, pot_hbm, left_out, right_out, lse_out, turned_out,
    source, start_map, target, pot, work, peaks, totals, sums, sems,
):
    copies = [
        pltpu.make_async_copy(src, dst, sems.at[k])
        for k, (src, dst) in enumerate(
            [(source_hbm, source), (map_hbm, start_map), (target_hbm, target), (pot_hbm, pot)]
        )
    ]
    for copy in copies:
        copy.start()
    for copy in copies:
        copy.wait()
    width = source.shape[1]
    rows = source.shape[0]
    for part in range(target.shape[0] // LANES):
        at = pl.ds(part * LANES, LANES)
        right_out[at, :width] = target[at, :]
        right_out[at, width:] = lane_parts(to_column(pot[:, at] * (1.0 / scale)), 0, 3)
    left_out[...] = jnp.dot(source[...], start_map[...].astype(BF16), preferred_element_type=F32).astype(BF16)
    for part in range(rows // LANES):
        here = slice(part * LANES, (part + 1) * LANES)
        turned_out[:, here] = source[here, :].T
    lane = lax.broadcasted_iota(jnp.int32, (CHUNK, LANES), 1)
    ones = jnp.where(lane < 3, 1.0, 0.0).astype(BF16)
    group = 16
    for start in range(0, rows, CHUNK):
        left = jnp.concatenate([left_out[start : start + CHUNK, :], ones], axis=1)
        work[start : start + CHUNK, :] = dot_t(left, right_out[...])
        for at in range(start, start + CHUNK, group):
            tiles = [work[at : at + group, k : k + LANES] for k in range(0, work.shape[1], LANES)]
            peak = functools.reduce(jnp.maximum, tiles)
            peaks[at : at + group, :] = peak
            totals[at : at + group, :] = functools.reduce(jnp.add, [jnp.exp2((tile - peak) * unit) for tile in tiles])
    for part in range(rows // LANES):
        here = slice(part * LANES, (part + 1) * LANES)
        lane_peak = peaks[here, :]
        peak = jnp.max(lane_peak, axis=1, keepdims=True)
        total = jnp.sum(totals[here, :] * jnp.exp2((lane_peak - peak) * unit), axis=1, keepdims=True)
        lse_out[part : part + 1, :] = to_lanes(peak)
        sums[part : part + 1, :] = to_lanes(total)
    lse_out[...] = lse_out[...] + jnp.log(sums[...]) * (1.0 / (unit * math.log(2.0)))


def col_first(group, unit, log_rows, left_in, right, *refs):
    parts, (block_out, pot_out, peak_out, lse_out, left, work) = received(refs, group)
    row_pot = -log_rows - tree_lse(unit, parts)
    pot_out[...] = row_pot
    rows, width = left_in.shape
    cols = right.shape[0]
    left[:, :width] = left_in[...]
    for part in range(rows // LANES):
        left[part * LANES : (part + 1) * LANES, width:] = lane_parts(to_column(row_pot[part : part + 1, :]), 3, 0)
    peak = None
    for start in range(0, rows, CHUNK):
        value = dot_t(left[start : start + CHUNK, :], right[...])
        work[start : start + CHUNK, :] = value
        top = jnp.max(value.reshape(CHUNK // 8, 8, cols), axis=0)
        peak = top if peak is None else jnp.maximum(peak, top)
    peak = jnp.max(peak, axis=0, keepdims=True)
    group_rows = 16

    def sums(step, total):
        for k in range(0, LANES, group_rows):
            at = pl.ds(pl.multiple_of(step * LANES + k, group_rows), group_rows)
            value = jnp.exp2((work[at, :] - peak) * unit)
            block_out[at, :] = value.astype(BF16)
            total = total + value[:8] + value[8:]
        return total

    total = lax.fori_loop(0, rows // LANES, sums, jnp.zeros((8, cols), F32))
    peak_out[...] = peak
    lse_out[...] = peak + jnp.log(jnp.sum(total, axis=0, keepdims=True)) * (1.0 / (unit * math.log(2.0)))


def column_factors(row):
    pieces = [to_column(row[:, at : at + LANES]) for at in range(0, row.shape[1], LANES)]
    return jnp.concatenate(pieces, axis=0)


def row_sums(block, row, sums_out):
    weights = jnp.concatenate(split(column_factors(row)), axis=1)
    for start in range(0, block.shape[0], CHUNK):
        wide = jnp.dot(block[start : start + CHUNK, :], weights, preferred_element_type=F32)
        sums = wide[:, :LANES] + wide[:, LANES:]
        for part in range(CHUNK // LANES):
            at = start // LANES + part
            sums_out[at : at + 1, :] = to_lanes(sums[part * LANES : (part + 1) * LANES])


def row_second(group, unit, log_cols, block, peak, pot, *refs):
    parts, (pot_out, scale_out, sums_out) = received(refs, group)
    lse = tree_lse(unit, parts)
    pot_out[...] = pot[...] - log_cols - lse
    scale = jnp.exp2(unit * (peak[...] - lse))
    scale_out[...] = scale
    row_sums(block, scale, sums_out)


def col_later(group, ratio, block, scale, *refs):
    parts, (sums_out, factor) = received(refs, group)
    factors = ratio / tree_sum(parts)
    rows, cols = block.shape
    for part in range(rows // LANES):
        factor[part * LANES : (part + 1) * LANES, :] = to_column(factors[part : part + 1, :])
    group_rows = 16

    def sums(step, total):
        for k in range(0, LANES, group_rows):
            at = pl.ds(pl.multiple_of(step * LANES + k, group_rows), group_rows)
            value = block[at, :].astype(F32) * jnp.concatenate([factor[at, :]] * (cols // LANES), axis=1)
            total = total + value[:8] + value[8:]
        return total

    total = lax.fori_loop(0, rows // LANES, sums, jnp.zeros((8, cols), F32))
    sums_out[...] = scale[...] * jnp.sum(total, axis=0, keepdims=True)


def row_later(group, block, scale, *refs):
    parts, (sums_out,) = received(refs, group)
    row_sums(block, scale[...] / tree_sum(parts), sums_out)


def row_last(group, unit, block, scale, pot, target, *refs):
    parts, (col_out, sums_out, bary_out, other) = received(refs, group)
    totals = tree_sum(parts)
    col_out[...] = (EPS * math.log(2.0)) * (unit * pot[...] - jnp.log(totals) * (1.0 / math.log(2.0)))
    factors = column_factors(scale[...] / totals)
    high, low = split(factors)
    lane = lax.broadcasted_iota(jnp.int32, factors.shape, 1)
    sides = jnp.where(lane < LANES // 2, high.astype(F32), low.astype(F32)).astype(BF16)
    scaled = (target[:, : factors.shape[1]].astype(F32) * factors).astype(BF16)
    weights = jnp.concatenate([scaled, sides], axis=1)
    for start in range(0, block.shape[0], CHUNK):
        wide = jnp.dot(block[start : start + CHUNK, :], weights, preferred_element_type=F32)
        bary_out[start : start + CHUNK, :] = wide[:, :LANES]
        for part in range(CHUNK // LANES):
            at = start // LANES + part
            sides = wide[part * LANES : (part + 1) * LANES, LANES:]
            sums_out[at : at + 1, :] = to_lanes(sides)
            other[at : at + 1, :] = to_lanes(sides, LANES // 2)
    sums_out[...] += pltpu.roll(other[...], LANES // 2, 1)


def cross_local(group, unit, ratio, turned, bary, pot, *refs):
    parts, (row_out, cross_out) = received(refs, group)
    totals = tree_sum(parts)
    row_out[...] = (EPS * math.log(2.0)) * (unit * pot[...] + jnp.log(ratio / totals) * (1.0 / math.log(2.0)))
    inverse = 1.0 / totals
    pieces = []
    for part in range(totals.shape[0]):
        piece = bary[part * LANES : (part + 1) * LANES, :] * to_column(inverse[part : part + 1, :])
        pieces.append(jnp.concatenate(split(piece), axis=1))
    cross = jnp.dot(turned[...], jnp.concatenate(pieces, axis=0), preferred_element_type=F32)
    width = cross_out.shape[1]
    cross_out[...] = cross[:, :width] + cross[:, width:]


def share_sum(shares, out):
    total = tree_sum([shares[k] for k in range(shares.shape[0])])
    for k in range(out.shape[0]):
        out[k] = total


def precise(a, b, axis=1):
    ah, al = split(a)
    bh, bl = split(b)
    dims = (((axis,), (0,)), ((), ()))
    return lax.dot_general(
        jnp.concatenate([ah, al], axis=axis), jnp.concatenate([bh, bh], axis=0), dims, preferred_element_type=F32
    ) + lax.dot_general(ah, bl, dims, preferred_element_type=F32)


def polar(cross_ref, out):
    cross = cross_ref[...]
    iterate = cross / jnp.sqrt(jnp.sum(cross * cross) + 1e-06)
    gram = precise(iterate, iterate, 0)
    for step in range(NEWTON):
        factor = jnp.where(eye_mask(), 1.5, 0.0) - 0.5 * gram
        if step < NEWTON - 1:
            gram = precise(precise(factor, gram), factor)
        iterate = precise(iterate, factor)
    out[...] = iterate


def exchange(x, axis):
    return lax.all_to_all(jnp.broadcast_to(x, (lax.axis_size(axis),) + x.shape), axis, 0, 0)


def shards(source, target, start_map, warm_potential):
    rows, width = source.shape
    cols = target.shape[0]
    n_src, n_tgt = lax.axis_size("src"), lax.axis_size("tgt")
    ratio = (cols * n_tgt) / (rows * n_src)
    scale = 1.0 / (math.sqrt(width) * EPS)
    unit = scale / math.log(2.0)
    log_rows, log_cols = math.log(rows * n_src) / scale, math.log(cols * n_tgt) / scale
    row_vec = jax.ShapeDtypeStruct((rows // LANES, LANES), F32)
    col_vec = jax.ShapeDtypeStruct((1, cols), F32)
    pot = warm_potential.reshape(1, cols)
    mac = rows * cols * width

    left, right, lse, turned = call(
        functools.partial(row_first, unit, scale),
        "row_first",
        (
            jax.ShapeDtypeStruct((rows, width), BF16),
            jax.ShapeDtypeStruct((cols, width + LANES), BF16),
            row_vec,
            jax.ShapeDtypeStruct((width, rows), BF16),
        ),
        scratch=[
            pltpu.VMEM((rows, width), BF16),
            pltpu.VMEM((width, width), F32),
            pltpu.VMEM((cols, width), BF16),
            pltpu.VMEM((1, cols), F32),
            pltpu.VMEM((rows, cols), F32),
            pltpu.VMEM((rows, LANES), F32),
            pltpu.VMEM((rows, LANES), F32),
            pltpu.VMEM(row_vec.shape, F32),
            pltpu.SemaphoreType.DMA((4,)),
        ],
        flops=4 * mac,
        space=pltpu.HBM,
    )(*[pltpu.with_memory_space_constraint(x, pltpu.HBM) for x in (source, start_map, target, pot)])
    block, row_pot, peak, lse = call(
        functools.partial(col_first, n_tgt, unit, log_rows),
        "col_first",
        (jax.ShapeDtypeStruct((rows, cols), BF16), row_vec, col_vec, col_vec),
        scratch=[pltpu.VMEM((rows, width + LANES), BF16), pltpu.VMEM((rows, cols), F32)],
        flops=4 * mac,
    )(left, right, exchange(lse, "tgt"))
    col_pot, col_scale, sums = call(
        functools.partial(row_second, n_src, unit, log_cols), "row_second", (col_vec, col_vec, row_vec), flops=2 * mac
    )(block, peak, pot * (1.0 / scale), exchange(lse, "src"))
    col_later_call = call(
        functools.partial(col_later, n_tgt, ratio),
        "col_later",
        col_vec,
        scratch=[pltpu.VMEM((rows, LANES), F32)],
        flops=2 * mac,
    )
    sums = col_later_call(block, col_scale, exchange(sums, "tgt"))
    sums = call(functools.partial(row_later, n_src), "row_later", row_vec, flops=2 * mac)(
        block, col_scale, exchange(sums, "src")
    )
    sums = col_later_call(block, col_scale, exchange(sums, "tgt"))
    col_out, sums, bary = call(
        functools.partial(row_last, n_src, unit),
        "row_last",
        (col_vec, row_vec, jax.ShapeDtypeStruct((rows, width), F32)),
        scratch=[pltpu.VMEM(row_vec.shape, F32)],
        flops=4 * mac,
    )(block, col_scale, col_pot, right, exchange(sums, "src"))
    square = jax.ShapeDtypeStruct((width, width), F32)
    share_shape = (width // n_src, width)
    row_out, cross = call(
        functools.partial(cross_local, n_tgt, unit, ratio),
        "cross_local",
        (row_vec, square),
        flops=2 * rows * width * width,
    )(turned, bary, row_pot, exchange(sums, "tgt"))
    shares = lax.all_to_all(cross.reshape((n_src,) + share_shape), "src", 0, 0)
    share = call(share_sum, "share_sum", jax.ShapeDtypeStruct((n_tgt,) + share_shape, F32))(shares)
    share = jnp.sum(lax.all_to_all(share, "tgt", 0, 0), axis=0)
    cross = exchange(share, "src").reshape(width, width)
    new_map = call(polar, "polar", square, flops=1 << 27)(cross)
    return row_out.reshape(rows), col_out.reshape(cols), new_map


def solution(mesh):
    placed = (P("src", None), P("tgt", None), P(), P("tgt"))
    return jax.shard_map(
        shards, mesh=mesh, in_specs=placed, out_specs=(P("src"), P("tgt"), P()), check_vma=False
    )
```

```python
import functools
import math

import jax
import jax.numpy as jnp
from jax import lax
from jax.experimental import pallas as pl
from jax.experimental.pallas import tpu as pltpu
from jax.sharding import PartitionSpec as P

NEWTON = 10
EPS = 0.05
LANES = 128
CHUNK = 256
VMEM_LIMIT = 40 * 1024 * 1024

F32 = jnp.float32
BF16 = jnp.bfloat16


def call(body, name, out_shape, scratch=(), flops=0, space=pltpu.VMEM):
    return lambda *args: pl.pallas_call(
        body,
        name=name,
        out_shape=out_shape,
        in_specs=[pl.BlockSpec(memory_space=space)] * len(args),
        out_specs=jax.tree.map(lambda _: pl.BlockSpec(memory_space=pltpu.VMEM), out_shape),
        scratch_shapes=scratch,
        compiler_params=pltpu.CompilerParams(vmem_limit_bytes=VMEM_LIMIT),
        cost_estimate=pl.CostEstimate(flops=flops, bytes_accessed=8 << 20, transcendentals=0),
    )(*args)


def eye_mask(shift=0):
    shape = (LANES, LANES)
    row, lane = (lax.broadcasted_iota(jnp.int32, shape, k) for k in range(2))
    return (row + shift) % LANES == lane if shift else row == lane


def to_lanes(column, shift=0):
    wide = jnp.broadcast_to(column, (LANES, LANES))
    return jnp.sum(jnp.where(eye_mask(shift), wide, 0.0), axis=0, keepdims=True)


def to_column(row):
    wide = jnp.broadcast_to(row, (LANES, LANES))
    return jnp.broadcast_to(jnp.sum(jnp.where(eye_mask(), wide, 0.0), axis=1, keepdims=True), (LANES, LANES))


def split(x):
    high = x.astype(BF16)
    return high, (x - high.astype(F32)).astype(BF16)


def lane_parts(wide):
    lane = lax.broadcasted_iota(jnp.int32, wide.shape, 1)
    rest = wide
    out = jnp.zeros_like(wide)
    for k in range(3):
        part = rest.astype(BF16).astype(F32)
        out = jnp.where(lane == k, part, out)
        rest = rest - part
    return out.astype(BF16)


def tree(combine, values):
    values = list(values)
    while len(values) > 1:
        values = [combine(a, b) for a, b in zip(values[::2], values[1::2])]
    return values[0]


def tree_sum(parts):
    return tree(jnp.add, parts)


def tree_lse(unit, parts):
    peak = tree(jnp.maximum, parts)
    total = tree(jnp.add, [jnp.exp2(unit * (part - peak)) for part in parts])
    return peak + jnp.log(total) * (1.0 / (unit * math.log(2.0)))


def received(refs, group):
    if len(refs[0].shape) == 3:
        return [refs[0][k] for k in range(group)], refs[1:]
    return [ref[...] for ref in refs[:group]], refs[group:]


def dot_t(a, b):
    return lax.dot_general(a, b, (((1,), (1,)), ((), ())), preferred_element_type=F32)


def row_first(
    unit, scale, source_hbm, map_hbm, target_hbm, pot_hbm, left_out, right_out, lse_out, turned_out,
    source, start_map, target, pot, work, peaks, totals, sums, sems,
):
    copies = [
        pltpu.make_async_copy(src, dst, sems.at[k])
        for k, (src, dst) in enumerate(
            [(source_hbm, source), (map_hbm, start_map), (target_hbm, target), (pot_hbm, pot)]
        )
    ]
    for copy in copies:
        copy.start()
    for copy in copies:
        copy.wait()
    width = source.shape[1]
    rows = source.shape[0]
    for part in range(target.shape[0] // LANES):
        at = pl.ds(part * LANES, LANES)
        right_out[at, :width] = target[at, :]
        right_out[at, width:] = lane_parts(to_column(pot[:, at] * (1.0 / scale)))
    left_out[...] = jnp.dot(source[...], start_map[...].astype(BF16), preferred_element_type=F32).astype(BF16)
    for part in range(rows // LANES):
        here = slice(part * LANES, (part + 1) * LANES)
        turned_out[:, here] = source[here, :].T
    lane = lax.broadcasted_iota(jnp.int32, (CHUNK, LANES), 1)
    ones = jnp.where(lane < 3, 1.0, 0.0).astype(BF16)
    group = 16
    for start in range(0, rows, CHUNK):
        left = jnp.concatenate([left_out[start : start + CHUNK, :], ones], axis=1)
        work[start : start + CHUNK, :] = dot_t(left, right_out[...])
        for at in range(start, start + CHUNK, group):
            tiles = [work[at : at + group, k : k + LANES] for k in range(0, work.shape[1], LANES)]
            peak = functools.reduce(jnp.maximum, tiles)
            peaks[at : at + group, :] = peak
            totals[at : at + group, :] = functools.reduce(jnp.add, [jnp.exp2((tile - peak) * unit) for tile in tiles])
    for part in range(rows // LANES):
        here = slice(part * LANES, (part + 1) * LANES)
        lane_peak = peaks[here, :]
        peak = jnp.max(lane_peak, axis=1, keepdims=True)
        total = jnp.sum(totals[here, :] * jnp.exp2((lane_peak - peak) * unit), axis=1, keepdims=True)
        lse_out[part : part + 1, :] = to_lanes(peak)
        sums[part : part + 1, :] = to_lanes(total)
    lse_out[...] = lse_out[...] + jnp.log(sums[...]) * (1.0 / (unit * math.log(2.0)))


def col_first(group, unit, log_rows, left_in, own, other, *refs):
    parts, (block_out, target_out, pot_out, peak_out, lse_out, left, right, work) = received(refs, group)
    row_pot = -log_rows - tree_lse(unit, parts)
    pot_out[...] = row_pot
    rows, width = left_in.shape
    half = own.shape[0]
    cols = 2 * half
    odd = lax.axis_index("tgt") & 1
    target_out[pl.ds(pl.multiple_of(odd * half, half), half), :] = own[:, :width]
    target_out[pl.ds(pl.multiple_of((1 - odd) * half, half), half), :] = other[...].astype(BF16)
    right[:, :width] = target_out[...]
    lane = lax.broadcasted_iota(jnp.int32, (cols, LANES), 1)
    right[:, width:] = jnp.where(lane < 3, 1.0, 0.0).astype(BF16)
    left[:, :width] = left_in[...]
    for part in range(rows // LANES):
        left[part * LANES : (part + 1) * LANES, width:] = lane_parts(to_column(row_pot[part : part + 1, :]))
    peak = None
    for start in range(0, rows, CHUNK):
        value = dot_t(left[start : start + CHUNK, :], right[...])
        work[start : start + CHUNK, :] = value
        top = jnp.max(value.reshape(CHUNK // 8, 8, cols), axis=0)
        peak = top if peak is None else jnp.maximum(peak, top)
    peak = jnp.max(peak, axis=0, keepdims=True)
    group_rows = 16

    def sums(step, total):
        for k in range(0, LANES, group_rows):
            at = pl.ds(pl.multiple_of(step * LANES + k, group_rows), group_rows)
            value = jnp.exp2((work[at, :] - peak) * unit)
            block_out[at, :] = value.astype(BF16)
            total = total + value[:8] + value[8:]
        return total

    total = lax.fori_loop(0, rows // LANES, sums, jnp.zeros((8, cols), F32))
    peak_out[...] = peak
    lse_out[...] = peak + jnp.log(jnp.sum(total, axis=0, keepdims=True)) * (1.0 / (unit * math.log(2.0)))


def column_factors(row):
    pieces = [to_column(row[:, at : at + LANES]) for at in range(0, row.shape[1], LANES)]
    return jnp.concatenate(pieces, axis=0)


def row_sums(block, row, sums_out):
    weights = jnp.concatenate(split(column_factors(row)), axis=1)
    for start in range(0, block.shape[0], CHUNK):
        wide = jnp.dot(block[start : start + CHUNK, :], weights, preferred_element_type=F32)
        sums = wide[:, :LANES] + wide[:, LANES:]
        for part in range(CHUNK // LANES):
            at = start // LANES + part
            sums_out[at : at + 1, :] = to_lanes(sums[part * LANES : (part + 1) * LANES])


def row_second(group, unit, log_cols, block, peak, *refs):
    parts, (pot_out, scale_out, sums_out) = received(refs, group)
    lse = tree_lse(unit, parts)
    pot_out[...] = -log_cols - lse
    scale = jnp.exp2(unit * (peak[...] - lse))
    scale_out[...] = scale
    row_sums(block, scale, sums_out)


def col_later(group, ratio, block, scale, *refs):
    parts, (sums_out, factor) = received(refs, group)
    factors = ratio / tree_sum(parts)
    rows, cols = block.shape
    for part in range(rows // LANES):
        factor[part * LANES : (part + 1) * LANES, :] = to_column(factors[part : part + 1, :])
    group_rows = 16

    def sums(step, total):
        for k in range(0, LANES, group_rows):
            at = pl.ds(pl.multiple_of(step * LANES + k, group_rows), group_rows)
            value = block[at, :].astype(F32) * jnp.concatenate([factor[at, :]] * (cols // LANES), axis=1)
            total = total + value[:8] + value[8:]
        return total

    total = lax.fori_loop(0, rows // LANES, sums, jnp.zeros((8, cols), F32))
    sums_out[...] = scale[...] * jnp.sum(total, axis=0, keepdims=True)


def row_later(group, block, scale, *refs):
    parts, (sums_out,) = received(refs, group)
    row_sums(block, scale[...] / tree_sum(parts), sums_out)


def row_last(group, unit, block, scale, pot, target, *refs):
    parts, (col_out, sums_out, bary_out, other) = received(refs, group)
    totals = tree_sum(parts)
    pots = (EPS * math.log(2.0)) * (unit * pot[...] - jnp.log(totals) * (1.0 / math.log(2.0)))
    half = col_out.shape[1]
    col_out[...] = jnp.where((lax.axis_index("tgt") & 1) == 0, pots[:, :half], pots[:, half:])
    factors = column_factors(scale[...] / totals)
    high, low = split(factors)
    lane = lax.broadcasted_iota(jnp.int32, factors.shape, 1)
    sides = jnp.where(lane < LANES // 2, high.astype(F32), low.astype(F32)).astype(BF16)
    scaled = (target[...].astype(F32) * factors).astype(BF16)
    weights = jnp.concatenate([scaled, sides], axis=1)
    for start in range(0, block.shape[0], CHUNK):
        wide = jnp.dot(block[start : start + CHUNK, :], weights, preferred_element_type=F32)
        bary_out[start : start + CHUNK, :] = wide[:, :LANES]
        for part in range(CHUNK // LANES):
            at = start // LANES + part
            sides = wide[part * LANES : (part + 1) * LANES, LANES:]
            sums_out[at : at + 1, :] = to_lanes(sides)
            other[at : at + 1, :] = to_lanes(sides, LANES // 2)
    sums_out[...] += pltpu.roll(other[...], LANES // 2, 1)


def cross_local(group, unit, ratio, turned, bary, pot, *refs):
    parts, (row_out, *share_outs, square) = received(refs, group)
    totals = tree_sum(parts)
    row_out[...] = (EPS * math.log(2.0)) * (unit * pot[...] + jnp.log(ratio / totals) * (1.0 / math.log(2.0)))
    inverse = 1.0 / totals
    pieces = []
    for part in range(totals.shape[0]):
        piece = bary[part * LANES : (part + 1) * LANES, :] * to_column(inverse[part : part + 1, :])
        pieces.append(jnp.concatenate(split(piece), axis=1))
    cross = jnp.dot(turned[...], jnp.concatenate(pieces, axis=0), preferred_element_type=F32)
    width = square.shape[0]
    square[...] = cross[:, :width] + cross[:, width:]
    index = lax.axis_index("src")
    count = len(share_outs)
    height = width // count
    for k, out in zip(range(count - 1, -1, -1), share_outs):
        out[...] = square[pl.ds(pl.multiple_of((index ^ k) * height, height), height), :]


def share_sum(*refs):
    refs[-1][...] = tree_sum([ref[...] for ref in refs[:-1]])


def precise(a, b, axis=1):
    ah, al = split(a)
    bh, bl = split(b)
    return lax.dot_general(
        jnp.concatenate([ah, ah, al], axis=axis),
        jnp.concatenate([bh, bl, bh], axis=0),
        (((axis,), (0,)), ((), ())),
        preferred_element_type=F32,
    )


def polar(*refs):
    shares, (out, square) = refs[:-2], refs[-2:]
    index = lax.axis_index("src")
    height = shares[0].shape[0]
    for k, share in enumerate(shares):
        square[pl.ds(pl.multiple_of((index ^ k) * height, height), height), :] = share[...]
    cross = square[...]
    iterate = cross / jnp.sqrt(jnp.sum(cross * cross) + 1e-06)
    gram = precise(iterate, iterate, 0)
    for step in range(NEWTON):
        factor = jnp.where(eye_mask(), 1.5, 0.0) - 0.5 * gram
        if step < NEWTON - 1:
            gram = precise(precise(factor, gram), factor)
        iterate = precise(iterate, factor)
    out[...] = iterate


def partners(values, axis, order):
    size = lax.axis_size(axis)
    return [lax.ppermute(values[k], axis, [(me, me ^ k) for me in range(size)]) if k else values[0] for k in order]


def over_src(x):
    size = lax.axis_size("src")
    return partners([x] * size, "src", range(size))


def over_pairs(x):
    size = lax.axis_size("tgt")
    return partners([x] * size, "tgt", range(0, size, 2))


def over_tgt(x):
    return lax.all_to_all(jnp.broadcast_to(x, (lax.axis_size("tgt"),) + x.shape), "tgt", 0, 0)


def shards(source, target, start_map, warm_potential):
    rows, width = source.shape
    cols = target.shape[0]
    n_src, n_tgt = lax.axis_size("src"), lax.axis_size("tgt")
    ratio = (cols * n_tgt) / (rows * n_src)
    scale = 1.0 / (math.sqrt(width) * EPS)
    unit = scale / math.log(2.0)
    log_rows, log_cols = math.log(rows * n_src) / scale, math.log(cols * n_tgt) / scale
    n_pairs = n_tgt // 2
    row_vec = jax.ShapeDtypeStruct((rows // LANES, LANES), F32)
    pair_vec = jax.ShapeDtypeStruct((1, 2 * cols), F32)
    mac = rows * cols * width

    other = lax.ppermute(target.astype(F32), "tgt", [(me, me ^ 1) for me in range(n_tgt)])
    left, right, lse, turned = call(
        functools.partial(row_first, unit, scale),
        "row_first",
        (
            jax.ShapeDtypeStruct((rows, width), BF16),
            jax.ShapeDtypeStruct((cols, width + LANES), BF16),
            row_vec,
            jax.ShapeDtypeStruct((width, rows), BF16),
        ),
        scratch=[
            pltpu.VMEM((rows, width), BF16),
            pltpu.VMEM((width, width), F32),
            pltpu.VMEM((cols, width), BF16),
            pltpu.VMEM((1, cols), F32),
            pltpu.VMEM((rows, cols), F32),
            pltpu.VMEM((rows, LANES), F32),
            pltpu.VMEM((rows, LANES), F32),
            pltpu.VMEM(row_vec.shape, F32),
            pltpu.SemaphoreType.DMA((4,)),
        ],
        flops=4 * mac,
        space=pltpu.HBM,
    )(*[pltpu.with_memory_space_constraint(x, pltpu.HBM) for x in (source, start_map, target, warm_potential.reshape(1, cols))])
    block, targets, row_pot, peak, lse = call(
        functools.partial(col_first, n_tgt, unit, log_rows),
        "col_first",
        (
            jax.ShapeDtypeStruct((rows, 2 * cols), BF16),
            jax.ShapeDtypeStruct((2 * cols, width), BF16),
            row_vec,
            pair_vec,
            pair_vec,
        ),
        scratch=[
            pltpu.VMEM((rows, width + LANES), BF16),
            pltpu.VMEM((2 * cols, width + LANES), BF16),
            pltpu.VMEM((rows, 2 * cols), F32),
        ],
        flops=8 * mac,
    )(left, right, other, over_tgt(lse))
    col_pot, col_scale, sums = call(
        functools.partial(row_second, n_src, unit, log_cols), "row_second", (pair_vec, pair_vec, row_vec), flops=4 * mac
    )(block, peak, *over_src(lse))
    col_later_call = call(
        functools.partial(col_later, n_pairs, ratio),
        "col_later",
        pair_vec,
        scratch=[pltpu.VMEM((rows, LANES), F32)],
        flops=4 * mac,
    )
    sums = col_later_call(block, col_scale, *over_pairs(sums))
    sums = call(functools.partial(row_later, n_src), "row_later", row_vec, flops=4 * mac)(
        block, col_scale, *over_src(sums)
    )
    sums = col_later_call(block, col_scale, *over_pairs(sums))
    col_out, sums, bary = call(
        functools.partial(row_last, n_src, unit),
        "row_last",
        (jax.ShapeDtypeStruct((1, cols), F32), row_vec, jax.ShapeDtypeStruct((rows, width), F32)),
        scratch=[pltpu.VMEM(row_vec.shape, F32)],
        flops=4 * mac,
    )(block, col_scale, col_pot, targets, *over_src(sums))
    square = jax.ShapeDtypeStruct((width, width), F32)
    share_shape = jax.ShapeDtypeStruct((width // n_src, width), F32)
    row_out, *shares = call(
        functools.partial(cross_local, n_pairs, unit, ratio),
        "cross_local",
        (row_vec,) + (share_shape,) * n_src,
        scratch=[pltpu.VMEM((width, width), F32)],
        flops=2 * rows * width * width,
    )(turned, bary, row_pot, *over_pairs(sums))
    share = call(share_sum, "share_sum", share_shape)(*partners(shares[::-1], "src", range(n_src - 1, -1, -1)))
    share = call(share_sum, "share_sum", share_shape)(*over_pairs(share))
    new_map = call(polar, "polar", square, scratch=[pltpu.VMEM((width, width), F32)], flops=1 << 27)(*over_src(share))
    return row_out.reshape(rows), col_out.reshape(cols), new_map


def solution(mesh):
    placed = (P("src", None), P("tgt", None), P(), P("tgt"))
    return jax.shard_map(
        shards, mesh=mesh, in_specs=placed, out_specs=(P("src"), P("tgt"), P()), check_vma=False
    )
```

```python
import functools
import math

import jax
import jax.numpy as jnp
from jax import lax
from jax.experimental import pallas as pl
from jax.experimental.pallas import tpu as pltpu
from jax.sharding import PartitionSpec as P

NEWTON = 10
EPS = 0.05
LANES = 128
CHUNK = 256
VMEM_LIMIT = 40 * 1024 * 1024

F32 = jnp.float32
BF16 = jnp.bfloat16


def call(body, name, out_shape, scratch=(), flops=0, space=pltpu.VMEM):
    return lambda *args: pl.pallas_call(
        body,
        name=name,
        out_shape=out_shape,
        in_specs=[pl.BlockSpec(memory_space=space)] * len(args),
        out_specs=jax.tree.map(lambda _: pl.BlockSpec(memory_space=pltpu.VMEM), out_shape),
        scratch_shapes=scratch,
        compiler_params=pltpu.CompilerParams(vmem_limit_bytes=VMEM_LIMIT),
        cost_estimate=pl.CostEstimate(flops=flops, bytes_accessed=8 << 20, transcendentals=0),
    )(*args)


def eye_mask(shift=0):
    shape = (LANES, LANES)
    row, lane = (lax.broadcasted_iota(jnp.int32, shape, k) for k in range(2))
    return (row + shift) % LANES == lane if shift else row == lane


def to_lanes(column, shift=0):
    wide = jnp.broadcast_to(column, (LANES, LANES))
    return jnp.sum(jnp.where(eye_mask(shift), wide, 0.0), axis=0, keepdims=True)


def to_column(row):
    wide = jnp.broadcast_to(row, (LANES, LANES))
    return jnp.broadcast_to(jnp.sum(jnp.where(eye_mask(), wide, 0.0), axis=1, keepdims=True), (LANES, LANES))


def split(x):
    high = x.astype(BF16)
    return high, (x - high.astype(F32)).astype(BF16)


def lane_parts(wide):
    lane = lax.broadcasted_iota(jnp.int32, wide.shape, 1)
    rest = wide
    out = jnp.zeros_like(wide)
    for k in range(3):
        part = rest.astype(BF16).astype(F32)
        out = jnp.where(lane == k, part, out)
        rest = rest - part
    return out.astype(BF16)


def tree(combine, values):
    values = list(values)
    while len(values) > 1:
        values = [combine(a, b) for a, b in zip(values[::2], values[1::2])]
    return values[0]


def tree_sum(parts):
    return tree(jnp.add, parts)


def tree_lse(unit, parts):
    peak = tree(jnp.maximum, parts)
    total = tree(jnp.add, [jnp.exp2(unit * (part - peak)) for part in parts])
    return peak + jnp.log(total) * (1.0 / (unit * math.log(2.0)))


def received(refs, group):
    if len(refs[0].shape) == 3:
        return [refs[0][k] for k in range(group)], refs[1:]
    return [ref[...] for ref in refs[:group]], refs[group:]


def dot_t(a, b):
    return lax.dot_general(a, b, (((1,), (1,)), ((), ())), preferred_element_type=F32)


def row_first(
    unit, scale, source_hbm, map_hbm, target_hbm, pot_hbm, left_out, right_out, lse_out, turned_out, plain_out,
    source, start_map, target, pot, work, peaks, totals, sums, sems,
):
    copies = [
        pltpu.make_async_copy(src, dst, sems.at[k])
        for k, (src, dst) in enumerate(
            [(source_hbm, source), (map_hbm, start_map), (target_hbm, target), (pot_hbm, pot)]
        )
    ]
    for copy in copies:
        copy.start()
    for copy in copies:
        copy.wait()
    width = source.shape[1]
    rows = source.shape[0]
    for part in range(target.shape[0] // LANES):
        at = pl.ds(part * LANES, LANES)
        right_out[at, :width] = target[at, :]
        right_out[at, width:] = lane_parts(to_column(pot[:, at] * (1.0 / scale)))
    left_out[...] = jnp.dot(source[...], start_map[...].astype(BF16), preferred_element_type=F32).astype(BF16)
    plain_out[...] = target[...].astype(F32)
    for part in range(rows // LANES):
        here = slice(part * LANES, (part + 1) * LANES)
        turned_out[:, here] = source[here, :].T
    lane = lax.broadcasted_iota(jnp.int32, (CHUNK, LANES), 1)
    ones = jnp.where(lane < 3, 1.0, 0.0).astype(BF16)
    group = 16
    for start in range(0, rows, CHUNK):
        left = jnp.concatenate([left_out[start : start + CHUNK, :], ones], axis=1)
        work[start : start + CHUNK, :] = dot_t(left, right_out[...])
        for at in range(start, start + CHUNK, group):
            tiles = [work[at : at + group, k : k + LANES] for k in range(0, work.shape[1], LANES)]
            peak = functools.reduce(jnp.maximum, tiles)
            peaks[at : at + group, :] = peak
            totals[at : at + group, :] = functools.reduce(jnp.add, [jnp.exp2((tile - peak) * unit) for tile in tiles])
    for part in range(rows // LANES):
        here = slice(part * LANES, (part + 1) * LANES)
        lane_peak = peaks[here, :]
        peak = jnp.max(lane_peak, axis=1, keepdims=True)
        total = jnp.sum(totals[here, :] * jnp.exp2((lane_peak - peak) * unit), axis=1, keepdims=True)
        lse_out[part : part + 1, :] = to_lanes(peak)
        sums[part : part + 1, :] = to_lanes(total)
    lse_out[...] = lse_out[...] + jnp.log(sums[...]) * (1.0 / (unit * math.log(2.0)))


def col_first(group, unit, log_rows, left_in, own, other, *refs):
    parts, (block_out, target_out, pot_out, peak_out, lse_out, left, right, *work) = received(refs, group)
    row_pot = -log_rows - tree_lse(unit, parts)
    pot_out[...] = row_pot
    rows, width = left_in.shape
    half = own.shape[0]
    cols = 2 * half
    odd = lax.axis_index("tgt") & 1
    target_out[pl.ds(pl.multiple_of(odd * half, half), half), :] = own[:, :width]
    target_out[pl.ds(pl.multiple_of((1 - odd) * half, half), half), :] = other[...].astype(BF16)
    right[:, :width] = target_out[...]
    lane = lax.broadcasted_iota(jnp.int32, (cols, LANES), 1)
    right[:, width:] = jnp.where(lane < 3, 1.0, 0.0).astype(BF16)
    left[:, :width] = left_in[...]
    for part in range(rows // LANES):
        left[part * LANES : (part + 1) * LANES, width:] = lane_parts(to_column(row_pot[part : part + 1, :]))
    span = work[0].shape[1]
    spans = [slice(at, at + span) for at in range(0, cols, span)]
    low = jnp.full((8, span), -jnp.inf, F32)

    def chunk_of(step):
        return pl.ds(pl.multiple_of(step * CHUNK, CHUNK), CHUNK)

    def product(step, top, k):
        value = dot_t(left[chunk_of(step), :], right[spans[k], :])
        work[k % 2][chunk_of(step), :] = value
        return jnp.maximum(top, jnp.max(value.reshape(CHUNK // 8, 8, span), axis=0))

    def weigh(step, total, k, peak):
        for at in range(0, CHUNK, 16):
            here = pl.ds(pl.multiple_of(step * CHUNK + at, 16), 16)
            value = jnp.exp2((work[k % 2][here, :] - peak) * unit)
            block_out[here, spans[k]] = value.astype(BF16)
            total = total + value[:8] + value[8:]
        return total

    top = lax.fori_loop(0, rows // CHUNK, functools.partial(product, k=0), low)
    for k in range(len(spans)):
        peak = jnp.max(top, axis=0, keepdims=True)

        def both(step, carry):
            total, top = carry
            if k + 1 < len(spans):
                top = product(step, top, k + 1)
            return weigh(step, total, k, peak), top

        total, top = lax.fori_loop(0, rows // CHUNK, both, (jnp.zeros((8, span), F32), low))
        peak_out[:, spans[k]] = peak
        lse_out[:, spans[k]] = peak + jnp.log(jnp.sum(total, axis=0, keepdims=True)) * (1.0 / (unit * math.log(2.0)))


def column_factors(row):
    pieces = [to_column(row[:, at : at + LANES]) for at in range(0, row.shape[1], LANES)]
    return jnp.concatenate(pieces, axis=0)


def row_sums(block, row, sums_out):
    rows, cols = block.shape
    cut = cols * 5 // 8 // 256 * 256
    weights = jnp.concatenate(split(column_factors(row[:, :cut])), axis=1)
    tiles = [(at, jnp.broadcast_to(row[:, at : at + LANES], (16, LANES))) for at in range(cut, cols, LANES)]
    for start in range(0, rows, CHUNK):
        wide = jnp.dot(block[start : start + CHUNK, :cut], weights, preferred_element_type=F32)
        rest = []
        for here in range(start, start + CHUNK, 16):
            terms = [block[here : here + 16, at : at + LANES].astype(F32) * factor for at, factor in tiles]
            rest.append(jnp.sum(functools.reduce(jnp.add, terms), axis=1, keepdims=True))
        sums = wide[:, :LANES] + wide[:, LANES:] + jnp.concatenate(rest, axis=0)
        for part in range(CHUNK // LANES):
            at = start // LANES + part
            sums_out[at : at + 1, :] = to_lanes(sums[part * LANES : (part + 1) * LANES])


def row_second(group, unit, log_cols, block, peak, *refs):
    parts, (pot_out, scale_out, sums_out) = received(refs, group)
    lse = tree_lse(unit, parts)
    pot_out[...] = -log_cols - lse
    scale = jnp.exp2(unit * (peak[...] - lse))
    scale_out[...] = scale
    row_sums(block, scale, sums_out)


def col_later(group, ratio, block, scale, *refs):
    parts, (sums_out,) = received(refs, group)
    factors = ratio / tree_sum(parts)
    rows, cols = block.shape
    cut = cols // 2
    row = jnp.concatenate([factors[k : k + 1, :] for k in range(rows // LANES)], axis=1)
    high, low = split(row)
    pair = jnp.concatenate([high.astype(F32), low.astype(F32), jnp.zeros((14, rows), F32)], axis=0).astype(BF16)
    product = jnp.zeros((16, cut), F32)
    total = jnp.zeros((8, cols - cut), F32)
    for start in range(0, rows, CHUNK):
        product += jnp.dot(pair[:, start : start + CHUNK], block[start : start + CHUNK, :cut], preferred_element_type=F32)
        for part in range(start // LANES, (start + CHUNK) // LANES):
            column = to_column(factors[part : part + 1, :])
            for at in range(0, LANES, 16):
                here = slice(part * LANES + at, part * LANES + at + 16)
                factor = jnp.concatenate([column[at : at + 16]] * ((cols - cut) // LANES), axis=1)
                value = block[here, cut:].astype(F32) * factor
                total = total + value[:8] + value[8:]
    sums_out[:, :cut] = scale[:, :cut] * (product[0:1] + product[1:2])
    sums_out[:, cut:] = scale[:, cut:] * jnp.sum(total, axis=0, keepdims=True)


def row_later(group, block, scale, *refs):
    parts, (sums_out,) = received(refs, group)
    row_sums(block, scale[...] / tree_sum(parts), sums_out)


def row_last(group, unit, block, scale, pot, target, *refs):
    parts, (col_out, sums_out, bary_out, other) = received(refs, group)
    totals = tree_sum(parts)
    pots = (EPS * math.log(2.0)) * (unit * pot[...] - jnp.log(totals) * (1.0 / math.log(2.0)))
    half = col_out.shape[1]
    col_out[...] = jnp.where((lax.axis_index("tgt") & 1) == 0, pots[:, :half], pots[:, half:])
    factors = column_factors(scale[...] / totals)
    high, low = split(factors)
    lane = lax.broadcasted_iota(jnp.int32, factors.shape, 1)
    sides = jnp.where(lane < LANES // 2, high.astype(F32), low.astype(F32)).astype(BF16)
    scaled = (target[...].astype(F32) * factors).astype(BF16)
    weights = jnp.concatenate([scaled, sides], axis=1)
    for start in range(0, block.shape[0], CHUNK):
        wide = jnp.dot(block[start : start + CHUNK, :], weights, preferred_element_type=F32)
        bary_out[start : start + CHUNK, :] = wide[:, :LANES]
        for part in range(CHUNK // LANES):
            at = start // LANES + part
            sides = wide[part * LANES : (part + 1) * LANES, LANES:]
            sums_out[at : at + 1, :] = to_lanes(sides)
            other[at : at + 1, :] = to_lanes(sides, LANES // 2)
    sums_out[...] += pltpu.roll(other[...], LANES // 2, 1)


def cross_local(group, unit, ratio, turned, bary, pot, *refs):
    parts, (row_out, *share_outs, square) = received(refs, group)
    totals = tree_sum(parts)
    row_out[...] = (EPS * math.log(2.0)) * (unit * pot[...] + jnp.log(ratio / totals) * (1.0 / math.log(2.0)))
    inverse = 1.0 / totals
    pieces = []
    for part in range(totals.shape[0]):
        piece = bary[part * LANES : (part + 1) * LANES, :] * to_column(inverse[part : part + 1, :])
        pieces.append(jnp.concatenate(split(piece), axis=1))
    cross = jnp.dot(turned[...], jnp.concatenate(pieces, axis=0), preferred_element_type=F32)
    width = square.shape[0]
    square[...] = cross[:, :width] + cross[:, width:]
    index = lax.axis_index("src")
    count = len(share_outs)
    height = width // count
    for k, out in zip(range(count - 1, -1, -1), share_outs):
        out[...] = square[pl.ds(pl.multiple_of((index ^ k) * height, height), height), :]


def share_sum(*refs):
    refs[-1][...] = tree_sum([ref[...] for ref in refs[:-1]])


def precise(a, b, axis=1):
    ah, al = split(a)
    bh, bl = split(b)
    return lax.dot_general(
        jnp.concatenate([ah, ah, al], axis=axis),
        jnp.concatenate([bh, bl, bh], axis=0),
        (((axis,), (0,)), ((), ())),
        preferred_element_type=F32,
    )


def polar(*refs):
    shares, (out, square) = refs[:-2], refs[-2:]
    index = lax.axis_index("src")
    height = shares[0].shape[0]
    for k, share in enumerate(shares):
        square[pl.ds(pl.multiple_of((index ^ k) * height, height), height), :] = share[...]
    cross = square[...]
    iterate = cross / jnp.sqrt(jnp.sum(cross * cross) + 1e-06)
    gram = precise(iterate, iterate, 0)
    for step in range(NEWTON):
        factor = jnp.where(eye_mask(), 1.5, 0.0) - 0.5 * gram
        if step < NEWTON - 1:
            gram = precise(precise(factor, gram), factor)
        iterate = precise(iterate, factor)
    out[...] = iterate


def partners(values, axis, order):
    size = lax.axis_size(axis)
    return [lax.ppermute(values[k], axis, [(me, me ^ k) for me in range(size)]) if k else values[0] for k in order]


def over_src(x):
    size = lax.axis_size("src")
    return partners([x] * size, "src", range(size))


def over_pairs(x):
    size = lax.axis_size("tgt")
    return partners([x] * size, "tgt", range(0, size, 2))


def over_tgt(x):
    return lax.all_to_all(jnp.broadcast_to(x, (lax.axis_size("tgt"),) + x.shape), "tgt", 0, 0)


def shards(source, target, start_map, warm_potential):
    rows, width = source.shape
    cols = target.shape[0]
    n_src, n_tgt = lax.axis_size("src"), lax.axis_size("tgt")
    ratio = (cols * n_tgt) / (rows * n_src)
    scale = 1.0 / (math.sqrt(width) * EPS)
    unit = scale / math.log(2.0)
    log_rows, log_cols = math.log(rows * n_src) / scale, math.log(cols * n_tgt) / scale
    n_pairs = n_tgt // 2
    row_vec = jax.ShapeDtypeStruct((rows // LANES, LANES), F32)
    pair_vec = jax.ShapeDtypeStruct((1, 2 * cols), F32)
    mac = rows * cols * width

    left, right, lse, turned, plain = call(
        functools.partial(row_first, unit, scale),
        "row_first",
        (
            jax.ShapeDtypeStruct((rows, width), BF16),
            jax.ShapeDtypeStruct((cols, width + LANES), BF16),
            row_vec,
            jax.ShapeDtypeStruct((width, rows), BF16),
            jax.ShapeDtypeStruct((cols, width), F32),
        ),
        scratch=[
            pltpu.VMEM((rows, width), BF16),
            pltpu.VMEM((width, width), F32),
            pltpu.VMEM((cols, width), BF16),
            pltpu.VMEM((1, cols), F32),
            pltpu.VMEM((rows, cols), F32),
            pltpu.VMEM((rows, LANES), F32),
            pltpu.VMEM((rows, LANES), F32),
            pltpu.VMEM(row_vec.shape, F32),
            pltpu.SemaphoreType.DMA((4,)),
        ],
        flops=4 * mac,
        space=pltpu.HBM,
    )(*[pltpu.with_memory_space_constraint(x, pltpu.HBM) for x in (source, start_map, target, warm_potential.reshape(1, cols))])
    other = lax.ppermute(plain, "tgt", [(me, me ^ 1) for me in range(n_tgt)])
    block, targets, row_pot, peak, lse = call(
        functools.partial(col_first, n_tgt, unit, log_rows),
        "col_first",
        (
            jax.ShapeDtypeStruct((rows, 2 * cols), BF16),
            jax.ShapeDtypeStruct((2 * cols, width), BF16),
            row_vec,
            pair_vec,
            pair_vec,
        ),
        scratch=[
            pltpu.VMEM((rows, width + LANES), BF16),
            pltpu.VMEM((2 * cols, width + LANES), BF16),
            pltpu.VMEM((rows, math.gcd(2 * cols, 512)), F32),
            pltpu.VMEM((rows, math.gcd(2 * cols, 512)), F32),
        ],
        flops=8 * mac,
    )(left, right, other, over_tgt(lse))
    col_pot, col_scale, sums = call(
        functools.partial(row_second, n_src, unit, log_cols), "row_second", (pair_vec, pair_vec, row_vec), flops=4 * mac
    )(block, peak, *over_src(lse))
    col_later_call = call(
        functools.partial(col_later, n_pairs, ratio),
        "col_later",
        pair_vec,
        flops=4 * mac,
    )
    sums = col_later_call(block, col_scale, *over_pairs(sums))
    sums = call(functools.partial(row_later, n_src), "row_later", row_vec, flops=4 * mac)(
        block, col_scale, *over_src(sums)
    )
    sums = col_later_call(block, col_scale, *over_pairs(sums))
    col_out, sums, bary = call(
        functools.partial(row_last, n_src, unit),
        "row_last",
        (jax.ShapeDtypeStruct((1, cols), F32), row_vec, jax.ShapeDtypeStruct((rows, width), F32)),
        scratch=[pltpu.VMEM(row_vec.shape, F32)],
        flops=4 * mac,
    )(block, col_scale, col_pot, targets, *over_src(sums))
    square = jax.ShapeDtypeStruct((width, width), F32)
    share_shape = jax.ShapeDtypeStruct((width // n_src, width), F32)
    row_out, *shares = call(
        functools.partial(cross_local, n_pairs, unit, ratio),
        "cross_local",
        (row_vec,) + (share_shape,) * n_src,
        scratch=[pltpu.VMEM((width, width), F32)],
        flops=2 * rows * width * width,
    )(turned, bary, row_pot, *over_pairs(sums))
    share = call(share_sum, "share_sum", share_shape)(*partners(shares[::-1], "src", range(n_src - 1, -1, -1)))
    share = call(share_sum, "share_sum", share_shape)(*over_pairs(share))
    new_map = call(polar, "polar", square, scratch=[pltpu.VMEM((width, width), F32)], flops=1 << 27)(*over_src(share))
    return row_out.reshape(rows), col_out.reshape(cols), new_map


def solution(mesh):
    placed = (P("src", None), P("tgt", None), P(), P("tgt"))
    return jax.shard_map(
        shards, mesh=mesh, in_specs=placed, out_specs=(P("src"), P("tgt"), P()), check_vma=False
    )
```

```python
import functools
import math

import jax
import jax.numpy as jnp
from jax import lax
from jax.experimental import pallas as pl
from jax.experimental.pallas import tpu as pltpu
from jax.sharding import PartitionSpec as P

NEWTON = 10
EPS = 0.05
LANES = 128
CHUNK = 256
VMEM_LIMIT = 40 * 1024 * 1024

F32 = jnp.float32
BF16 = jnp.bfloat16


def call(body, name, out_shape, scratch=(), flops=0, space=pltpu.VMEM):
    return lambda *args: pl.pallas_call(
        body,
        name=name,
        out_shape=out_shape,
        in_specs=[pl.BlockSpec(memory_space=space)] * len(args),
        out_specs=jax.tree.map(lambda _: pl.BlockSpec(memory_space=pltpu.VMEM), out_shape),
        scratch_shapes=scratch,
        compiler_params=pltpu.CompilerParams(vmem_limit_bytes=VMEM_LIMIT),
        cost_estimate=pl.CostEstimate(flops=flops, bytes_accessed=8 << 20, transcendentals=0),
    )(*args)


def eye_mask(shift=0):
    shape = (LANES, LANES)
    row, lane = (lax.broadcasted_iota(jnp.int32, shape, k) for k in range(2))
    return (row + shift) % LANES == lane if shift else row == lane


def to_lanes(column, shift=0):
    wide = jnp.broadcast_to(column, (LANES, LANES))
    return jnp.sum(jnp.where(eye_mask(shift), wide, 0.0), axis=0, keepdims=True)


def to_column(row):
    wide = jnp.broadcast_to(row, (LANES, LANES))
    return jnp.broadcast_to(jnp.sum(jnp.where(eye_mask(), wide, 0.0), axis=1, keepdims=True), (LANES, LANES))


def split(x):
    high = x.astype(BF16)
    return high, (x - high.astype(F32)).astype(BF16)


def lane_parts(wide):
    lane = lax.broadcasted_iota(jnp.int32, wide.shape, 1)
    rest = wide
    out = jnp.zeros_like(wide)
    for k in range(3):
        part = rest.astype(BF16).astype(F32)
        out = jnp.where(lane == k, part, out)
        rest = rest - part
    return out.astype(BF16)


def tree(combine, values):
    values = list(values)
    while len(values) > 1:
        values = [combine(a, b) for a, b in zip(values[::2], values[1::2])]
    return values[0]


def tree_sum(parts):
    return tree(jnp.add, parts)


def tree_lse(unit, parts):
    peak = tree(jnp.maximum, parts)
    total = tree(jnp.add, [jnp.exp2(unit * (part - peak)) for part in parts])
    return peak + jnp.log(total) * (1.0 / (unit * math.log(2.0)))


def received(refs, group):
    if len(refs[0].shape) == 3:
        return [refs[0][k] for k in range(group)], refs[1:]
    return [ref[...] for ref in refs[:group]], refs[group:]


def dot_t(a, b):
    return lax.dot_general(a, b, (((1,), (1,)), ((), ())), preferred_element_type=F32)


def prepare(
    scale, source_hbm, map_hbm, target_hbm, pot_hbm, left_out, right_out, turned_out, plain_out,
    source, start_map, target, pot, sems,
):
    copies = [
        pltpu.make_async_copy(src, dst, sems.at[k])
        for k, (src, dst) in enumerate(
            [(source_hbm, source), (map_hbm, start_map), (target_hbm, target), (pot_hbm, pot)]
        )
    ]
    for copy in copies:
        copy.start()
    for copy in copies:
        copy.wait()
    width = source.shape[1]
    plain_out[...] = target[...].astype(F32)
    for part in range(target.shape[0] // LANES):
        at = pl.ds(part * LANES, LANES)
        right_out[at, :width] = target[at, :]
        right_out[at, width:] = lane_parts(to_column(pot[:, at] * (1.0 / scale)))
    left_out[...] = jnp.dot(source[...], start_map[...].astype(BF16), preferred_element_type=F32).astype(BF16)
    for part in range(source.shape[0] // LANES):
        here = slice(part * LANES, (part + 1) * LANES)
        turned_out[:, here] = source[here, :].T


def row_first(unit, left_in, right, lse_out, work, peaks, totals, sums):
    rows = left_in.shape[0]
    lane = lax.broadcasted_iota(jnp.int32, (CHUNK, LANES), 1)
    ones = jnp.where(lane < 3, 1.0, 0.0).astype(BF16)
    group = 16
    for start in range(0, rows, CHUNK):
        left = jnp.concatenate([left_in[start : start + CHUNK, :], ones], axis=1)
        work[start : start + CHUNK, :] = dot_t(left, right[...])
        for at in range(start, start + CHUNK, group):
            tiles = [work[at : at + group, k : k + LANES] for k in range(0, work.shape[1], LANES)]
            peak = functools.reduce(jnp.maximum, tiles)
            peaks[at : at + group, :] = peak
            totals[at : at + group, :] = functools.reduce(jnp.add, [jnp.exp2((tile - peak) * unit) for tile in tiles])
    for part in range(rows // LANES):
        here = slice(part * LANES, (part + 1) * LANES)
        lane_peak = peaks[here, :]
        peak = jnp.max(lane_peak, axis=1, keepdims=True)
        total = jnp.sum(totals[here, :] * jnp.exp2((lane_peak - peak) * unit), axis=1, keepdims=True)
        lse_out[part : part + 1, :] = to_lanes(peak)
        sums[part : part + 1, :] = to_lanes(total)
    lse_out[...] = lse_out[...] + jnp.log(sums[...]) * (1.0 / (unit * math.log(2.0)))


def col_first(group, unit, log_rows, left_in, own, other, *refs):
    parts, (block_out, target_out, pot_out, peak_out, lse_out, left, right, *work) = received(refs, group)
    row_pot = -log_rows - tree_lse(unit, parts)
    pot_out[...] = row_pot
    rows, width = left_in.shape
    half = own.shape[0]
    cols = 2 * half
    odd = lax.axis_index("tgt") & 1
    target_out[pl.ds(pl.multiple_of(odd * half, half), half), :] = own[:, :width]
    target_out[pl.ds(pl.multiple_of((1 - odd) * half, half), half), :] = other[...].astype(BF16)
    right[:, :width] = target_out[...]
    lane = lax.broadcasted_iota(jnp.int32, (cols, LANES), 1)
    right[:, width:] = jnp.where(lane < 3, 1.0, 0.0).astype(BF16)
    left[:, :width] = left_in[...]
    for part in range(rows // LANES):
        left[part * LANES : (part + 1) * LANES, width:] = lane_parts(to_column(row_pot[part : part + 1, :]))
    span = work[0].shape[1]
    spans = [slice(at, at + span) for at in range(0, cols, span)]
    low = jnp.full((8, span), -jnp.inf, F32)

    def product(start, top, k):
        value = dot_t(left[start : start + CHUNK, :], right[spans[k], :])
        work[k % 2][start : start + CHUNK, :] = value
        return jnp.maximum(top, jnp.max(value.reshape(CHUNK // 8, 8, span), axis=0))

    top = low
    for start in range(0, rows, CHUNK):
        top = product(start, top, 0)
    for k in range(len(spans)):
        peak = jnp.max(top, axis=0, keepdims=True)
        total = jnp.zeros((8, span), F32)
        top = low
        for start in range(0, rows, CHUNK):
            if k + 1 < len(spans):
                top = product(start, top, k + 1)
            for at in range(start, start + CHUNK, 16):
                value = jnp.exp2((work[k % 2][at : at + 16, :] - peak) * unit)
                block_out[at : at + 16, spans[k]] = value.astype(BF16)
                total = total + value[:8] + value[8:]
        peak_out[:, spans[k]] = peak
        lse_out[:, spans[k]] = peak + jnp.log(jnp.sum(total, axis=0, keepdims=True)) * (1.0 / (unit * math.log(2.0)))


def column_factors(row):
    pieces = [to_column(row[:, at : at + LANES]) for at in range(0, row.shape[1], LANES)]
    return jnp.concatenate(pieces, axis=0)


def two_rows(row):
    high, low = split(row)
    zeros = jnp.zeros((14, row.shape[1]), F32)
    return jnp.concatenate([high.astype(F32), low.astype(F32), zeros], axis=0).astype(BF16)


def row_sums(block, row, sums_out):
    pair = two_rows(row)
    for start in range(0, block.shape[0], CHUNK):
        both = dot_t(pair, block[start : start + CHUNK, :])
        sums = both[0:1] + both[1:2]
        for part in range(CHUNK // LANES):
            at = start // LANES + part
            sums_out[at : at + 1, :] = sums[:, part * LANES : (part + 1) * LANES]


def row_second(group, unit, log_cols, block, peak, *refs):
    parts, (pot_out, scale_out, sums_out) = received(refs, group)
    lse = tree_lse(unit, parts)
    pot_out[...] = -log_cols - lse
    scale = jnp.exp2(unit * (peak[...] - lse))
    scale_out[...] = scale
    row_sums(block, scale, sums_out)


def col_later(group, ratio, block, scale, *refs):
    parts, (sums_out,) = received(refs, group)
    factors = ratio / tree_sum(parts)
    rows, cols = block.shape
    cut = cols * 3 // 4 // LANES * LANES
    pair = two_rows(jnp.concatenate([factors[k : k + 1, :] for k in range(rows // LANES)], axis=1))
    product = jnp.zeros((16, cut), F32)
    total = jnp.zeros((8, cols - cut), F32)
    for start in range(0, rows, CHUNK):
        product += jnp.dot(pair[:, start : start + CHUNK], block[start : start + CHUNK, :cut], preferred_element_type=F32)
        for part in range(start // LANES, (start + CHUNK) // LANES):
            column = to_column(factors[part : part + 1, :])
            for at in range(0, LANES, 16):
                here = slice(part * LANES + at, part * LANES + at + 16)
                factor = jnp.concatenate([column[at : at + 16]] * ((cols - cut) // LANES), axis=1)
                value = block[here, cut:].astype(F32) * factor
                total = total + value[:8] + value[8:]
    sums_out[:, :cut] = scale[:, :cut] * (product[0:1] + product[1:2])
    sums_out[:, cut:] = scale[:, cut:] * jnp.sum(total, axis=0, keepdims=True)


def row_later(group, block, scale, *refs):
    parts, (sums_out,) = received(refs, group)
    row_sums(block, scale[...] / tree_sum(parts), sums_out)


def row_last(group, unit, block, scale, pot, target, *refs):
    parts, (col_out, sums_out, bary_out, other) = received(refs, group)
    totals = tree_sum(parts)
    pots = (EPS * math.log(2.0)) * (unit * pot[...] - jnp.log(totals) * (1.0 / math.log(2.0)))
    half = col_out.shape[1]
    col_out[...] = jnp.where((lax.axis_index("tgt") & 1) == 0, pots[:, :half], pots[:, half:])
    factors = column_factors(scale[...] / totals)
    high, low = split(factors)
    lane = lax.broadcasted_iota(jnp.int32, factors.shape, 1)
    sides = jnp.where(lane < LANES // 2, high.astype(F32), low.astype(F32)).astype(BF16)
    scaled = (target[...].astype(F32) * factors).astype(BF16)
    weights = jnp.concatenate([scaled, sides], axis=1)
    for start in range(0, block.shape[0], CHUNK):
        wide = jnp.dot(block[start : start + CHUNK, :], weights, preferred_element_type=F32)
        bary_out[start : start + CHUNK, :] = wide[:, :LANES]
        for part in range(CHUNK // LANES):
            at = start // LANES + part
            sides = wide[part * LANES : (part + 1) * LANES, LANES:]
            sums_out[at : at + 1, :] = to_lanes(sides)
            other[at : at + 1, :] = to_lanes(sides, LANES // 2)
    sums_out[...] += pltpu.roll(other[...], LANES // 2, 1)


def cross_local(group, unit, ratio, turned, bary, pot, *refs):
    parts, (row_out, *share_outs, square) = received(refs, group)
    totals = tree_sum(parts)
    row_out[...] = (EPS * math.log(2.0)) * (unit * pot[...] + jnp.log(ratio / totals) * (1.0 / math.log(2.0)))
    inverse = 1.0 / totals
    pieces = []
    for part in range(totals.shape[0]):
        piece = bary[part * LANES : (part + 1) * LANES, :] * to_column(inverse[part : part + 1, :])
        pieces.append(jnp.concatenate(split(piece), axis=1))
    cross = jnp.dot(turned[...], jnp.concatenate(pieces, axis=0), preferred_element_type=F32)
    width = square.shape[0]
    square[...] = cross[:, :width] + cross[:, width:]
    index = lax.axis_index("src")
    count = len(share_outs)
    height = width // count
    for k, out in zip(range(count - 1, -1, -1), share_outs):
        out[...] = square[pl.ds(pl.multiple_of((index ^ k) * height, height), height), :]


def share_sum(*refs):
    refs[-1][...] = tree_sum([ref[...] for ref in refs[:-1]])


def precise(a, b, axis=1):
    ah, al = split(a)
    bh, bl = split(b)
    return lax.dot_general(
        jnp.concatenate([ah, ah, al], axis=axis),
        jnp.concatenate([bh, bl, bh], axis=0),
        (((axis,), (0,)), ((), ())),
        preferred_element_type=F32,
    )


def polar(*refs):
    shares, (out, square) = refs[:-2], refs[-2:]
    index = lax.axis_index("src")
    height = shares[0].shape[0]
    for k, share in enumerate(shares):
        square[pl.ds(pl.multiple_of((index ^ k) * height, height), height), :] = share[...]
    cross = square[...]
    iterate = cross / jnp.sqrt(jnp.sum(cross * cross) + 1e-06)
    gram = precise(iterate, iterate, 0)
    for step in range(NEWTON):
        factor = jnp.where(eye_mask(), 1.5, 0.0) - 0.5 * gram
        if step < NEWTON - 1:
            gram = precise(precise(factor, gram), factor)
        iterate = precise(iterate, factor)
    out[...] = iterate


def partners(values, axis, order):
    size = lax.axis_size(axis)
    return [lax.ppermute(values[k], axis, [(me, me ^ k) for me in range(size)]) if k else values[0] for k in order]


def over_src(x):
    size = lax.axis_size("src")
    return partners([x] * size, "src", range(size))


def over_pairs(x):
    size = lax.axis_size("tgt")
    return partners([x] * size, "tgt", range(0, size, 2))


def over_tgt(x):
    return lax.all_to_all(jnp.broadcast_to(x, (lax.axis_size("tgt"),) + x.shape), "tgt", 0, 0)


def shards(source, target, start_map, warm_potential):
    rows, width = source.shape
    cols = target.shape[0]
    n_src, n_tgt = lax.axis_size("src"), lax.axis_size("tgt")
    ratio = (cols * n_tgt) / (rows * n_src)
    scale = 1.0 / (math.sqrt(width) * EPS)
    unit = scale / math.log(2.0)
    log_rows, log_cols = math.log(rows * n_src) / scale, math.log(cols * n_tgt) / scale
    n_pairs = n_tgt // 2
    row_vec = jax.ShapeDtypeStruct((rows // LANES, LANES), F32)
    pair_vec = jax.ShapeDtypeStruct((1, 2 * cols), F32)
    mac = rows * cols * width

    left, right, turned, plain = call(
        functools.partial(prepare, scale),
        "prepare",
        (
            jax.ShapeDtypeStruct((rows, width), BF16),
            jax.ShapeDtypeStruct((cols, width + LANES), BF16),
            jax.ShapeDtypeStruct((width, rows), BF16),
            jax.ShapeDtypeStruct((cols, width), F32),
        ),
        scratch=[
            pltpu.VMEM((rows, width), BF16),
            pltpu.VMEM((width, width), F32),
            pltpu.VMEM((cols, width), BF16),
            pltpu.VMEM((1, cols), F32),
            pltpu.SemaphoreType.DMA((4,)),
        ],
        flops=2 * rows * width * width,
        space=pltpu.HBM,
    )(*[pltpu.with_memory_space_constraint(x, pltpu.HBM) for x in (source, start_map, target, warm_potential.reshape(1, cols))])
    other = lax.ppermute(plain, "tgt", [(me, me ^ 1) for me in range(n_tgt)])
    lse = call(
        functools.partial(row_first, unit),
        "row_first",
        row_vec,
        scratch=[
            pltpu.VMEM((rows, cols), F32),
            pltpu.VMEM((rows, LANES), F32),
            pltpu.VMEM((rows, LANES), F32),
            pltpu.VMEM(row_vec.shape, F32),
        ],
        flops=4 * mac,
    )(left, right)
    block, targets, row_pot, peak, lse = call(
        functools.partial(col_first, n_tgt, unit, log_rows),
        "col_first",
        (
            jax.ShapeDtypeStruct((rows, 2 * cols), BF16),
            jax.ShapeDtypeStruct((2 * cols, width), BF16),
            row_vec,
            pair_vec,
            pair_vec,
        ),
        scratch=[
            pltpu.VMEM((rows, width + LANES), BF16),
            pltpu.VMEM((2 * cols, width + LANES), BF16),
            pltpu.VMEM((rows, math.gcd(2 * cols, 512)), F32),
            pltpu.VMEM((rows, math.gcd(2 * cols, 512)), F32),
        ],
        flops=8 * mac,
    )(left, right, other, over_tgt(lse))
    col_pot, col_scale, sums = call(
        functools.partial(row_second, n_src, unit, log_cols), "row_second", (pair_vec, pair_vec, row_vec), flops=4 * mac
    )(block, peak, *over_src(lse))
    col_later_call = call(
        functools.partial(col_later, n_pairs, ratio),
        "col_later",
        pair_vec,
        flops=4 * mac,
    )
    sums = col_later_call(block, col_scale, *over_pairs(sums))
    sums = call(functools.partial(row_later, n_src), "row_later", row_vec, flops=4 * mac)(
        block, col_scale, *over_src(sums)
    )
    sums = col_later_call(block, col_scale, *over_pairs(sums))
    col_out, sums, bary = call(
        functools.partial(row_last, n_src, unit),
        "row_last",
        (jax.ShapeDtypeStruct((1, cols), F32), row_vec, jax.ShapeDtypeStruct((rows, width), F32)),
        scratch=[pltpu.VMEM(row_vec.shape, F32)],
        flops=4 * mac,
    )(block, col_scale, col_pot, targets, *over_src(sums))
    square = jax.ShapeDtypeStruct((width, width), F32)
    share_shape = jax.ShapeDtypeStruct((width // n_src, width), F32)
    row_out, *shares = call(
        functools.partial(cross_local, n_pairs, unit, ratio),
        "cross_local",
        (row_vec,) + (share_shape,) * n_src,
        scratch=[pltpu.VMEM((width, width), F32)],
        flops=2 * rows * width * width,
    )(turned, bary, row_pot, *over_pairs(sums))
    share = call(share_sum, "share_sum", share_shape)(*partners(shares[::-1], "src", range(n_src - 1, -1, -1)))
    share = call(share_sum, "share_sum", share_shape)(*over_pairs(share))
    new_map = call(polar, "polar", square, scratch=[pltpu.VMEM((width, width), F32)], flops=1 << 27)(*over_src(share))
    return row_out.reshape(rows), col_out.reshape(cols), new_map


def solution(mesh):
    placed = (P("src", None), P("tgt", None), P(), P("tgt"))
    return jax.shard_map(
        shards, mesh=mesh, in_specs=placed, out_specs=(P("src"), P("tgt"), P()), check_vma=False
    )
```

```python
import functools
import math

import jax
import jax.numpy as jnp
from jax import lax
from jax.experimental import pallas as pl
from jax.experimental.pallas import tpu as pltpu
from jax.sharding import PartitionSpec as P

NEWTON = 10
EPS = 0.05
LANES = 128
CHUNK = 256
VMEM_LIMIT = 40 * 1024 * 1024

F32 = jnp.float32
BF16 = jnp.bfloat16


def call(body, name, out_shape, scratch=(), flops=0, space=pltpu.VMEM):
    return lambda *args: pl.pallas_call(
        body,
        name=name,
        out_shape=out_shape,
        in_specs=[pl.BlockSpec(memory_space=space)] * len(args),
        out_specs=jax.tree.map(lambda _: pl.BlockSpec(memory_space=pltpu.VMEM), out_shape),
        scratch_shapes=scratch,
        compiler_params=pltpu.CompilerParams(vmem_limit_bytes=VMEM_LIMIT),
        cost_estimate=pl.CostEstimate(flops=flops, bytes_accessed=8 << 20, transcendentals=0),
    )(*args)


def eye_mask():
    row, lane = (lax.broadcasted_iota(jnp.int32, (LANES, LANES), k) for k in range(2))
    return row == lane


def to_lanes(column):
    wide = jnp.broadcast_to(column, (LANES, LANES))
    return jnp.sum(jnp.where(eye_mask(), wide, 0.0), axis=0, keepdims=True)


def to_column(row):
    wide = jnp.broadcast_to(row, (LANES, LANES))
    return jnp.broadcast_to(jnp.sum(jnp.where(eye_mask(), wide, 0.0), axis=1, keepdims=True), (LANES, LANES))


def split(x):
    high = x.astype(BF16)
    return high, (x - high.astype(F32)).astype(BF16)


def lane_parts(wide):
    lane = lax.broadcasted_iota(jnp.int32, wide.shape, 1)
    rest = wide
    out = jnp.zeros_like(wide)
    for k in range(3):
        part = rest.astype(BF16).astype(F32)
        out = jnp.where(lane == k, part, out)
        rest = rest - part
    return out.astype(BF16)


def tree(combine, values):
    values = list(values)
    while len(values) > 1:
        values = [combine(a, b) for a, b in zip(values[::2], values[1::2])]
    return values[0]


def tree_sum(parts):
    return tree(jnp.add, parts)


def tree_lse(unit, parts):
    peak = tree(jnp.maximum, parts)
    total = tree(jnp.add, [jnp.exp2(unit * (part - peak)) for part in parts])
    return peak + jnp.log(total) * (1.0 / (unit * math.log(2.0)))


def received(refs, group):
    if len(refs[0].shape) == 3:
        return [refs[0][k] for k in range(group)], refs[1:]
    return [ref[...] for ref in refs[:group]], refs[group:]


def dot_t(a, b):
    return lax.dot_general(a, b, (((1,), (1,)), ((), ())), preferred_element_type=F32)


def prepare(
    scale, source_hbm, map_hbm, target_hbm, pot_hbm, source, left_out, right_out, plain_out,
    start_map, target, pot, sems,
):
    copies = [
        pltpu.make_async_copy(src, dst, sems.at[k])
        for k, (src, dst) in enumerate(
            [(source_hbm, source), (map_hbm, start_map), (target_hbm, target), (pot_hbm, pot)]
        )
    ]
    for copy in copies:
        copy.start()
    for copy in copies:
        copy.wait()
    width = source.shape[1]
    plain_out[...] = target[...].astype(F32)
    for part in range(target.shape[0] // LANES):
        at = pl.ds(part * LANES, LANES)
        right_out[at, :width] = target[at, :]
        right_out[at, width:] = lane_parts(to_column(pot[:, at] * (1.0 / scale)))
    left_out[...] = jnp.dot(source[...], start_map[...].astype(BF16), preferred_element_type=F32).astype(BF16)


def row_first(unit, left_in, right, lse_out, work, peaks, totals, sums):
    rows = left_in.shape[0]
    lane = lax.broadcasted_iota(jnp.int32, (CHUNK, LANES), 1)
    ones = jnp.where(lane < 3, 1.0, 0.0).astype(BF16)
    group = 16
    for start in range(0, rows, CHUNK):
        left = jnp.concatenate([left_in[start : start + CHUNK, :], ones], axis=1)
        work[start : start + CHUNK, :] = dot_t(left, right[...])
        for at in range(start, start + CHUNK, group):
            tiles = [work[at : at + group, k : k + LANES] for k in range(0, work.shape[1], LANES)]
            peak = functools.reduce(jnp.maximum, tiles)
            peaks[at : at + group, :] = peak
            totals[at : at + group, :] = functools.reduce(jnp.add, [jnp.exp2((tile - peak) * unit) for tile in tiles])
    for part in range(rows // LANES):
        here = slice(part * LANES, (part + 1) * LANES)
        lane_peak = peaks[here, :]
        peak = jnp.max(lane_peak, axis=1, keepdims=True)
        total = jnp.sum(totals[here, :] * jnp.exp2((lane_peak - peak) * unit), axis=1, keepdims=True)
        lse_out[part : part + 1, :] = to_lanes(peak)
        sums[part : part + 1, :] = to_lanes(total)
    lse_out[...] = lse_out[...] + jnp.log(sums[...]) * (1.0 / (unit * math.log(2.0)))


def col_first(group, unit, log_rows, left_in, own, other, *refs):
    parts, (block_out, target_out, pot_out, peak_out, lse_out, left, right, *work) = received(refs, group)
    row_pot = -log_rows - tree_lse(unit, parts)
    pot_out[...] = row_pot
    rows, width = left_in.shape
    half = own.shape[0]
    cols = 2 * half
    odd = lax.axis_index("tgt") & 1
    right[pl.ds(pl.multiple_of(odd * half, half), half), :width] = own[:, :width]
    right[pl.ds(pl.multiple_of((1 - odd) * half, half), half), :width] = other[...].astype(BF16)
    for at in range(0, cols, LANES):
        target_out[:, at : at + LANES] = right[at : at + LANES, :width].T
    lane = lax.broadcasted_iota(jnp.int32, (cols, LANES), 1)
    right[:, width:] = jnp.where(lane < 3, 1.0, 0.0).astype(BF16)
    left[:, :width] = left_in[...]
    for part in range(rows // LANES):
        left[part * LANES : (part + 1) * LANES, width:] = lane_parts(to_column(row_pot[part : part + 1, :]))
    span = work[0].shape[1]
    spans = [slice(at, at + span) for at in range(0, cols, span)]
    low = jnp.full((8, span), -jnp.inf, F32)

    def product(start, top, k):
        value = dot_t(left[start : start + CHUNK, :], right[spans[k], :])
        work[k % 2][start : start + CHUNK, :] = value
        return jnp.maximum(top, jnp.max(value.reshape(CHUNK // 8, 8, span), axis=0))

    top = low
    for start in range(0, rows, CHUNK):
        top = product(start, top, 0)
    for k in range(len(spans)):
        peak = jnp.max(top, axis=0, keepdims=True)
        total = jnp.zeros((8, span), F32)
        top = low
        for start in range(0, rows, CHUNK):
            if k + 1 < len(spans):
                top = product(start, top, k + 1)
            for at in range(start, start + CHUNK, 16):
                value = jnp.exp2((work[k % 2][at : at + 16, :] - peak) * unit)
                block_out[at : at + 16, spans[k]] = value.astype(BF16)
                total = total + value[:8] + value[8:]
        peak_out[:, spans[k]] = peak
        lse_out[:, spans[k]] = peak + jnp.log(jnp.sum(total, axis=0, keepdims=True)) * (1.0 / (unit * math.log(2.0)))


def two_rows(row):
    high, low = split(row)
    zeros = jnp.zeros((14, row.shape[1]), F32)
    return jnp.concatenate([high.astype(F32), low.astype(F32), zeros], axis=0).astype(BF16)


def put_rows(out, start, row):
    for part in range(row.shape[1] // LANES):
        at = start // LANES + part
        out[at : at + 1, :] = row[:, part * LANES : (part + 1) * LANES]


def row_sums(block, row, sums_out):
    rows, cols = block.shape
    cut = cols // 2
    first = lax.broadcasted_iota(jnp.int32, (16, 2 * LANES), 0) == 0
    pair = jnp.concatenate([two_rows(row[:, :cut]), jnp.where(first, 1.0, 0.0).astype(BF16)], axis=1)
    tiles = [(at, jnp.broadcast_to(row[:, at : at + LANES], (16, LANES))) for at in range(cut, cols, LANES)]
    for start in range(0, rows, CHUNK):
        folded = []
        for here in range(start, start + CHUNK, 16):
            terms = [block[here : here + 16, at : at + LANES].astype(F32) * factor for at, factor in tiles]
            folded.append(functools.reduce(jnp.add, terms))
        folded = split(jnp.concatenate(folded, axis=0))
        both = dot_t(pair, jnp.concatenate([block[start : start + CHUNK, :cut], *folded], axis=1))
        put_rows(sums_out, start, both[0:1] + both[1:2])


def row_second(group, unit, log_cols, block, peak, *refs):
    parts, (pot_out, scale_out, sums_out) = received(refs, group)
    lse = tree_lse(unit, parts)
    pot_out[...] = -log_cols - lse
    scale = jnp.exp2(unit * (peak[...] - lse))
    scale_out[...] = scale
    row_sums(block, scale, sums_out)


def col_later(group, ratio, block, scale, *refs):
    parts, (sums_out,) = received(refs, group)
    factors = ratio / tree_sum(parts)
    rows, cols = block.shape
    cut = cols * 3 // 4 // LANES * LANES
    pair = two_rows(jnp.concatenate([factors[k : k + 1, :] for k in range(rows // LANES)], axis=1))
    product = jnp.zeros((16, cut), F32)
    total = jnp.zeros((8, cols - cut), F32)
    for start in range(0, rows, CHUNK):
        product += jnp.dot(pair[:, start : start + CHUNK], block[start : start + CHUNK, :cut], preferred_element_type=F32)
        for part in range(start // LANES, (start + CHUNK) // LANES):
            column = to_column(factors[part : part + 1, :])
            for at in range(0, LANES, 16):
                here = slice(part * LANES + at, part * LANES + at + 16)
                factor = jnp.concatenate([column[at : at + 16]] * ((cols - cut) // LANES), axis=1)
                value = block[here, cut:].astype(F32) * factor
                total = total + value[:8] + value[8:]
    sums_out[:, :cut] = scale[:, :cut] * (product[0:1] + product[1:2])
    sums_out[:, cut:] = scale[:, cut:] * jnp.sum(total, axis=0, keepdims=True)


def row_later(group, block, scale, *refs):
    parts, (sums_out,) = received(refs, group)
    row_sums(block, scale[...] / tree_sum(parts), sums_out)


def row_last(group, unit, block, scale, pot, target, *refs):
    parts, (col_out, sums_out, bary_out) = received(refs, group)
    totals = tree_sum(parts)
    pots = (EPS * math.log(2.0)) * (unit * pot[...] - jnp.log(totals) * (1.0 / math.log(2.0)))
    half = col_out.shape[1]
    col_out[...] = jnp.where((lax.axis_index("tgt") & 1) == 0, pots[:, :half], pots[:, half:])
    row = scale[...] / totals
    scaled = (target[...].astype(F32) * row).astype(BF16)
    left = jnp.concatenate([scaled, two_rows(row)], axis=0)
    width = target.shape[0]
    for start in range(0, block.shape[0], CHUNK):
        both = dot_t(left, block[start : start + CHUNK, :])
        bary_out[:, start : start + CHUNK] = both[:width]
        put_rows(sums_out, start, both[width : width + 1] + both[width + 1 : width + 2])


def cross_local(group, unit, ratio, source, bary, pot, *refs):
    parts, (row_out, *share_outs, square) = received(refs, group)
    totals = tree_sum(parts)
    row_out[...] = (EPS * math.log(2.0)) * (unit * pot[...] + jnp.log(ratio / totals) * (1.0 / math.log(2.0)))
    inverse = 1.0 / totals
    inverse = jnp.concatenate([inverse[k : k + 1, :] for k in range(inverse.shape[0])], axis=1)
    both = jnp.concatenate(split(bary[...] * inverse), axis=0)
    cross = jnp.dot(both, source[...], preferred_element_type=F32)
    width = square.shape[0]
    square[...] = (cross[:width, :] + cross[width:, :]).T
    index = lax.axis_index("src")
    count = len(share_outs)
    height = width // count
    for k, out in zip(range(count - 1, -1, -1), share_outs):
        out[...] = square[pl.ds(pl.multiple_of((index ^ k) * height, height), height), :]


def share_sum(*refs):
    refs[-1][...] = tree_sum([ref[...] for ref in refs[:-1]])


def precise(a, b, axis=1):
    ah, al = split(a)
    bh, bl = split(b)
    return lax.dot_general(
        jnp.concatenate([ah, ah, al], axis=axis),
        jnp.concatenate([bh, bl, bh], axis=0),
        (((axis,), (0,)), ((), ())),
        preferred_element_type=F32,
    )


def polar(*refs):
    shares, (out, square) = refs[:-2], refs[-2:]
    index = lax.axis_index("src")
    height = shares[0].shape[0]
    for k, share in enumerate(shares):
        square[pl.ds(pl.multiple_of((index ^ k) * height, height), height), :] = share[...]
    cross = square[...]
    iterate = cross / jnp.sqrt(jnp.sum(cross * cross) + 1e-06)
    gram = precise(iterate, iterate, 0)
    for step in range(NEWTON):
        factor = jnp.where(eye_mask(), 1.5, 0.0) - 0.5 * gram
        if step < NEWTON - 1:
            gram = precise(precise(factor, gram), factor)
        iterate = precise(iterate, factor)
    out[...] = iterate


def partners(values, axis, order):
    size = lax.axis_size(axis)
    return [lax.ppermute(values[k], axis, [(me, me ^ k) for me in range(size)]) if k else values[0] for k in order]


def over_src(x):
    size = lax.axis_size("src")
    return partners([x] * size, "src", range(size))


def over_pairs(x):
    size = lax.axis_size("tgt")
    return partners([x] * size, "tgt", range(0, size, 2))


def over_tgt(x):
    return lax.all_to_all(jnp.broadcast_to(x, (lax.axis_size("tgt"),) + x.shape), "tgt", 0, 0)


def shards(source, target, start_map, warm_potential):
    rows, width = source.shape
    cols = target.shape[0]
    n_src, n_tgt = lax.axis_size("src"), lax.axis_size("tgt")
    ratio = (cols * n_tgt) / (rows * n_src)
    scale = 1.0 / (math.sqrt(width) * EPS)
    unit = scale / math.log(2.0)
    log_rows, log_cols = math.log(rows * n_src) / scale, math.log(cols * n_tgt) / scale
    n_pairs = n_tgt // 2
    row_vec = jax.ShapeDtypeStruct((rows // LANES, LANES), F32)
    pair_vec = jax.ShapeDtypeStruct((1, 2 * cols), F32)
    mac = rows * cols * width

    source, left, right, plain = call(
        functools.partial(prepare, scale),
        "prepare",
        (
            jax.ShapeDtypeStruct((rows, width), BF16),
            jax.ShapeDtypeStruct((rows, width), BF16),
            jax.ShapeDtypeStruct((cols, width + LANES), BF16),
            jax.ShapeDtypeStruct((cols, width), F32),
        ),
        scratch=[
            pltpu.VMEM((width, width), F32),
            pltpu.VMEM((cols, width), BF16),
            pltpu.VMEM((1, cols), F32),
            pltpu.SemaphoreType.DMA((4,)),
        ],
        flops=2 * rows * width * width,
        space=pltpu.HBM,
    )(*[pltpu.with_memory_space_constraint(x, pltpu.HBM) for x in (source, start_map, target, warm_potential.reshape(1, cols))])
    other = lax.ppermute(plain, "tgt", [(me, me ^ 1) for me in range(n_tgt)])
    lse = call(
        functools.partial(row_first, unit),
        "row_first",
        row_vec,
        scratch=[
            pltpu.VMEM((rows, cols), F32),
            pltpu.VMEM((rows, LANES), F32),
            pltpu.VMEM((rows, LANES), F32),
            pltpu.VMEM(row_vec.shape, F32),
        ],
        flops=4 * mac,
    )(left, right)
    block, targets, row_pot, peak, lse = call(
        functools.partial(col_first, n_tgt, unit, log_rows),
        "col_first",
        (
            jax.ShapeDtypeStruct((rows, 2 * cols), BF16),
            jax.ShapeDtypeStruct((width, 2 * cols), BF16),
            row_vec,
            pair_vec,
            pair_vec,
        ),
        scratch=[
            pltpu.VMEM((rows, width + LANES), BF16),
            pltpu.VMEM((2 * cols, width + LANES), BF16),
            pltpu.VMEM((rows, math.gcd(2 * cols, 512)), F32),
            pltpu.VMEM((rows, math.gcd(2 * cols, 512)), F32),
        ],
        flops=8 * mac,
    )(left, right, other, over_tgt(lse))
    col_pot, col_scale, sums = call(
        functools.partial(row_second, n_src, unit, log_cols), "row_second", (pair_vec, pair_vec, row_vec), flops=4 * mac
    )(block, peak, *over_src(lse))
    col_later_call = call(
        functools.partial(col_later, n_pairs, ratio),
        "col_later",
        pair_vec,
        flops=4 * mac,
    )
    sums = col_later_call(block, col_scale, *over_pairs(sums))
    sums = call(functools.partial(row_later, n_src), "row_later", row_vec, flops=4 * mac)(
        block, col_scale, *over_src(sums)
    )
    sums = col_later_call(block, col_scale, *over_pairs(sums))
    col_out, sums, bary = call(
        functools.partial(row_last, n_src, unit),
        "row_last",
        (jax.ShapeDtypeStruct((1, cols), F32), row_vec, jax.ShapeDtypeStruct((width, rows), F32)),
        flops=4 * mac,
    )(block, col_scale, col_pot, targets, *over_src(sums))
    square = jax.ShapeDtypeStruct((width, width), F32)
    share_shape = jax.ShapeDtypeStruct((width // n_src, width), F32)
    row_out, *shares = call(
        functools.partial(cross_local, n_pairs, unit, ratio),
        "cross_local",
        (row_vec,) + (share_shape,) * n_src,
        scratch=[pltpu.VMEM((width, width), F32)],
        flops=2 * rows * width * width,
    )(source, bary, row_pot, *over_pairs(sums))
    share = call(share_sum, "share_sum", share_shape)(*partners(shares[::-1], "src", range(n_src - 1, -1, -1)))
    share = call(share_sum, "share_sum", share_shape)(*over_pairs(share))
    new_map = call(polar, "polar", square, scratch=[pltpu.VMEM((width, width), F32)], flops=1 << 27)(*over_src(share))
    return row_out.reshape(rows), col_out.reshape(cols), new_map


def solution(mesh):
    placed = (P("src", None), P("tgt", None), P(), P("tgt"))
    return jax.shard_map(
        shards, mesh=mesh, in_specs=placed, out_specs=(P("src"), P("tgt"), P()), check_vma=False
    )
```

```python
import functools
import math

import jax
import jax.numpy as jnp
from jax import lax
from jax.experimental import pallas as pl
from jax.experimental.pallas import tpu as pltpu
from jax.sharding import PartitionSpec as P

NEWTON = 10
EPS = 0.05
LANES = 128
CHUNK = 256
VMEM_LIMIT = 40 * 1024 * 1024

F32 = jnp.float32
BF16 = jnp.bfloat16


def call(body, name, out_shape, scratch=(), flops=0, space=pltpu.VMEM):
    return lambda *args: pl.pallas_call(
        body,
        name=name,
        out_shape=out_shape,
        in_specs=[pl.BlockSpec(memory_space=space)] * len(args),
        out_specs=jax.tree.map(lambda _: pl.BlockSpec(memory_space=pltpu.VMEM), out_shape),
        scratch_shapes=scratch,
        compiler_params=pltpu.CompilerParams(vmem_limit_bytes=VMEM_LIMIT),
        cost_estimate=pl.CostEstimate(flops=flops, bytes_accessed=8 << 20, transcendentals=0),
    )(*args)


def eye_mask():
    row, lane = (lax.broadcasted_iota(jnp.int32, (LANES, LANES), k) for k in range(2))
    return row == lane


def to_lanes(column):
    wide = jnp.broadcast_to(column, (LANES, LANES))
    return jnp.sum(jnp.where(eye_mask(), wide, 0.0), axis=0, keepdims=True)


def to_column(row):
    wide = jnp.broadcast_to(row, (LANES, LANES))
    return jnp.broadcast_to(jnp.sum(jnp.where(eye_mask(), wide, 0.0), axis=1, keepdims=True), (LANES, LANES))


def split(x):
    high = x.astype(BF16)
    return high, (x - high.astype(F32)).astype(BF16)


def lane_parts(wide):
    lane = lax.broadcasted_iota(jnp.int32, wide.shape, 1)
    rest = wide
    out = jnp.zeros_like(wide)
    for k in range(3):
        part = rest.astype(BF16).astype(F32)
        out = jnp.where(lane == k, part, out)
        rest = rest - part
    return out.astype(BF16)


def tree(combine, values):
    values = list(values)
    while len(values) > 1:
        values = [combine(a, b) for a, b in zip(values[::2], values[1::2])]
    return values[0]


def tree_sum(parts):
    return tree(jnp.add, parts)


def tree_lse(unit, parts):
    peak = tree(jnp.maximum, parts)
    total = tree(jnp.add, [jnp.exp2(unit * (part - peak)) for part in parts])
    return peak + jnp.log(total) * (1.0 / (unit * math.log(2.0)))


def received(refs, group):
    if len(refs[0].shape) == 3:
        return [refs[0][k] for k in range(group)], refs[1:]
    return [ref[...] for ref in refs[:group]], refs[group:]


def dot_t(a, b):
    return lax.dot_general(a, b, (((1,), (1,)), ((), ())), preferred_element_type=F32)


def prepare(
    scale, source_hbm, map_hbm, target_hbm, pot_hbm, source, left_out, turned_out, right_out, plain_out,
    start_map, target, pot, sems,
):
    copies = [
        pltpu.make_async_copy(src, dst, sems.at[k])
        for k, (src, dst) in enumerate(
            [(source_hbm, source), (map_hbm, start_map), (target_hbm, target), (pot_hbm, pot)]
        )
    ]
    for copy in copies:
        copy.start()
    for copy in copies:
        copy.wait()
    width = source.shape[1]
    plain_out[...] = target[...].astype(F32)
    for part in range(target.shape[0] // LANES):
        at = pl.ds(part * LANES, LANES)
        right_out[at, :width] = target[at, :]
        right_out[at, width:] = lane_parts(to_column(pot[:, at] * (1.0 / scale)))
    left_out[...] = jnp.dot(source[...], start_map[...].astype(BF16), preferred_element_type=F32).astype(BF16)
    for at in range(0, source.shape[0], LANES):
        turned_out[:, at : at + LANES] = left_out[at : at + LANES, :].T


def row_first(unit, left_in, right, lse_out, work, peaks, totals, sums):
    rows = left_in.shape[0]
    lane = lax.broadcasted_iota(jnp.int32, (CHUNK, LANES), 1)
    ones = jnp.where(lane < 3, 1.0, 0.0).astype(BF16)
    group = 16
    for start in range(0, rows, CHUNK):
        left = jnp.concatenate([left_in[start : start + CHUNK, :], ones], axis=1)
        work[start : start + CHUNK, :] = dot_t(left, right[...])
        for at in range(start, start + CHUNK, group):
            tiles = [work[at : at + group, k : k + LANES] for k in range(0, work.shape[1], LANES)]
            peak = functools.reduce(jnp.maximum, tiles)
            peaks[at : at + group, :] = peak
            totals[at : at + group, :] = functools.reduce(jnp.add, [jnp.exp2((tile - peak) * unit) for tile in tiles])
    for part in range(rows // LANES):
        here = slice(part * LANES, (part + 1) * LANES)
        lane_peak = peaks[here, :]
        peak = jnp.max(lane_peak, axis=1, keepdims=True)
        total = jnp.sum(totals[here, :] * jnp.exp2((lane_peak - peak) * unit), axis=1, keepdims=True)
        lse_out[part : part + 1, :] = to_lanes(peak)
        sums[part : part + 1, :] = to_lanes(total)
    lse_out[...] = lse_out[...] + jnp.log(sums[...]) * (1.0 / (unit * math.log(2.0)))


def in_row(parts):
    return jnp.concatenate([parts[k : k + 1, :] for k in range(parts.shape[0])], axis=1)


def col_first(group, unit, log_rows, turned, own, other, *refs):
    parts, (block_out, target_out, pot_out, peak_out, lse_out, left, right, *work) = received(refs, group)
    row_pot = -log_rows - tree_lse(unit, parts)
    pot_out[...] = row_pot
    width, rows = turned.shape
    half = own.shape[0]
    cols = 2 * half
    odd = lax.axis_index("tgt") & 1
    right[pl.ds(pl.multiple_of(odd * half, half), half), :width] = own[:, :width]
    right[pl.ds(pl.multiple_of((1 - odd) * half, half), half), :width] = other[...].astype(BF16)
    for at in range(0, cols, LANES):
        target_out[:, at : at + LANES] = right[at : at + LANES, :width].T
    lane = lax.broadcasted_iota(jnp.int32, (cols, LANES), 1)
    right[:, width:] = jnp.where(lane < 3, 1.0, 0.0).astype(BF16)
    left[:width, :] = turned[...]
    rest = in_row(row_pot)
    pieces = []
    for _ in range(3):
        pieces.append(rest.astype(BF16).astype(F32))
        rest = rest - pieces[-1]
    left[width:, :] = jnp.concatenate([*pieces, jnp.zeros((LANES - 3, rows), F32)], axis=0).astype(BF16)
    for start in range(0, cols, CHUNK):
        scores = work[start // CHUNK % 2]
        scores[...] = jnp.dot(right[start : start + CHUNK, :], left[...], preferred_element_type=F32)
        peaks, sums = [], []
        for at in range(0, CHUNK, 16):
            tiles = [scores[at : at + 16, k : k + LANES] for k in range(0, rows, LANES)]
            peaks.append(functools.reduce(jnp.maximum, tiles))
        peak = jnp.max(jnp.concatenate(peaks, axis=0), axis=1, keepdims=True)
        peak = jnp.broadcast_to(peak, (CHUNK, LANES))
        for at in range(0, CHUNK, 16):
            top = peak[at : at + 16]
            total = None
            for k in range(0, rows, LANES):
                value = jnp.exp2((scores[at : at + 16, k : k + LANES] - top) * unit)
                block_out[start + at : start + at + 16, k : k + LANES] = value.astype(BF16)
                total = value if total is None else total + value
            sums.append(total)
        total = jnp.sum(jnp.concatenate(sums, axis=0), axis=1, keepdims=True)
        for part in range(0, CHUNK, LANES):
            here = slice(start + part, start + part + LANES)
            peak_out[:, here] = to_lanes(peak[part : part + LANES])
            lse_out[:, here] = to_lanes(total[part : part + LANES])
    lse_out[...] = peak_out[...] + jnp.log(lse_out[...]) * (1.0 / (unit * math.log(2.0)))


def two_rows(row):
    high, low = split(row)
    zeros = jnp.zeros((14, row.shape[1]), F32)
    return jnp.concatenate([high.astype(F32), low.astype(F32), zeros], axis=0).astype(BF16)


def put_rows(out, start, row):
    for part in range(row.shape[1] // LANES):
        at = start // LANES + part
        out[at : at + 1, :] = row[:, part * LANES : (part + 1) * LANES]


def sums_down(block, row, out):
    rows, cols = block.shape
    cut = cols * 3 // 4 // LANES * LANES
    pair = two_rows(row)
    product = jnp.zeros((16, cut), F32)
    total = jnp.zeros((8, cols - cut), F32)
    for start in range(0, rows, CHUNK):
        product += jnp.dot(pair[:, start : start + CHUNK], block[start : start + CHUNK, :cut], preferred_element_type=F32)
        for part in range(start, start + CHUNK, LANES):
            column = to_column(row[:, part : part + LANES])
            for at in range(0, LANES, 16):
                factor = jnp.concatenate([column[at : at + 16]] * ((cols - cut) // LANES), axis=1)
                value = block[part + at : part + at + 16, cut:].astype(F32) * factor
                total = total + value[:8] + value[8:]
    put_rows(out, 0, jnp.concatenate([product[0:1] + product[1:2], jnp.sum(total, axis=0, keepdims=True)], axis=1))


def sums_across(block, row, out):
    rows, cols = block.shape
    cut = cols // 2
    first = lax.broadcasted_iota(jnp.int32, (16, 2 * LANES), 0) == 0
    pair = jnp.concatenate([two_rows(row[:, :cut]), jnp.where(first, 1.0, 0.0).astype(BF16)], axis=1)
    tiles = [(at, jnp.broadcast_to(row[:, at : at + LANES], (16, LANES))) for at in range(cut, cols, LANES)]
    for start in range(0, rows, CHUNK):
        folded = []
        for here in range(start, start + CHUNK, 16):
            terms = [block[here : here + 16, at : at + LANES].astype(F32) * factor for at, factor in tiles]
            folded.append(functools.reduce(jnp.add, terms))
        folded = split(jnp.concatenate(folded, axis=0))
        both = dot_t(pair, jnp.concatenate([block[start : start + CHUNK, :cut], *folded], axis=1))
        out[:, start : start + CHUNK] = both[0:1] + both[1:2]


def row_second(group, unit, log_cols, block, peak, *refs):
    parts, (pot_out, scale_out, sums_out) = received(refs, group)
    lse = tree_lse(unit, parts)
    pot_out[...] = -log_cols - lse
    scale = jnp.exp2(unit * (peak[...] - lse))
    scale_out[...] = scale
    sums_down(block, scale, sums_out)


def col_later(group, ratio, block, scale, *refs):
    parts, (sums_out,) = received(refs, group)
    sums_across(block, in_row(ratio / tree_sum(parts)), sums_out)
    sums_out[...] *= scale[...]


def row_later(group, block, scale, *refs):
    parts, (sums_out,) = received(refs, group)
    sums_down(block, scale[...] / tree_sum(parts), sums_out)


def row_last(group, unit, block, scale, pot, target, *refs):
    parts, (col_out, sums_out, bary_out) = received(refs, group)
    totals = tree_sum(parts)
    pots = (EPS * math.log(2.0)) * (unit * pot[...] - jnp.log(totals) * (1.0 / math.log(2.0)))
    half = col_out.shape[1]
    col_out[...] = jnp.where((lax.axis_index("tgt") & 1) == 0, pots[:, :half], pots[:, half:])
    row = scale[...] / totals
    scaled = (target[...].astype(F32) * row).astype(BF16)
    left = jnp.concatenate([scaled, two_rows(row)], axis=0)
    width = target.shape[0]
    for start in range(0, block.shape[1], CHUNK):
        both = jnp.dot(left, block[:, start : start + CHUNK], preferred_element_type=F32)
        bary_out[:, start : start + CHUNK] = both[:width]
        put_rows(sums_out, start, both[width : width + 1] + both[width + 1 : width + 2])


def cross_local(group, unit, ratio, source, bary, pot, *refs):
    parts, (row_out, *share_outs, square) = received(refs, group)
    totals = tree_sum(parts)
    row_out[...] = (EPS * math.log(2.0)) * (unit * pot[...] + jnp.log(ratio / totals) * (1.0 / math.log(2.0)))
    inverse = in_row(1.0 / totals)
    both = jnp.concatenate(split(bary[...] * inverse), axis=0)
    cross = jnp.dot(both, source[...], preferred_element_type=F32)
    width = square.shape[0]
    square[...] = (cross[:width, :] + cross[width:, :]).T
    index = lax.axis_index("src")
    count = len(share_outs)
    height = width // count
    for k, out in zip(range(count - 1, -1, -1), share_outs):
        out[...] = square[pl.ds(pl.multiple_of((index ^ k) * height, height), height), :]


def share_sum(*refs):
    refs[-1][...] = tree_sum([ref[...] for ref in refs[:-1]])


def precise(a, b, axis=1):
    ah, al = split(a)
    bh, bl = split(b)
    return lax.dot_general(
        jnp.concatenate([ah, ah, al], axis=axis),
        jnp.concatenate([bh, bl, bh], axis=0),
        (((axis,), (0,)), ((), ())),
        preferred_element_type=F32,
    )


def polar(*refs):
    shares, (out, square) = refs[:-2], refs[-2:]
    index = lax.axis_index("src")
    height = shares[0].shape[0]
    for k, share in enumerate(shares):
        square[pl.ds(pl.multiple_of((index ^ k) * height, height), height), :] = share[...]
    cross = square[...]
    iterate = cross / jnp.sqrt(jnp.sum(cross * cross) + 1e-06)
    gram = precise(iterate, iterate, 0)
    for step in range(NEWTON):
        factor = jnp.where(eye_mask(), 1.5, 0.0) - 0.5 * gram
        if step < NEWTON - 1:
            gram = precise(precise(factor, gram), factor)
        iterate = precise(iterate, factor)
    out[...] = iterate


def partners(values, axis, order):
    size = lax.axis_size(axis)
    return [lax.ppermute(values[k], axis, [(me, me ^ k) for me in range(size)]) if k else values[0] for k in order]


def over_src(x):
    size = lax.axis_size("src")
    return partners([x] * size, "src", range(size))


def over_pairs(x):
    size = lax.axis_size("tgt")
    return partners([x] * size, "tgt", range(0, size, 2))


def over_tgt(x):
    return lax.all_to_all(jnp.broadcast_to(x, (lax.axis_size("tgt"),) + x.shape), "tgt", 0, 0)


def shards(source, target, start_map, warm_potential):
    rows, width = source.shape
    cols = target.shape[0]
    n_src, n_tgt = lax.axis_size("src"), lax.axis_size("tgt")
    ratio = (cols * n_tgt) / (rows * n_src)
    scale = 1.0 / (math.sqrt(width) * EPS)
    unit = scale / math.log(2.0)
    log_rows, log_cols = math.log(rows * n_src) / scale, math.log(cols * n_tgt) / scale
    n_pairs = n_tgt // 2
    row_vec = jax.ShapeDtypeStruct((rows // LANES, LANES), F32)
    pair_vec = jax.ShapeDtypeStruct((1, 2 * cols), F32)
    mac = rows * cols * width

    source, left, turned, right, plain = call(
        functools.partial(prepare, scale),
        "prepare",
        (
            jax.ShapeDtypeStruct((rows, width), BF16),
            jax.ShapeDtypeStruct((rows, width), BF16),
            jax.ShapeDtypeStruct((width, rows), BF16),
            jax.ShapeDtypeStruct((cols, width + LANES), BF16),
            jax.ShapeDtypeStruct((cols, width), F32),
        ),
        scratch=[
            pltpu.VMEM((width, width), F32),
            pltpu.VMEM((cols, width), BF16),
            pltpu.VMEM((1, cols), F32),
            pltpu.SemaphoreType.DMA((4,)),
        ],
        flops=2 * rows * width * width,
        space=pltpu.HBM,
    )(*[pltpu.with_memory_space_constraint(x, pltpu.HBM) for x in (source, start_map, target, warm_potential.reshape(1, cols))])
    other = lax.ppermute(plain, "tgt", [(me, me ^ 1) for me in range(n_tgt)])
    lse = call(
        functools.partial(row_first, unit),
        "row_first",
        row_vec,
        scratch=[
            pltpu.VMEM((rows, cols), F32),
            pltpu.VMEM((rows, LANES), F32),
            pltpu.VMEM((rows, LANES), F32),
            pltpu.VMEM(row_vec.shape, F32),
        ],
        flops=4 * mac,
    )(left, right)
    block, targets, row_pot, peak, lse = call(
        functools.partial(col_first, n_tgt, unit, log_rows),
        "col_first",
        (
            jax.ShapeDtypeStruct((2 * cols, rows), BF16),
            jax.ShapeDtypeStruct((width, 2 * cols), BF16),
            row_vec,
            pair_vec,
            pair_vec,
        ),
        scratch=[
            pltpu.VMEM((width + LANES, rows), BF16),
            pltpu.VMEM((2 * cols, width + LANES), BF16),
            pltpu.VMEM((CHUNK, rows), F32),
            pltpu.VMEM((CHUNK, rows), F32),
        ],
        flops=8 * mac,
    )(turned, right, other, over_tgt(lse))
    col_pot, col_scale, sums = call(
        functools.partial(row_second, n_src, unit, log_cols), "row_second", (pair_vec, pair_vec, row_vec), flops=4 * mac
    )(block, peak, *over_src(lse))
    col_later_call = call(
        functools.partial(col_later, n_pairs, ratio),
        "col_later",
        pair_vec,
        flops=4 * mac,
    )
    sums = col_later_call(block, col_scale, *over_pairs(sums))
    sums = call(functools.partial(row_later, n_src), "row_later", row_vec, flops=4 * mac)(
        block, col_scale, *over_src(sums)
    )
    sums = col_later_call(block, col_scale, *over_pairs(sums))
    col_out, sums, bary = call(
        functools.partial(row_last, n_src, unit),
        "row_last",
        (jax.ShapeDtypeStruct((1, cols), F32), row_vec, jax.ShapeDtypeStruct((width, rows), F32)),
        flops=4 * mac,
    )(block, col_scale, col_pot, targets, *over_src(sums))
    square = jax.ShapeDtypeStruct((width, width), F32)
    share_shape = jax.ShapeDtypeStruct((width // n_src, width), F32)
    row_out, *shares = call(
        functools.partial(cross_local, n_pairs, unit, ratio),
        "cross_local",
        (row_vec,) + (share_shape,) * n_src,
        scratch=[pltpu.VMEM((width, width), F32)],
        flops=2 * rows * width * width,
    )(source, bary, row_pot, *over_pairs(sums))
    share = call(share_sum, "share_sum", share_shape)(*partners(shares[::-1], "src", range(n_src - 1, -1, -1)))
    share = call(share_sum, "share_sum", share_shape)(*over_pairs(share))
    new_map = call(polar, "polar", square, scratch=[pltpu.VMEM((width, width), F32)], flops=1 << 27)(*over_src(share))
    return row_out.reshape(rows), col_out.reshape(cols), new_map


def solution(mesh):
    placed = (P("src", None), P("tgt", None), P(), P("tgt"))
    return jax.shard_map(
        shards, mesh=mesh, in_specs=placed, out_specs=(P("src"), P("tgt"), P()), check_vma=False
    )
```

```python
import functools
import math

import jax
import jax.numpy as jnp
from jax import lax
from jax.experimental import pallas as pl
from jax.experimental.pallas import tpu as pltpu
from jax.sharding import PartitionSpec as P

NEWTON = 10
EPS = 0.05
LANES = 128
CHUNK = 256
VMEM_LIMIT = 40 * 1024 * 1024

F32 = jnp.float32
BF16 = jnp.bfloat16


def call(body, name, out_shape, scratch=(), flops=0, space=pltpu.VMEM):
    return lambda *args: pl.pallas_call(
        body,
        name=name,
        out_shape=out_shape,
        in_specs=[pl.BlockSpec(memory_space=space)] * len(args),
        out_specs=jax.tree.map(lambda _: pl.BlockSpec(memory_space=pltpu.VMEM), out_shape),
        scratch_shapes=scratch,
        compiler_params=pltpu.CompilerParams(vmem_limit_bytes=VMEM_LIMIT),
        cost_estimate=pl.CostEstimate(flops=flops, bytes_accessed=8 << 20, transcendentals=0),
    )(*args)


def eye_mask():
    row, lane = (lax.broadcasted_iota(jnp.int32, (LANES, LANES), k) for k in range(2))
    return row == lane


def to_lanes(column):
    wide = jnp.broadcast_to(column, (LANES, LANES))
    return jnp.sum(jnp.where(eye_mask(), wide, 0.0), axis=0, keepdims=True)


def to_column(row):
    wide = jnp.broadcast_to(row, (LANES, LANES))
    return jnp.broadcast_to(jnp.sum(jnp.where(eye_mask(), wide, 0.0), axis=1, keepdims=True), (LANES, LANES))


def split(x):
    high = x.astype(BF16)
    return high, (x - high.astype(F32)).astype(BF16)


def lane_parts(wide):
    lane = lax.broadcasted_iota(jnp.int32, wide.shape, 1)
    rest = wide
    out = jnp.zeros_like(wide)
    for k in range(3):
        part = rest.astype(BF16).astype(F32)
        out = jnp.where(lane == k, part, out)
        rest = rest - part
    return out.astype(BF16)


def tree(combine, values):
    values = list(values)
    while len(values) > 1:
        values = [combine(a, b) for a, b in zip(values[::2], values[1::2])]
    return values[0]


def tree_sum(parts):
    return tree(jnp.add, parts)


def tree_lse(unit, parts):
    peak = tree(jnp.maximum, parts)
    total = tree(jnp.add, [jnp.exp2(unit * (part - peak)) for part in parts])
    return peak + jnp.log(total) * (1.0 / (unit * math.log(2.0)))


def received(refs, group):
    if len(refs[0].shape) == 3:
        return [refs[0][k] for k in range(group)], refs[1:]
    return [ref[...] for ref in refs[:group]], refs[group:]


def dot_t(a, b):
    return lax.dot_general(a, b, (((1,), (1,)), ((), ())), preferred_element_type=F32)


def prepare(
    scale, source_hbm, map_hbm, target_hbm, pot_hbm, source, left_out, turned_out, right_out, plain_out,
    start_map, target, pot, sems,
):
    copies = [
        pltpu.make_async_copy(src, dst, sems.at[k])
        for k, (src, dst) in enumerate(
            [(source_hbm, source), (map_hbm, start_map), (target_hbm, target), (pot_hbm, pot)]
        )
    ]
    for copy in copies:
        copy.start()
    for copy in copies:
        copy.wait()
    width = source.shape[1]
    plain_out[...] = target[...].astype(F32)
    for part in range(target.shape[0] // LANES):
        at = pl.ds(part * LANES, LANES)
        right_out[at, :width] = target[at, :]
        right_out[at, width:] = lane_parts(to_column(pot[:, at] * (1.0 / scale)))
    left_out[...] = jnp.dot(source[...], start_map[...].astype(BF16), preferred_element_type=F32).astype(BF16)
    for at in range(0, source.shape[0], LANES):
        turned_out[:, at : at + LANES] = left_out[at : at + LANES, :].T


def row_first(unit, left_in, right, lse_out, work, peaks, totals, sums):
    rows = left_in.shape[0]
    lane = lax.broadcasted_iota(jnp.int32, (CHUNK, LANES), 1)
    ones = jnp.where(lane < 3, 1.0, 0.0).astype(BF16)
    group = 16
    for start in range(0, rows, CHUNK):
        left = jnp.concatenate([left_in[start : start + CHUNK, :], ones], axis=1)
        work[start : start + CHUNK, :] = dot_t(left, right[...])
        for at in range(start, start + CHUNK, group):
            tiles = [work[at : at + group, k : k + LANES] for k in range(0, work.shape[1], LANES)]
            peak = functools.reduce(jnp.maximum, tiles)
            peaks[at : at + group, :] = peak
            values = [jnp.exp2(((tile - peak) * unit).astype(BF16)).astype(F32) for tile in tiles]
            totals[at : at + group, :] = functools.reduce(jnp.add, values)
    for part in range(rows // LANES):
        here = slice(part * LANES, (part + 1) * LANES)
        lane_peak = peaks[here, :]
        peak = jnp.max(lane_peak, axis=1, keepdims=True)
        total = jnp.sum(totals[here, :] * jnp.exp2((lane_peak - peak) * unit), axis=1, keepdims=True)
        lse_out[part : part + 1, :] = to_lanes(peak)
        sums[part : part + 1, :] = to_lanes(total)
    lse_out[...] = lse_out[...] + jnp.log(sums[...]) * (1.0 / (unit * math.log(2.0)))


def in_row(parts):
    return jnp.concatenate([parts[k : k + 1, :] for k in range(parts.shape[0])], axis=1)


def col_first(group, unit, log_rows, turned, own, other, *refs):
    parts, (block_out, target_out, pot_out, peak_out, lse_out, left, right, *work) = received(refs, group)
    row_pot = -log_rows - tree_lse(unit, parts)
    pot_out[...] = row_pot
    width, rows = turned.shape
    half = own.shape[0]
    cols = 2 * half
    odd = lax.axis_index("tgt") & 1
    right[pl.ds(pl.multiple_of(odd * half, half), half), :width] = own[:, :width]
    right[pl.ds(pl.multiple_of((1 - odd) * half, half), half), :width] = other[...].astype(BF16)
    for at in range(0, cols, LANES):
        target_out[:, at : at + LANES] = right[at : at + LANES, :width].T
    lane = lax.broadcasted_iota(jnp.int32, (cols, LANES), 1)
    right[:, width:] = jnp.where(lane < 3, 1.0, 0.0).astype(BF16)
    left[:width, :] = turned[...]
    rest = in_row(row_pot)
    pieces = []
    for _ in range(3):
        pieces.append(rest.astype(BF16).astype(F32))
        rest = rest - pieces[-1]
    left[width:, :] = jnp.concatenate([*pieces, jnp.zeros((LANES - 3, rows), F32)], axis=0).astype(BF16)
    for start in range(0, cols, CHUNK):
        scores = work[start // CHUNK % 2]
        scores[...] = jnp.dot(right[start : start + CHUNK, :], left[...], preferred_element_type=F32)
        peaks, sums = [], []
        for at in range(0, CHUNK, 16):
            tiles = [scores[at : at + 16, k : k + LANES] for k in range(0, rows, LANES)]
            peaks.append(functools.reduce(jnp.maximum, tiles))
        peak = jnp.max(jnp.concatenate(peaks, axis=0), axis=1, keepdims=True)
        peak = jnp.broadcast_to(peak, (CHUNK, LANES))
        for at in range(0, CHUNK, 16):
            top = peak[at : at + 16]
            total = None
            for k in range(0, rows, LANES):
                value = jnp.exp2((scores[at : at + 16, k : k + LANES] - top) * unit)
                block_out[start + at : start + at + 16, k : k + LANES] = value.astype(BF16)
                total = value if total is None else total + value
            sums.append(total)
        total = jnp.sum(jnp.concatenate(sums, axis=0), axis=1, keepdims=True)
        for part in range(0, CHUNK, LANES):
            here = slice(start + part, start + part + LANES)
            peak_out[:, here] = to_lanes(peak[part : part + LANES])
            lse_out[:, here] = to_lanes(total[part : part + LANES])
    lse_out[...] = peak_out[...] + jnp.log(lse_out[...]) * (1.0 / (unit * math.log(2.0)))


def two_rows(row):
    high, low = split(row)
    zeros = jnp.zeros((14, row.shape[1]), F32)
    return jnp.concatenate([high.astype(F32), low.astype(F32), zeros], axis=0).astype(BF16)


def put_rows(out, start, row):
    for part in range(row.shape[1] // LANES):
        at = start // LANES + part
        out[at : at + 1, :] = row[:, part * LANES : (part + 1) * LANES]


def sums_down(block, row, out):
    rows, cols = block.shape
    cut = cols * 3 // 4 // LANES * LANES
    pair = two_rows(row)
    product = jnp.zeros((16, cut), F32)
    total = jnp.zeros((8, cols - cut), F32)
    for start in range(0, rows, CHUNK):
        product += jnp.dot(pair[:, start : start + CHUNK], block[start : start + CHUNK, :cut], preferred_element_type=F32)
        for part in range(start, start + CHUNK, LANES):
            column = to_column(row[:, part : part + LANES])
            for at in range(0, LANES, 16):
                factor = jnp.concatenate([column[at : at + 16]] * ((cols - cut) // LANES), axis=1)
                value = block[part + at : part + at + 16, cut:].astype(F32) * factor
                total = total + value[:8] + value[8:]
    put_rows(out, 0, jnp.concatenate([product[0:1] + product[1:2], jnp.sum(total, axis=0, keepdims=True)], axis=1))


def sums_across(block, row, out):
    rows, cols = block.shape
    cut = cols // 4 // LANES * LANES
    first = lax.broadcasted_iota(jnp.int32, (16, 2 * LANES), 0) == 0
    pair = jnp.concatenate([two_rows(row[:, :cut]), jnp.where(first, 1.0, 0.0).astype(BF16)], axis=1)
    tiles = [(at, jnp.broadcast_to(row[:, at : at + LANES], (16, LANES))) for at in range(cut, cols, LANES)]
    for start in range(0, rows, CHUNK):
        folded = []
        for here in range(start, start + CHUNK, 16):
            terms = [block[here : here + 16, at : at + LANES].astype(F32) * factor for at, factor in tiles]
            folded.append(functools.reduce(jnp.add, terms))
        folded = split(jnp.concatenate(folded, axis=0))
        both = dot_t(pair, jnp.concatenate([block[start : start + CHUNK, :cut], *folded], axis=1))
        out[:, start : start + CHUNK] = both[0:1] + both[1:2]


def row_second(group, unit, log_cols, block, peak, *refs):
    parts, (pot_out, scale_out, sums_out) = received(refs, group)
    lse = tree_lse(unit, parts)
    pot_out[...] = -log_cols - lse
    scale = jnp.exp2(unit * (peak[...] - lse))
    scale_out[...] = scale
    sums_down(block, scale, sums_out)


def col_later(group, ratio, block, scale, *refs):
    parts, (sums_out,) = received(refs, group)
    sums_across(block, in_row(ratio / tree_sum(parts)), sums_out)
    sums_out[...] *= scale[...]


def row_later(group, block, scale, *refs):
    parts, (sums_out,) = received(refs, group)
    sums_down(block, scale[...] / tree_sum(parts), sums_out)


def row_last(group, unit, block, scale, pot, target, *refs):
    parts, (col_out, sums_out, bary_out) = received(refs, group)
    totals = tree_sum(parts)
    pots = (EPS * math.log(2.0)) * (unit * pot[...] - jnp.log(totals) * (1.0 / math.log(2.0)))
    half = col_out.shape[1]
    col_out[...] = jnp.where((lax.axis_index("tgt") & 1) == 0, pots[:, :half], pots[:, half:])
    row = scale[...] / totals
    scaled = (target[...].astype(F32) * row).astype(BF16)
    left = jnp.concatenate([scaled, two_rows(row)], axis=0)
    width = target.shape[0]
    for start in range(0, block.shape[1], CHUNK):
        both = jnp.dot(left, block[:, start : start + CHUNK], preferred_element_type=F32)
        bary_out[:, start : start + CHUNK] = both[:width]
        put_rows(sums_out, start, both[width : width + 1] + both[width + 1 : width + 2])


def cross_local(group, unit, ratio, source, bary, pot, *refs):
    parts, (row_out, *share_outs, square) = received(refs, group)
    totals = tree_sum(parts)
    row_out[...] = (EPS * math.log(2.0)) * (unit * pot[...] + jnp.log(ratio / totals) * (1.0 / math.log(2.0)))
    inverse = in_row(1.0 / totals)
    both = jnp.concatenate(split(bary[...] * inverse), axis=0)
    cross = jnp.dot(both, source[...], preferred_element_type=F32)
    width = square.shape[0]
    square[...] = (cross[:width, :] + cross[width:, :]).T
    index = lax.axis_index("src")
    count = len(share_outs)
    height = width // count
    for k, out in zip(range(count - 1, -1, -1), share_outs):
        out[...] = square[pl.ds(pl.multiple_of((index ^ k) * height, height), height), :]


def share_sum(*refs):
    refs[-1][...] = tree_sum([ref[...] for ref in refs[:-1]])


def precise(a, b, axis=1):
    ah, al = split(a)
    bh, bl = split(b)
    return lax.dot_general(
        jnp.concatenate([ah, ah, al], axis=axis),
        jnp.concatenate([bh, bl, bh], axis=0),
        (((axis,), (0,)), ((), ())),
        preferred_element_type=F32,
    )


def polar(*refs):
    shares, (out, square) = refs[:-2], refs[-2:]
    index = lax.axis_index("src")
    height = shares[0].shape[0]
    for k, share in enumerate(shares):
        square[pl.ds(pl.multiple_of((index ^ k) * height, height), height), :] = share[...]
    cross = square[...]
    iterate = cross / jnp.sqrt(jnp.sum(cross * cross) + 1e-06)
    unity = jnp.where(eye_mask(), 1.0, 0.0)
    error = unity - precise(iterate, iterate, 0)
    size = error.shape[0]
    for step in range(NEWTON - 1):
        both = precise(jnp.concatenate([error, iterate], axis=0), error)
        iterate = iterate + 0.5 * both[size:]
        error = precise(both[:size], 0.75 * unity + 0.25 * error)
    out[...] = iterate + 0.5 * precise(iterate, error)


def partners(values, axis, order):
    size = lax.axis_size(axis)
    return [lax.ppermute(values[k], axis, [(me, me ^ k) for me in range(size)]) if k else values[0] for k in order]


def over_src(x):
    size = lax.axis_size("src")
    return partners([x] * size, "src", range(size))


def over_pairs(x):
    size = lax.axis_size("tgt")
    return partners([x] * size, "tgt", range(0, size, 2))


def over_tgt(x):
    return lax.all_to_all(jnp.broadcast_to(x, (lax.axis_size("tgt"),) + x.shape), "tgt", 0, 0)


def shards(source, target, start_map, warm_potential):
    rows, width = source.shape
    cols = target.shape[0]
    n_src, n_tgt = lax.axis_size("src"), lax.axis_size("tgt")
    ratio = (cols * n_tgt) / (rows * n_src)
    scale = 1.0 / (math.sqrt(width) * EPS)
    unit = scale / math.log(2.0)
    log_rows, log_cols = math.log(rows * n_src) / scale, math.log(cols * n_tgt) / scale
    n_pairs = n_tgt // 2
    row_vec = jax.ShapeDtypeStruct((rows // LANES, LANES), F32)
    pair_vec = jax.ShapeDtypeStruct((1, 2 * cols), F32)
    mac = rows * cols * width

    source, left, turned, right, plain = call(
        functools.partial(prepare, scale),
        "prepare",
        (
            jax.ShapeDtypeStruct((rows, width), BF16),
            jax.ShapeDtypeStruct((rows, width), BF16),
            jax.ShapeDtypeStruct((width, rows), BF16),
            jax.ShapeDtypeStruct((cols, width + LANES), BF16),
            jax.ShapeDtypeStruct((cols, width), F32),
        ),
        scratch=[
            pltpu.VMEM((width, width), F32),
            pltpu.VMEM((cols, width), BF16),
            pltpu.VMEM((1, cols), F32),
            pltpu.SemaphoreType.DMA((4,)),
        ],
        flops=2 * rows * width * width,
        space=pltpu.HBM,
    )(*[pltpu.with_memory_space_constraint(x, pltpu.HBM) for x in (source, start_map, target, warm_potential.reshape(1, cols))])
    other = lax.ppermute(plain, "tgt", [(me, me ^ 1) for me in range(n_tgt)])
    lse = call(
        functools.partial(row_first, unit),
        "row_first",
        row_vec,
        scratch=[
            pltpu.VMEM((rows, cols), F32),
            pltpu.VMEM((rows, LANES), F32),
            pltpu.VMEM((rows, LANES), F32),
            pltpu.VMEM(row_vec.shape, F32),
        ],
        flops=4 * mac,
    )(left, right)
    block, targets, row_pot, peak, lse = call(
        functools.partial(col_first, n_tgt, unit, log_rows),
        "col_first",
        (
            jax.ShapeDtypeStruct((2 * cols, rows), BF16),
            jax.ShapeDtypeStruct((width, 2 * cols), BF16),
            row_vec,
            pair_vec,
            pair_vec,
        ),
        scratch=[
            pltpu.VMEM((width + LANES, rows), BF16),
            pltpu.VMEM((2 * cols, width + LANES), BF16),
            pltpu.VMEM((CHUNK, rows), F32),
            pltpu.VMEM((CHUNK, rows), F32),
        ],
        flops=8 * mac,
    )(turned, right, other, over_tgt(lse))
    col_pot, col_scale, sums = call(
        functools.partial(row_second, n_src, unit, log_cols), "row_second", (pair_vec, pair_vec, row_vec), flops=4 * mac
    )(block, peak, *over_src(lse))
    col_later_call = call(
        functools.partial(col_later, n_pairs, ratio),
        "col_later",
        pair_vec,
        flops=4 * mac,
    )
    sums = col_later_call(block, col_scale, *over_pairs(sums))
    sums = call(functools.partial(row_later, n_src), "row_later", row_vec, flops=4 * mac)(
        block, col_scale, *over_src(sums)
    )
    sums = col_later_call(block, col_scale, *over_pairs(sums))
    col_out, sums, bary = call(
        functools.partial(row_last, n_src, unit),
        "row_last",
        (jax.ShapeDtypeStruct((1, cols), F32), row_vec, jax.ShapeDtypeStruct((width, rows), F32)),
        flops=4 * mac,
    )(block, col_scale, col_pot, targets, *over_src(sums))
    square = jax.ShapeDtypeStruct((width, width), F32)
    share_shape = jax.ShapeDtypeStruct((width // n_src, width), F32)
    row_out, *shares = call(
        functools.partial(cross_local, n_pairs, unit, ratio),
        "cross_local",
        (row_vec,) + (share_shape,) * n_src,
        scratch=[pltpu.VMEM((width, width), F32)],
        flops=2 * rows * width * width,
    )(source, bary, row_pot, *over_pairs(sums))
    share = call(share_sum, "share_sum", share_shape)(*partners(shares[::-1], "src", range(n_src - 1, -1, -1)))
    share = call(share_sum, "share_sum", share_shape)(*over_pairs(share))
    new_map = call(polar, "polar", square, scratch=[pltpu.VMEM((width, width), F32)], flops=1 << 27)(*over_src(share))
    return row_out.reshape(rows), col_out.reshape(cols), new_map


def solution(mesh):
    placed = (P("src", None), P("tgt", None), P(), P("tgt"))
    return jax.shard_map(
        shards, mesh=mesh, in_specs=placed, out_specs=(P("src"), P("tgt"), P()), check_vma=False
    )
```

```python
import functools
import math

import jax
import jax.numpy as jnp
from jax import lax
from jax.experimental import pallas as pl
from jax.experimental.pallas import tpu as pltpu
from jax.sharding import PartitionSpec as P

NEWTON = 10
EPS = 0.05
LANES = 128
CHUNK = 256
VMEM_LIMIT = 40 * 1024 * 1024

F32 = jnp.float32
BF16 = jnp.bfloat16


def call(body, name, out_shape, scratch=(), flops=0, space=pltpu.VMEM):
    return lambda *args: pl.pallas_call(
        body,
        name=name,
        out_shape=out_shape,
        in_specs=[pl.BlockSpec(memory_space=space)] * len(args),
        out_specs=jax.tree.map(lambda _: pl.BlockSpec(memory_space=pltpu.VMEM), out_shape),
        scratch_shapes=scratch,
        compiler_params=pltpu.CompilerParams(vmem_limit_bytes=VMEM_LIMIT),
        cost_estimate=pl.CostEstimate(flops=flops, bytes_accessed=8 << 20, transcendentals=0),
    )(*args)


def eye_mask():
    row, lane = (lax.broadcasted_iota(jnp.int32, (LANES, LANES), k) for k in range(2))
    return row == lane


def to_lanes(column):
    wide = jnp.broadcast_to(column, (LANES, LANES))
    return jnp.sum(jnp.where(eye_mask(), wide, 0.0), axis=0, keepdims=True)


def to_column(row):
    wide = jnp.broadcast_to(row, (LANES, LANES))
    return jnp.broadcast_to(jnp.sum(jnp.where(eye_mask(), wide, 0.0), axis=1, keepdims=True), (LANES, LANES))


def split(x):
    high = x.astype(BF16)
    return high, (x - high.astype(F32)).astype(BF16)


def lane_parts(wide):
    lane = lax.broadcasted_iota(jnp.int32, wide.shape, 1)
    rest = wide
    out = jnp.zeros_like(wide)
    for k in range(3):
        part = rest.astype(BF16).astype(F32)
        out = jnp.where(lane == k, part, out)
        rest = rest - part
    return out.astype(BF16)


def tree(combine, values):
    values = list(values)
    while len(values) > 1:
        values = [combine(a, b) for a, b in zip(values[::2], values[1::2])]
    return values[0]


def tree_sum(parts):
    return tree(jnp.add, parts)


def tree_lse(unit, parts):
    peak = tree(jnp.maximum, parts)
    total = tree(jnp.add, [jnp.exp2(unit * (part - peak)) for part in parts])
    return peak + jnp.log(total) * (1.0 / (unit * math.log(2.0)))


def received(refs, group):
    if len(refs[0].shape) == 3:
        return [refs[0][k] for k in range(group)], refs[1:]
    return [ref[...] for ref in refs[:group]], refs[group:]


def dot_t(a, b):
    return lax.dot_general(a, b, (((1,), (1,)), ((), ())), preferred_element_type=F32)


def prepare(
    scale, source_hbm, map_hbm, target_hbm, pot_hbm, source, left_out, turned_out, right_out, plain_out,
    start_map, target, pot, sems,
):
    copies = [
        pltpu.make_async_copy(src, dst, sems.at[k])
        for k, (src, dst) in enumerate(
            [(source_hbm, source), (map_hbm, start_map), (target_hbm, target), (pot_hbm, pot)]
        )
    ]
    for copy in copies:
        copy.start()
    for copy in copies:
        copy.wait()
    width = source.shape[1]
    plain_out[...] = target[...].astype(F32)
    for part in range(target.shape[0] // LANES):
        at = pl.ds(part * LANES, LANES)
        right_out[at, :width] = target[at, :]
        right_out[at, width:] = lane_parts(to_column(pot[:, at] * (1.0 / scale)))
    left_out[...] = jnp.dot(source[...], start_map[...].astype(BF16), preferred_element_type=F32).astype(BF16)
    for at in range(0, source.shape[0], LANES):
        turned_out[:, at : at + LANES] = left_out[at : at + LANES, :].T


def row_first(unit, left_in, right, lse_out, work, peaks, totals, sums):
    rows = left_in.shape[0]
    natural = unit * math.log(2.0)
    lane = lax.broadcasted_iota(jnp.int32, (CHUNK, LANES), 1)
    ones = jnp.where(lane < 3, 1.0, 0.0).astype(BF16)
    group = 16
    for start in range(0, rows, CHUNK):
        left = jnp.concatenate([left_in[start : start + CHUNK, :], ones], axis=1)
        work[start : start + CHUNK, :] = dot_t(left, right[...])
        for at in range(start, start + CHUNK, group):
            tiles = [work[at : at + group, k : k + LANES] for k in range(0, work.shape[1], LANES)]
            peak = functools.reduce(jnp.maximum, tiles)
            peaks[at : at + group, :] = peak
            totals[at : at + group, :] = functools.reduce(jnp.add, [jnp.exp((tile - peak) * natural) for tile in tiles])
    for part in range(rows // LANES):
        here = slice(part * LANES, (part + 1) * LANES)
        lane_peak = peaks[here, :]
        peak = jnp.max(lane_peak, axis=1, keepdims=True)
        total = jnp.sum(totals[here, :] * jnp.exp2((lane_peak - peak) * unit), axis=1, keepdims=True)
        lse_out[part : part + 1, :] = to_lanes(peak)
        sums[part : part + 1, :] = to_lanes(total)
    lse_out[...] = lse_out[...] + jnp.log(sums[...]) * (1.0 / (unit * math.log(2.0)))


def in_row(parts):
    return jnp.concatenate([parts[k : k + 1, :] for k in range(parts.shape[0])], axis=1)


def col_first(group, unit, log_rows, turned, own, other, *refs):
    parts, (block_out, target_out, pot_out, peak_out, lse_out, left, right, *work) = received(refs, group)
    row_pot = -log_rows - tree_lse(unit, parts)
    pot_out[...] = row_pot
    width, rows = turned.shape
    natural = unit * math.log(2.0)
    half = own.shape[0]
    cols = 2 * half
    odd = lax.axis_index("tgt") & 1
    right[pl.ds(pl.multiple_of(odd * half, half), half), :width] = own[:, :width]
    right[pl.ds(pl.multiple_of((1 - odd) * half, half), half), :width] = other[...].astype(BF16)
    for at in range(0, cols, LANES):
        target_out[:, at : at + LANES] = right[at : at + LANES, :width].T
    lane = lax.broadcasted_iota(jnp.int32, (cols, LANES), 1)
    right[:, width:] = jnp.where(lane < 3, 1.0, 0.0).astype(BF16)
    left[:width, :] = turned[...]
    rest = in_row(row_pot)
    pieces = []
    for _ in range(3):
        pieces.append(rest.astype(BF16).astype(F32))
        rest = rest - pieces[-1]
    left[width:, :] = jnp.concatenate([*pieces, jnp.zeros((LANES - 3, rows), F32)], axis=0).astype(BF16)
    for start in range(0, cols, CHUNK):
        scores = work[start // CHUNK % 2]
        scores[...] = jnp.dot(right[start : start + CHUNK, :], left[...], preferred_element_type=F32)
        peaks, sums = [], []
        for at in range(0, CHUNK, 16):
            tiles = [scores[at : at + 16, k : k + LANES] for k in range(0, rows, LANES)]
            peaks.append(functools.reduce(jnp.maximum, tiles))
        peak = jnp.max(jnp.concatenate(peaks, axis=0), axis=1, keepdims=True)
        peak = jnp.broadcast_to(peak, (CHUNK, LANES))
        for at in range(0, CHUNK, 16):
            top = peak[at : at + 16]
            total = None
            for k in range(0, rows, LANES):
                value = jnp.exp((scores[at : at + 16, k : k + LANES] - top) * natural)
                block_out[start + at : start + at + 16, k : k + LANES] = value.astype(BF16)
                total = value if total is None else total + value
            sums.append(total)
        total = jnp.sum(jnp.concatenate(sums, axis=0), axis=1, keepdims=True)
        for part in range(0, CHUNK, LANES):
            here = slice(start + part, start + part + LANES)
            peak_out[:, here] = to_lanes(peak[part : part + LANES])
            lse_out[:, here] = to_lanes(total[part : part + LANES])
    lse_out[...] = peak_out[...] + jnp.log(lse_out[...]) * (1.0 / (unit * math.log(2.0)))


def two_rows(row):
    high, low = split(row)
    zeros = jnp.zeros((14, row.shape[1]), F32)
    return jnp.concatenate([high.astype(F32), low.astype(F32), zeros], axis=0).astype(BF16)


def put_rows(out, start, row):
    for part in range(row.shape[1] // LANES):
        at = start // LANES + part
        out[at : at + 1, :] = row[:, part * LANES : (part + 1) * LANES]


def sums_down(block, row, out):
    rows, cols = block.shape
    cut = cols * 3 // 4 // LANES * LANES
    pair = two_rows(row)
    product = jnp.zeros((16, cut), F32)
    total = jnp.zeros((8, cols - cut), F32)
    for start in range(0, rows, CHUNK):
        product += jnp.dot(pair[:, start : start + CHUNK], block[start : start + CHUNK, :cut], preferred_element_type=F32)
        for part in range(start, start + CHUNK, LANES):
            column = to_column(row[:, part : part + LANES])
            for at in range(0, LANES, 16):
                factor = jnp.concatenate([column[at : at + 16]] * ((cols - cut) // LANES), axis=1)
                value = block[part + at : part + at + 16, cut:].astype(F32) * factor
                total = total + value[:8] + value[8:]
    put_rows(out, 0, jnp.concatenate([product[0:1] + product[1:2], jnp.sum(total, axis=0, keepdims=True)], axis=1))


def sums_across(block, row, out):
    rows, cols = block.shape
    cut = cols // 4 // LANES * LANES
    first = lax.broadcasted_iota(jnp.int32, (16, 2 * LANES), 0) == 0
    pair = jnp.concatenate([two_rows(row[:, :cut]), jnp.where(first, 1.0, 0.0).astype(BF16)], axis=1)
    tiles = [(at, jnp.broadcast_to(row[:, at : at + LANES], (16, LANES))) for at in range(cut, cols, LANES)]
    for start in range(0, rows, CHUNK):
        folded = []
        for here in range(start, start + CHUNK, 16):
            terms = [block[here : here + 16, at : at + LANES].astype(F32) * factor for at, factor in tiles]
            folded.append(functools.reduce(jnp.add, terms))
        folded = split(jnp.concatenate(folded, axis=0))
        both = dot_t(pair, jnp.concatenate([block[start : start + CHUNK, :cut], *folded], axis=1))
        out[:, start : start + CHUNK] = both[0:1] + both[1:2]


def row_second(group, unit, log_cols, block, peak, *refs):
    parts, (pot_out, scale_out, sums_out) = received(refs, group)
    lse = tree_lse(unit, parts)
    pot_out[...] = -log_cols - lse
    scale = jnp.exp2(unit * (peak[...] - lse))
    scale_out[...] = scale
    sums_down(block, scale, sums_out)


def col_later(group, ratio, block, scale, *refs):
    parts, (sums_out,) = received(refs, group)
    sums_across(block, in_row(ratio / tree_sum(parts)), sums_out)
    sums_out[...] *= scale[...]


def row_later(group, block, scale, *refs):
    parts, (sums_out,) = received(refs, group)
    sums_down(block, scale[...] / tree_sum(parts), sums_out)


def row_last(group, unit, block, scale, pot, target, *refs):
    parts, (col_out, sums_out, bary_out) = received(refs, group)
    totals = tree_sum(parts)
    pots = (EPS * math.log(2.0)) * (unit * pot[...] - jnp.log(totals) * (1.0 / math.log(2.0)))
    half = col_out.shape[1]
    col_out[...] = jnp.where((lax.axis_index("tgt") & 1) == 0, pots[:, :half], pots[:, half:])
    row = scale[...] / totals
    scaled = (target[...].astype(F32) * row).astype(BF16)
    left = jnp.concatenate([scaled, two_rows(row)], axis=0)
    width = target.shape[0]
    for start in range(0, block.shape[1], CHUNK):
        both = jnp.dot(left, block[:, start : start + CHUNK], preferred_element_type=F32)
        bary_out[:, start : start + CHUNK] = both[:width]
        put_rows(sums_out, start, both[width : width + 1] + both[width + 1 : width + 2])


def cross_local(group, unit, ratio, source, bary, pot, *refs):
    parts, (row_out, *share_outs, square) = received(refs, group)
    totals = tree_sum(parts)
    row_out[...] = (EPS * math.log(2.0)) * (unit * pot[...] + jnp.log(ratio / totals) * (1.0 / math.log(2.0)))
    inverse = in_row(1.0 / totals)
    both = jnp.concatenate(split(bary[...] * inverse), axis=0)
    cross = jnp.dot(both, source[...], preferred_element_type=F32)
    width = square.shape[0]
    square[...] = (cross[:width, :] + cross[width:, :]).T
    index = lax.axis_index("src")
    count = len(share_outs)
    height = width // count
    for k, out in zip(range(count - 1, -1, -1), share_outs):
        out[...] = square[pl.ds(pl.multiple_of((index ^ k) * height, height), height), :]


def share_sum(*refs):
    refs[-1][...] = tree_sum([ref[...] for ref in refs[:-1]])


def precise(a, b, axis=1):
    ah, al = split(a)
    bh, bl = split(b)
    return lax.dot_general(
        jnp.concatenate([ah, ah, al], axis=axis),
        jnp.concatenate([bh, bl, bh], axis=0),
        (((axis,), (0,)), ((), ())),
        preferred_element_type=F32,
    )


def polar(*refs):
    shares, (out, square) = refs[:-2], refs[-2:]
    index = lax.axis_index("src")
    height = shares[0].shape[0]
    for k, share in enumerate(shares):
        square[pl.ds(pl.multiple_of((index ^ k) * height, height), height), :] = share[...]
    cross = square[...]
    iterate = cross / jnp.sqrt(jnp.sum(cross * cross) + 1e-06)
    unity = jnp.where(eye_mask(), 1.0, 0.0)
    error = unity - precise(iterate, iterate, 0)
    size = error.shape[0]
    for step in range(NEWTON - 1):
        both = precise(jnp.concatenate([error, iterate], axis=0), error)
        iterate = iterate + 0.5 * both[size:]
        error = precise(both[:size], 0.75 * unity + 0.25 * error)
    out[...] = iterate + 0.5 * precise(iterate, error)


def partners(values, axis, order):
    size = lax.axis_size(axis)
    return [lax.ppermute(values[k], axis, [(me, me ^ k) for me in range(size)]) if k else values[0] for k in order]


def over_src(x):
    size = lax.axis_size("src")
    return partners([x] * size, "src", range(size))


def over_pairs(x):
    size = lax.axis_size("tgt")
    return partners([x] * size, "tgt", range(0, size, 2))


def over_tgt(x):
    return lax.all_to_all(jnp.broadcast_to(x, (lax.axis_size("tgt"),) + x.shape), "tgt", 0, 0)


def shards(source, target, start_map, warm_potential):
    rows, width = source.shape
    cols = target.shape[0]
    n_src, n_tgt = lax.axis_size("src"), lax.axis_size("tgt")
    ratio = (cols * n_tgt) / (rows * n_src)
    scale = 1.0 / (math.sqrt(width) * EPS)
    unit = scale / math.log(2.0)
    log_rows, log_cols = math.log(rows * n_src) / scale, math.log(cols * n_tgt) / scale
    n_pairs = n_tgt // 2
    row_vec = jax.ShapeDtypeStruct((rows // LANES, LANES), F32)
    pair_vec = jax.ShapeDtypeStruct((1, 2 * cols), F32)
    mac = rows * cols * width

    source, left, turned, right, plain = call(
        functools.partial(prepare, scale),
        "prepare",
        (
            jax.ShapeDtypeStruct((rows, width), BF16),
            jax.ShapeDtypeStruct((rows, width), BF16),
            jax.ShapeDtypeStruct((width, rows), BF16),
            jax.ShapeDtypeStruct((cols, width + LANES), BF16),
            jax.ShapeDtypeStruct((cols, width), F32),
        ),
        scratch=[
            pltpu.VMEM((width, width), F32),
            pltpu.VMEM((cols, width), BF16),
            pltpu.VMEM((1, cols), F32),
            pltpu.SemaphoreType.DMA((4,)),
        ],
        flops=2 * rows * width * width,
        space=pltpu.HBM,
    )(*[pltpu.with_memory_space_constraint(x, pltpu.HBM) for x in (source, start_map, target, warm_potential.reshape(1, cols))])
    other = lax.ppermute(plain, "tgt", [(me, me ^ 1) for me in range(n_tgt)])
    lse = call(
        functools.partial(row_first, unit),
        "row_first",
        row_vec,
        scratch=[
            pltpu.VMEM((rows, cols), F32),
            pltpu.VMEM((rows, LANES), F32),
            pltpu.VMEM((rows, LANES), F32),
            pltpu.VMEM(row_vec.shape, F32),
        ],
        flops=4 * mac,
    )(left, right)
    block, targets, row_pot, peak, lse = call(
        functools.partial(col_first, n_tgt, unit, log_rows),
        "col_first",
        (
            jax.ShapeDtypeStruct((2 * cols, rows), BF16),
            jax.ShapeDtypeStruct((width, 2 * cols), BF16),
            row_vec,
            pair_vec,
            pair_vec,
        ),
        scratch=[
            pltpu.VMEM((width + LANES, rows), BF16),
            pltpu.VMEM((2 * cols, width + LANES), BF16),
            pltpu.VMEM((CHUNK, rows), F32),
            pltpu.VMEM((CHUNK, rows), F32),
        ],
        flops=8 * mac,
    )(turned, right, other, over_tgt(lse))
    col_pot, col_scale, sums = call(
        functools.partial(row_second, n_src, unit, log_cols), "row_second", (pair_vec, pair_vec, row_vec), flops=4 * mac
    )(block, peak, *over_src(lse))
    col_later_call = call(
        functools.partial(col_later, n_pairs, ratio),
        "col_later",
        pair_vec,
        flops=4 * mac,
    )
    sums = col_later_call(block, col_scale, *over_pairs(sums))
    sums = call(functools.partial(row_later, n_src), "row_later", row_vec, flops=4 * mac)(
        block, col_scale, *over_src(sums)
    )
    sums = col_later_call(block, col_scale, *over_pairs(sums))
    col_out, sums, bary = call(
        functools.partial(row_last, n_src, unit),
        "row_last",
        (jax.ShapeDtypeStruct((1, cols), F32), row_vec, jax.ShapeDtypeStruct((width, rows), F32)),
        flops=4 * mac,
    )(block, col_scale, col_pot, targets, *over_src(sums))
    square = jax.ShapeDtypeStruct((width, width), F32)
    share_shape = jax.ShapeDtypeStruct((width // n_src, width), F32)
    row_out, *shares = call(
        functools.partial(cross_local, n_pairs, unit, ratio),
        "cross_local",
        (row_vec,) + (share_shape,) * n_src,
        scratch=[pltpu.VMEM((width, width), F32)],
        flops=2 * rows * width * width,
    )(source, bary, row_pot, *over_pairs(sums))
    share = call(share_sum, "share_sum", share_shape)(*partners(shares[::-1], "src", range(n_src - 1, -1, -1)))
    share = call(share_sum, "share_sum", share_shape)(*over_pairs(share))
    new_map = call(polar, "polar", square, scratch=[pltpu.VMEM((width, width), F32)], flops=1 << 27)(*over_src(share))
    return row_out.reshape(rows), col_out.reshape(cols), new_map


def solution(mesh):
    placed = (P("src", None), P("tgt", None), P(), P("tgt"))
    return jax.shard_map(
        shards, mesh=mesh, in_specs=placed, out_specs=(P("src"), P("tgt"), P()), check_vma=False
    )
```

```python
import functools
import math

import jax
import jax.numpy as jnp
from jax import lax
from jax.experimental import pallas as pl
from jax.experimental.pallas import tpu as pltpu
from jax.sharding import PartitionSpec as P

NEWTON = 10
EPS = 0.05
LANES = 128
CHUNK = 256
VMEM_LIMIT = 40 * 1024 * 1024

F32 = jnp.float32
BF16 = jnp.bfloat16


def call(body, name, out_shape, scratch=(), flops=0, space=pltpu.VMEM):
    return lambda *args: pl.pallas_call(
        body,
        name=name,
        out_shape=out_shape,
        in_specs=[pl.BlockSpec(memory_space=space)] * len(args),
        out_specs=jax.tree.map(lambda _: pl.BlockSpec(memory_space=pltpu.VMEM), out_shape),
        scratch_shapes=scratch,
        compiler_params=pltpu.CompilerParams(vmem_limit_bytes=VMEM_LIMIT),
        cost_estimate=pl.CostEstimate(flops=flops, bytes_accessed=8 << 20, transcendentals=0),
    )(*args)


def eye_mask():
    row, lane = (lax.broadcasted_iota(jnp.int32, (LANES, LANES), k) for k in range(2))
    return row == lane


def to_lanes(column):
    wide = jnp.broadcast_to(column, (LANES, LANES))
    return jnp.sum(jnp.where(eye_mask(), wide, 0.0), axis=0, keepdims=True)


def to_column(row):
    wide = jnp.broadcast_to(row, (LANES, LANES))
    return jnp.broadcast_to(jnp.sum(jnp.where(eye_mask(), wide, 0.0), axis=1, keepdims=True), (LANES, LANES))


def split(x):
    high = x.astype(BF16)
    return high, (x - high.astype(F32)).astype(BF16)


def lane_parts(wide):
    lane = lax.broadcasted_iota(jnp.int32, wide.shape, 1)
    rest = wide
    out = jnp.zeros_like(wide)
    for k in range(3):
        part = rest.astype(BF16).astype(F32)
        out = jnp.where(lane == k, part, out)
        rest = rest - part
    return out.astype(BF16)


def tree(combine, values):
    values = list(values)
    while len(values) > 1:
        values = [combine(a, b) for a, b in zip(values[::2], values[1::2])]
    return values[0]


def tree_sum(parts):
    return tree(jnp.add, parts)


def tree_lse(unit, parts):
    peak = tree(jnp.maximum, parts)
    total = tree(jnp.add, [jnp.exp2(unit * (part - peak)) for part in parts])
    return peak + jnp.log(total) * (1.0 / (unit * math.log(2.0)))


def received(refs, group):
    if len(refs[0].shape) == 3:
        return [refs[0][k] for k in range(group)], refs[1:]
    return [ref[...] for ref in refs[:group]], refs[group:]


def dot_t(a, b):
    return lax.dot_general(a, b, (((1,), (1,)), ((), ())), preferred_element_type=F32)


def prepare(
    scale, source_hbm, map_hbm, target_hbm, pot_hbm, source, left_out, turned_out, right_out, plain_out,
    start_map, target, pot, sems,
):
    copies = [
        pltpu.make_async_copy(src, dst, sems.at[k])
        for k, (src, dst) in enumerate(
            [(source_hbm, source), (map_hbm, start_map), (target_hbm, target), (pot_hbm, pot)]
        )
    ]
    for copy in copies:
        copy.start()
    for copy in copies:
        copy.wait()
    width = source.shape[1]
    plain_out[...] = target[...].astype(F32)
    for part in range(target.shape[0] // LANES):
        at = pl.ds(part * LANES, LANES)
        right_out[at, :width] = target[at, :]
        right_out[at, width:] = lane_parts(to_column(pot[:, at] * (1.0 / scale)))
    left_out[...] = jnp.dot(source[...], start_map[...].astype(BF16), preferred_element_type=F32).astype(BF16)
    for at in range(0, source.shape[0], LANES):
        turned_out[:, at : at + LANES] = left_out[at : at + LANES, :].T


def row_first(unit, left_in, right, lse_out, work, peaks, totals, sums):
    rows = left_in.shape[0]
    lane = lax.broadcasted_iota(jnp.int32, (CHUNK, LANES), 1)
    ones = jnp.where(lane < 3, 1.0, 0.0).astype(BF16)
    group = 16
    for start in range(0, rows, CHUNK):
        left = jnp.concatenate([left_in[start : start + CHUNK, :], ones], axis=1)
        work[start : start + CHUNK, :] = dot_t(left, right[...])
        for at in range(start, start + CHUNK, group):
            tiles = [work[at : at + group, k : k + LANES] for k in range(0, work.shape[1], LANES)]
            peak = functools.reduce(jnp.maximum, tiles)
            peaks[at : at + group, :] = peak
            totals[at : at + group, :] = functools.reduce(jnp.add, [jnp.exp2((tile - peak) * unit) for tile in tiles])
    for part in range(rows // LANES):
        here = slice(part * LANES, (part + 1) * LANES)
        lane_peak = peaks[here, :]
        peak = jnp.max(lane_peak, axis=1, keepdims=True)
        total = jnp.sum(totals[here, :] * jnp.exp2((lane_peak - peak) * unit), axis=1, keepdims=True)
        lse_out[part : part + 1, :] = to_lanes(peak)
        sums[part : part + 1, :] = to_lanes(total)
    lse_out[...] = lse_out[...] + jnp.log(sums[...]) * (1.0 / (unit * math.log(2.0)))


def in_row(parts):
    return jnp.concatenate([parts[k : k + 1, :] for k in range(parts.shape[0])], axis=1)


def col_first(group, unit, log_rows, turned, own, other, *refs):
    parts, (block_out, target_out, pot_out, peak_out, lse_out, left, right, *work) = received(refs, group)
    row_pot = -log_rows - tree_lse(unit, parts)
    pot_out[...] = row_pot
    width, rows = turned.shape
    half = own.shape[0]
    cols = 2 * half
    odd = lax.axis_index("tgt") & 1
    right[pl.ds(pl.multiple_of(odd * half, half), half), :width] = own[:, :width]
    right[pl.ds(pl.multiple_of((1 - odd) * half, half), half), :width] = other[...].astype(BF16)
    target_out[...] = right[:, :width]
    lane = lax.broadcasted_iota(jnp.int32, (cols, LANES), 1)
    right[:, width:] = jnp.where(lane < 3, 1.0, 0.0).astype(BF16)
    left[:width, :] = turned[...]
    rest = in_row(row_pot)
    pieces = []
    for _ in range(3):
        pieces.append(rest.astype(BF16).astype(F32))
        rest = rest - pieces[-1]
    left[width:, :] = jnp.concatenate([*pieces, jnp.zeros((LANES - 3, rows), F32)], axis=0).astype(BF16)
    for start in range(0, cols, CHUNK):
        scores = work[start // CHUNK % 2]
        scores[...] = jnp.dot(right[start : start + CHUNK, :], left[...], preferred_element_type=F32)
        peaks, sums = [], []
        for at in range(0, CHUNK, 16):
            tiles = [scores[at : at + 16, k : k + LANES] for k in range(0, rows, LANES)]
            peaks.append(functools.reduce(jnp.maximum, tiles))
        peak = jnp.max(jnp.concatenate(peaks, axis=0), axis=1, keepdims=True)
        peak = jnp.broadcast_to(peak, (CHUNK, LANES))
        for at in range(0, CHUNK, 16):
            top = peak[at : at + 16]
            total = None
            for k in range(0, rows, LANES):
                value = jnp.exp2((scores[at : at + 16, k : k + LANES] - top) * unit)
                block_out[start + at : start + at + 16, k : k + LANES] = value.astype(BF16)
                total = value if total is None else total + value
            sums.append(total)
        total = jnp.sum(jnp.concatenate(sums, axis=0), axis=1, keepdims=True)
        for part in range(0, CHUNK, LANES):
            here = slice(start + part, start + part + LANES)
            peak_out[:, here] = to_lanes(peak[part : part + LANES])
            lse_out[:, here] = to_lanes(total[part : part + LANES])
    lse_out[...] = peak_out[...] + jnp.log(lse_out[...]) * (1.0 / (unit * math.log(2.0)))


def two_rows(row):
    high, low = split(row)
    zeros = jnp.zeros((14, row.shape[1]), F32)
    return jnp.concatenate([high.astype(F32), low.astype(F32), zeros], axis=0).astype(BF16)


def put_rows(out, start, row):
    for part in range(row.shape[1] // LANES):
        at = start // LANES + part
        out[at : at + 1, :] = row[:, part * LANES : (part + 1) * LANES]


def sums_down(block, row, out):
    rows, cols = block.shape
    cut = cols * 3 // 4 // LANES * LANES
    pair = two_rows(row)
    product = jnp.zeros((16, cut), F32)
    total = jnp.zeros((8, cols - cut), F32)
    for start in range(0, rows, CHUNK):
        product += jnp.dot(pair[:, start : start + CHUNK], block[start : start + CHUNK, :cut], preferred_element_type=F32)
        for part in range(start, start + CHUNK, LANES):
            column = to_column(row[:, part : part + LANES])
            for at in range(0, LANES, 16):
                factor = jnp.concatenate([column[at : at + 16]] * ((cols - cut) // LANES), axis=1)
                value = block[part + at : part + at + 16, cut:].astype(F32) * factor
                total = total + value[:8] + value[8:]
    put_rows(out, 0, jnp.concatenate([product[0:1] + product[1:2], jnp.sum(total, axis=0, keepdims=True)], axis=1))


def sums_across(block, row, out):
    rows, cols = block.shape
    cut = cols // 4 // LANES * LANES
    first = lax.broadcasted_iota(jnp.int32, (16, 2 * LANES), 0) == 0
    pair = jnp.concatenate([two_rows(row[:, :cut]), jnp.where(first, 1.0, 0.0).astype(BF16)], axis=1)
    tiles = [(at, jnp.broadcast_to(row[:, at : at + LANES], (16, LANES))) for at in range(cut, cols, LANES)]
    for start in range(0, rows, CHUNK):
        folded = []
        for here in range(start, start + CHUNK, 16):
            terms = [block[here : here + 16, at : at + LANES].astype(F32) * factor for at, factor in tiles]
            folded.append(functools.reduce(jnp.add, terms))
        folded = split(jnp.concatenate(folded, axis=0))
        both = dot_t(pair, jnp.concatenate([block[start : start + CHUNK, :cut], *folded], axis=1))
        out[:, start : start + CHUNK] = both[0:1] + both[1:2]


def row_second(group, unit, log_cols, block, peak, *refs):
    parts, (pot_out, scale_out, sums_out) = received(refs, group)
    lse = tree_lse(unit, parts)
    pot_out[...] = -log_cols - lse
    scale = jnp.exp2(unit * (peak[...] - lse))
    scale_out[...] = scale
    sums_down(block, scale, sums_out)


def col_later(group, ratio, block, scale, *refs):
    parts, (sums_out,) = received(refs, group)
    sums_across(block, in_row(ratio / tree_sum(parts)), sums_out)
    sums_out[...] *= scale[...]


def row_later(group, block, scale, *refs):
    parts, (sums_out,) = received(refs, group)
    sums_down(block, scale[...] / tree_sum(parts), sums_out)


def row_last(group, unit, block, scale, pot, *refs):
    parts, (col_out, factor_out, sums_out) = received(refs, group)
    totals = tree_sum(parts)
    pots = (EPS * math.log(2.0)) * (unit * pot[...] - jnp.log(totals) * (1.0 / math.log(2.0)))
    half = col_out.shape[1]
    col_out[...] = jnp.where((lax.axis_index("tgt") & 1) == 0, pots[:, :half], pots[:, half:])
    row = scale[...] / totals
    factor_out[...] = row
    sums_down(block, row, sums_out)


def barycentre(block, factor, target, bary_out):
    pieces = []
    for at in range(0, target.shape[0], LANES):
        pieces.append((target[at : at + LANES, :].T.astype(F32) * factor[:, at : at + LANES]).astype(BF16))
    left = jnp.concatenate(pieces, axis=1)
    for start in range(0, block.shape[1], CHUNK):
        bary_out[:, start : start + CHUNK] = jnp.dot(
            left, block[:, start : start + CHUNK], preferred_element_type=F32
        )


def cross_local(group, unit, ratio, source, bary, pot, *refs):
    parts, (row_out, *share_outs, square) = received(refs, group)
    totals = tree_sum(parts)
    row_out[...] = (EPS * math.log(2.0)) * (unit * pot[...] + jnp.log(ratio / totals) * (1.0 / math.log(2.0)))
    inverse = in_row(1.0 / totals)
    both = jnp.concatenate(split(bary[...] * inverse), axis=0)
    cross = jnp.dot(both, source[...], preferred_element_type=F32)
    width = square.shape[0]
    square[...] = (cross[:width, :] + cross[width:, :]).T
    index = lax.axis_index("src")
    count = len(share_outs)
    height = width // count
    for k, out in zip(range(count - 1, -1, -1), share_outs):
        out[...] = square[pl.ds(pl.multiple_of((index ^ k) * height, height), height), :]


def share_sum(*refs):
    refs[-1][...] = tree_sum([ref[...] for ref in refs[:-1]])


def precise(a, b, axis=1):
    ah, al = split(a)
    bh, bl = split(b)
    return lax.dot_general(
        jnp.concatenate([ah, ah, al], axis=axis),
        jnp.concatenate([bh, bl, bh], axis=0),
        (((axis,), (0,)), ((), ())),
        preferred_element_type=F32,
    )


def polar(*refs):
    shares, (out, square) = refs[:-2], refs[-2:]
    index = lax.axis_index("src")
    height = shares[0].shape[0]
    for k, share in enumerate(shares):
        square[pl.ds(pl.multiple_of((index ^ k) * height, height), height), :] = share[...]
    cross = square[...]
    iterate = cross / jnp.sqrt(jnp.sum(cross * cross) + 1e-06)
    unity = jnp.where(eye_mask(), 1.0, 0.0)
    error = unity - precise(iterate, iterate, 0)
    size = error.shape[0]
    for step in range(NEWTON - 1):
        both = precise(jnp.concatenate([error, iterate], axis=0), error)
        iterate = iterate + 0.5 * both[size:]
        error = precise(both[:size], 0.75 * unity + 0.25 * error)
    out[...] = iterate + 0.5 * precise(iterate, error)


def partners(values, axis, order):
    size = lax.axis_size(axis)
    return [lax.ppermute(values[k], axis, [(me, me ^ k) for me in range(size)]) if k else values[0] for k in order]


def over_src(x):
    size = lax.axis_size("src")
    return partners([x] * size, "src", range(size))


def over_pairs(x):
    size = lax.axis_size("tgt")
    return partners([x] * size, "tgt", range(0, size, 2))


def over_tgt(x):
    return lax.all_to_all(jnp.broadcast_to(x, (lax.axis_size("tgt"),) + x.shape), "tgt", 0, 0)


def shards(source, target, start_map, warm_potential):
    rows, width = source.shape
    cols = target.shape[0]
    n_src, n_tgt = lax.axis_size("src"), lax.axis_size("tgt")
    ratio = (cols * n_tgt) / (rows * n_src)
    scale = 1.0 / (math.sqrt(width) * EPS)
    unit = scale / math.log(2.0)
    log_rows, log_cols = math.log(rows * n_src) / scale, math.log(cols * n_tgt) / scale
    n_pairs = n_tgt // 2
    row_vec = jax.ShapeDtypeStruct((rows // LANES, LANES), F32)
    pair_vec = jax.ShapeDtypeStruct((1, 2 * cols), F32)
    mac = rows * cols * width

    source, left, turned, right, plain = call(
        functools.partial(prepare, scale),
        "prepare",
        (
            jax.ShapeDtypeStruct((rows, width), BF16),
            jax.ShapeDtypeStruct((rows, width), BF16),
            jax.ShapeDtypeStruct((width, rows), BF16),
            jax.ShapeDtypeStruct((cols, width + LANES), BF16),
            jax.ShapeDtypeStruct((cols, width), F32),
        ),
        scratch=[
            pltpu.VMEM((width, width), F32),
            pltpu.VMEM((cols, width), BF16),
            pltpu.VMEM((1, cols), F32),
            pltpu.SemaphoreType.DMA((4,)),
        ],
        flops=2 * rows * width * width,
        space=pltpu.HBM,
    )(*[pltpu.with_memory_space_constraint(x, pltpu.HBM) for x in (source, start_map, target, warm_potential.reshape(1, cols))])
    other = lax.ppermute(plain, "tgt", [(me, me ^ 1) for me in range(n_tgt)])
    lse = call(
        functools.partial(row_first, unit),
        "row_first",
        row_vec,
        scratch=[
            pltpu.VMEM((rows, cols), F32),
            pltpu.VMEM((rows, LANES), F32),
            pltpu.VMEM((rows, LANES), F32),
            pltpu.VMEM(row_vec.shape, F32),
        ],
        flops=4 * mac,
    )(left, right)
    block, targets, row_pot, peak, lse = call(
        functools.partial(col_first, n_tgt, unit, log_rows),
        "col_first",
        (
            jax.ShapeDtypeStruct((2 * cols, rows), BF16),
            jax.ShapeDtypeStruct((2 * cols, width), BF16),
            row_vec,
            pair_vec,
            pair_vec,
        ),
        scratch=[
            pltpu.VMEM((width + LANES, rows), BF16),
            pltpu.VMEM((2 * cols, width + LANES), BF16),
            pltpu.VMEM((CHUNK, rows), F32),
            pltpu.VMEM((CHUNK, rows), F32),
        ],
        flops=8 * mac,
    )(turned, right, other, over_tgt(lse))
    col_pot, col_scale, sums = call(
        functools.partial(row_second, n_src, unit, log_cols), "row_second", (pair_vec, pair_vec, row_vec), flops=4 * mac
    )(block, peak, *over_src(lse))
    col_later_call = call(
        functools.partial(col_later, n_pairs, ratio),
        "col_later",
        pair_vec,
        flops=4 * mac,
    )
    sums = col_later_call(block, col_scale, *over_pairs(sums))
    sums = call(functools.partial(row_later, n_src), "row_later", row_vec, flops=4 * mac)(
        block, col_scale, *over_src(sums)
    )
    sums = col_later_call(block, col_scale, *over_pairs(sums))
    col_out, factor, sums = call(
        functools.partial(row_last, n_src, unit),
        "row_last",
        (jax.ShapeDtypeStruct((1, cols), F32), pair_vec, row_vec),
        flops=4 * mac,
    )(block, col_scale, col_pot, *over_src(sums))
    bary = call(barycentre, "barycentre", jax.ShapeDtypeStruct((width, rows), F32), flops=4 * mac)(
        block, factor, targets
    )
    square = jax.ShapeDtypeStruct((width, width), F32)
    share_shape = jax.ShapeDtypeStruct((width // n_src, width), F32)
    row_out, *shares = call(
        functools.partial(cross_local, n_pairs, unit, ratio),
        "cross_local",
        (row_vec,) + (share_shape,) * n_src,
        scratch=[pltpu.VMEM((width, width), F32)],
        flops=2 * rows * width * width,
    )(source, bary, row_pot, *over_pairs(sums))
    share = call(share_sum, "share_sum", share_shape)(*partners(shares[::-1], "src", range(n_src - 1, -1, -1)))
    share = call(share_sum, "share_sum", share_shape)(*over_pairs(share))
    new_map = call(polar, "polar", square, scratch=[pltpu.VMEM((width, width), F32)], flops=1 << 27)(*over_src(share))
    return row_out.reshape(rows), col_out.reshape(cols), new_map


def solution(mesh):
    placed = (P("src", None), P("tgt", None), P(), P("tgt"))
    return jax.shard_map(
        shards, mesh=mesh, in_specs=placed, out_specs=(P("src"), P("tgt"), P()), check_vma=False
    )
```

```python
import functools
import math

import jax
import jax.numpy as jnp
from jax import lax
from jax.experimental import pallas as pl
from jax.experimental.pallas import tpu as pltpu
from jax.sharding import PartitionSpec as P

NEWTON = 10
EPS = 0.05
LANES = 128
CHUNK = 256
VMEM_LIMIT = 40 * 1024 * 1024

F32 = jnp.float32
BF16 = jnp.bfloat16


def call(body, name, out_shape, scratch=(), flops=0, space=pltpu.VMEM):
    return lambda *args: pl.pallas_call(
        body,
        name=name,
        out_shape=out_shape,
        in_specs=[pl.BlockSpec(memory_space=space)] * len(args),
        out_specs=jax.tree.map(lambda _: pl.BlockSpec(memory_space=pltpu.VMEM), out_shape),
        scratch_shapes=scratch,
        compiler_params=pltpu.CompilerParams(vmem_limit_bytes=VMEM_LIMIT),
        cost_estimate=pl.CostEstimate(flops=flops, bytes_accessed=8 << 20, transcendentals=0),
    )(*args)


def eye_mask():
    row, lane = (lax.broadcasted_iota(jnp.int32, (LANES, LANES), k) for k in range(2))
    return row == lane


def to_lanes(column):
    wide = jnp.broadcast_to(column, (LANES, LANES))
    return jnp.sum(jnp.where(eye_mask(), wide, 0.0), axis=0, keepdims=True)


def to_column(row):
    wide = jnp.broadcast_to(row, (LANES, LANES))
    return jnp.broadcast_to(jnp.sum(jnp.where(eye_mask(), wide, 0.0), axis=1, keepdims=True), (LANES, LANES))


def split(x):
    high = x.astype(BF16)
    return high, (x - high.astype(F32)).astype(BF16)


def lane_parts(wide):
    lane = lax.broadcasted_iota(jnp.int32, wide.shape, 1)
    rest = wide
    out = jnp.zeros_like(wide)
    for k in range(3):
        part = rest.astype(BF16).astype(F32)
        out = jnp.where(lane == k, part, out)
        rest = rest - part
    return out.astype(BF16)


def tree(combine, values):
    values = list(values)
    while len(values) > 1:
        values = [combine(a, b) for a, b in zip(values[::2], values[1::2])]
    return values[0]


def tree_sum(parts):
    return tree(jnp.add, parts)


def tree_lse(unit, parts):
    peak = tree(jnp.maximum, parts)
    total = tree(jnp.add, [jnp.exp2(unit * (part - peak)) for part in parts])
    return peak + jnp.log(total) * (1.0 / (unit * math.log(2.0)))


def received(refs, group):
    if len(refs[0].shape) == 3:
        return [refs[0][k] for k in range(group)], refs[1:]
    return [ref[...] for ref in refs[:group]], refs[group:]


def dot_t(a, b):
    return lax.dot_general(a, b, (((1,), (1,)), ((), ())), preferred_element_type=F32)


def prepare(
    scale, source_hbm, map_hbm, target_hbm, pot_hbm, source, left_out, turned_out, right_out, plain_out,
    start_map, target, pot, sems,
):
    copies = [
        pltpu.make_async_copy(src, dst, sems.at[k])
        for k, (src, dst) in enumerate(
            [(source_hbm, source), (map_hbm, start_map), (target_hbm, target), (pot_hbm, pot)]
        )
    ]
    for copy in copies:
        copy.start()
    for copy in copies:
        copy.wait()
    width = source.shape[1]
    plain_out[...] = target[...].astype(F32)
    for part in range(target.shape[0] // LANES):
        at = pl.ds(part * LANES, LANES)
        right_out[at, :width] = target[at, :]
        right_out[at, width:] = lane_parts(to_column(pot[:, at] * (1.0 / scale)))
    left_out[...] = jnp.dot(source[...], start_map[...].astype(BF16), preferred_element_type=F32).astype(BF16)
    for at in range(0, source.shape[0], LANES):
        turned_out[:, at : at + LANES] = left_out[at : at + LANES, :].T


def row_first(unit, left_in, right, lse_out, work, peaks, totals, sums):
    rows = left_in.shape[0]
    lane = lax.broadcasted_iota(jnp.int32, (CHUNK, LANES), 1)
    ones = jnp.where(lane < 3, 1.0, 0.0).astype(BF16)
    group = 16
    for start in range(0, rows, CHUNK):
        left = jnp.concatenate([left_in[start : start + CHUNK, :], ones], axis=1)
        work[start : start + CHUNK, :] = dot_t(left, right[...])
        for at in range(start, start + CHUNK, group):
            tiles = [work[at : at + group, k : k + LANES] for k in range(0, work.shape[1], LANES)]
            peak = functools.reduce(jnp.maximum, tiles)
            peaks[at : at + group, :] = peak
            totals[at : at + group, :] = functools.reduce(jnp.add, [jnp.exp2((tile - peak) * unit) for tile in tiles])
    for part in range(rows // LANES):
        here = slice(part * LANES, (part + 1) * LANES)
        lane_peak = peaks[here, :]
        peak = jnp.max(lane_peak, axis=1, keepdims=True)
        total = jnp.sum(totals[here, :] * jnp.exp2((lane_peak - peak) * unit), axis=1, keepdims=True)
        lse_out[part : part + 1, :] = to_lanes(peak)
        sums[part : part + 1, :] = to_lanes(total)
    lse_out[...] = lse_out[...] + jnp.log(sums[...]) * (1.0 / (unit * math.log(2.0)))


def in_row(parts):
    return jnp.concatenate([parts[k : k + 1, :] for k in range(parts.shape[0])], axis=1)


def col_first(group, unit, log_rows, turned, own, other, *refs):
    parts, (block_out, target_out, pot_out, peak_out, lse_out, left, right, *work) = received(refs, group)
    row_pot = -log_rows - tree_lse(unit, parts)
    pot_out[...] = row_pot
    width, rows = turned.shape
    half = own.shape[0]
    cols = 2 * half
    odd = lax.axis_index("tgt") & 1
    right[pl.ds(pl.multiple_of(odd * half, half), half), :width] = own[:, :width]
    right[pl.ds(pl.multiple_of((1 - odd) * half, half), half), :width] = other[...].astype(BF16)
    target_out[...] = right[:, :width]
    lane = lax.broadcasted_iota(jnp.int32, (cols, LANES), 1)
    right[:, width:] = jnp.where(lane < 3, 1.0, 0.0).astype(BF16)
    left[:width, :] = turned[...]
    rest = in_row(row_pot)
    pieces = []
    for _ in range(3):
        pieces.append(rest.astype(BF16).astype(F32))
        rest = rest - pieces[-1]
    left[width:, :] = jnp.concatenate([*pieces, jnp.zeros((LANES - 3, rows), F32)], axis=0).astype(BF16)
    for start in range(0, cols, CHUNK):
        scores = work[start // CHUNK % 2]
        scores[...] = jnp.dot(right[start : start + CHUNK, :], left[...], preferred_element_type=F32)
        peaks, sums = [], []
        for at in range(0, CHUNK, 16):
            tiles = [scores[at : at + 16, k : k + LANES] for k in range(0, rows, LANES)]
            peaks.append(functools.reduce(jnp.maximum, tiles))
        peak = jnp.max(jnp.concatenate(peaks, axis=0), axis=1, keepdims=True)
        peak = jnp.broadcast_to(peak, (CHUNK, LANES))
        for at in range(0, CHUNK, 16):
            top = peak[at : at + 16]
            total = None
            for k in range(0, rows, LANES):
                value = jnp.exp2((scores[at : at + 16, k : k + LANES] - top) * unit)
                block_out[start + at : start + at + 16, k : k + LANES] = value.astype(BF16)
                total = value if total is None else total + value
            sums.append(total)
        total = jnp.sum(jnp.concatenate(sums, axis=0), axis=1, keepdims=True)
        for part in range(0, CHUNK, LANES):
            here = slice(start + part, start + part + LANES)
            peak_out[:, here] = to_lanes(peak[part : part + LANES])
            lse_out[:, here] = to_lanes(total[part : part + LANES])
    lse_out[...] = peak_out[...] + jnp.log(lse_out[...]) * (1.0 / (unit * math.log(2.0)))


def two_rows(row):
    high, low = split(row)
    zeros = jnp.zeros((14, row.shape[1]), F32)
    return jnp.concatenate([high.astype(F32), low.astype(F32), zeros], axis=0).astype(BF16)


def put_rows(out, start, row):
    for part in range(row.shape[1] // LANES):
        at = start // LANES + part
        out[at : at + 1, :] = row[:, part * LANES : (part + 1) * LANES]


def sums_down(block, row, out):
    rows, cols = block.shape
    cut = cols * 3 // 4 // LANES * LANES
    pair = two_rows(row)
    product = jnp.zeros((16, cut), F32)
    total = jnp.zeros((8, cols - cut), F32)
    for start in range(0, rows, CHUNK):
        product += jnp.dot(pair[:, start : start + CHUNK], block[start : start + CHUNK, :cut], preferred_element_type=F32)
        for part in range(start, start + CHUNK, LANES):
            column = to_column(row[:, part : part + LANES])
            for at in range(0, LANES, 16):
                factor = jnp.concatenate([column[at : at + 16]] * ((cols - cut) // LANES), axis=1)
                value = block[part + at : part + at + 16, cut:].astype(F32) * factor
                total = total + value[:8] + value[8:]
    put_rows(out, 0, jnp.concatenate([product[0:1] + product[1:2], jnp.sum(total, axis=0, keepdims=True)], axis=1))


def sums_across(block, row, out):
    rows, cols = block.shape
    cut = cols // 4 // LANES * LANES
    first = lax.broadcasted_iota(jnp.int32, (16, 2 * LANES), 0) == 0
    pair = jnp.concatenate([two_rows(row[:, :cut]), jnp.where(first, 1.0, 0.0).astype(BF16)], axis=1)
    tiles = [(at, jnp.broadcast_to(row[:, at : at + LANES], (16, LANES))) for at in range(cut, cols, LANES)]
    for start in range(0, rows, CHUNK):
        folded = []
        for here in range(start, start + CHUNK, 16):
            terms = [block[here : here + 16, at : at + LANES].astype(F32) * factor for at, factor in tiles]
            folded.append(functools.reduce(jnp.add, terms))
        folded = split(jnp.concatenate(folded, axis=0))
        both = dot_t(pair, jnp.concatenate([block[start : start + CHUNK, :cut], *folded], axis=1))
        out[:, start : start + CHUNK] = both[0:1] + both[1:2]


def row_second(group, unit, log_cols, block, peak, *refs):
    parts, (pot_out, scale_out, sums_out) = received(refs, group)
    lse = tree_lse(unit, parts)
    pot_out[...] = -log_cols - lse
    scale = jnp.exp2(unit * (peak[...] - lse))
    scale_out[...] = scale
    sums_down(block, scale, sums_out)


def col_later(group, ratio, block, scale, *refs):
    parts, (sums_out,) = received(refs, group)
    sums_across(block, in_row(ratio / tree_sum(parts)), sums_out)
    sums_out[...] *= scale[...]


def row_later(group, block, scale, *refs):
    parts, (sums_out,) = received(refs, group)
    sums_down(block, scale[...] / tree_sum(parts), sums_out)


def row_last(group, block, scale, *refs):
    parts, (totals_out, factor_out, sums_out) = received(refs, group)
    totals = tree_sum(parts)
    totals_out[...] = totals
    row = scale[...] / totals
    factor_out[...] = row
    sums_down(block, row, sums_out)


def barycentre(unit, block, factor, target, pot, totals, bary_out, col_out):
    pots = (EPS * math.log(2.0)) * (unit * pot[...] - jnp.log(totals[...]) * (1.0 / math.log(2.0)))
    half = col_out.shape[1]
    col_out[...] = jnp.where((lax.axis_index("tgt") & 1) == 0, pots[:, :half], pots[:, half:])
    pieces = []
    for at in range(0, target.shape[0], LANES):
        pieces.append((target[at : at + LANES, :].T.astype(F32) * factor[:, at : at + LANES]).astype(BF16))
    left = jnp.concatenate(pieces, axis=1)
    for start in range(0, block.shape[1], CHUNK):
        bary_out[:, start : start + CHUNK] = jnp.dot(
            left, block[:, start : start + CHUNK], preferred_element_type=F32
        )


def row_potential(unit, ratio, pot, totals, out):
    out[...] = (EPS * math.log(2.0)) * (unit * pot[...] + jnp.log(ratio / totals[...]) * (1.0 / math.log(2.0)))


def cross_local(group, source, bary, *refs):
    parts, (totals_out, *share_outs, square) = received(refs, group)
    totals = tree_sum(parts)
    totals_out[...] = totals
    inverse = in_row(1.0 / totals)
    both = jnp.concatenate(split(bary[...] * inverse), axis=0)
    cross = jnp.dot(both, source[...], preferred_element_type=F32)
    width = square.shape[0]
    square[...] = (cross[:width, :] + cross[width:, :]).T
    index = lax.axis_index("src")
    count = len(share_outs)
    height = width // count
    for k, out in zip(range(count - 1, -1, -1), share_outs):
        out[...] = square[pl.ds(pl.multiple_of((index ^ k) * height, height), height), :]


def share_sum(*refs):
    refs[-1][...] = tree_sum([ref[...] for ref in refs[:-1]])


def precise(a, b, axis=1):
    ah, al = split(a)
    bh, bl = split(b)
    return lax.dot_general(
        jnp.concatenate([ah, ah, al], axis=axis),
        jnp.concatenate([bh, bl, bh], axis=0),
        (((axis,), (0,)), ((), ())),
        preferred_element_type=F32,
    )


def polar(*refs):
    shares, (out, square) = refs[:-2], refs[-2:]
    index = lax.axis_index("src")
    height = shares[0].shape[0]
    for k, share in enumerate(shares):
        square[pl.ds(pl.multiple_of((index ^ k) * height, height), height), :] = share[...]
    cross = square[...]
    iterate = cross / jnp.sqrt(jnp.sum(cross * cross) + 1e-06)
    unity = jnp.where(eye_mask(), 1.0, 0.0)
    error = unity - precise(iterate, iterate, 0)
    size = error.shape[0]
    for step in range(NEWTON - 1):
        both = precise(jnp.concatenate([error, iterate], axis=0), error)
        iterate = iterate + 0.5 * both[size:]
        error = precise(both[:size], 0.75 * unity + 0.25 * error)
    out[...] = iterate + 0.5 * precise(iterate, error)


def partners(values, axis, order):
    size = lax.axis_size(axis)
    return [lax.ppermute(values[k], axis, [(me, me ^ k) for me in range(size)]) if k else values[0] for k in order]


def over_src(x):
    size = lax.axis_size("src")
    return partners([x] * size, "src", range(size))


def over_pairs(x):
    size = lax.axis_size("tgt")
    return partners([x] * size, "tgt", range(0, size, 2))


def over_tgt(x):
    return lax.all_to_all(jnp.broadcast_to(x, (lax.axis_size("tgt"),) + x.shape), "tgt", 0, 0)


def shards(source, target, start_map, warm_potential):
    rows, width = source.shape
    cols = target.shape[0]
    n_src, n_tgt = lax.axis_size("src"), lax.axis_size("tgt")
    ratio = (cols * n_tgt) / (rows * n_src)
    scale = 1.0 / (math.sqrt(width) * EPS)
    unit = scale / math.log(2.0)
    log_rows, log_cols = math.log(rows * n_src) / scale, math.log(cols * n_tgt) / scale
    n_pairs = n_tgt // 2
    row_vec = jax.ShapeDtypeStruct((rows // LANES, LANES), F32)
    pair_vec = jax.ShapeDtypeStruct((1, 2 * cols), F32)
    mac = rows * cols * width

    source, left, turned, right, plain = call(
        functools.partial(prepare, scale),
        "prepare",
        (
            jax.ShapeDtypeStruct((rows, width), BF16),
            jax.ShapeDtypeStruct((rows, width), BF16),
            jax.ShapeDtypeStruct((width, rows), BF16),
            jax.ShapeDtypeStruct((cols, width + LANES), BF16),
            jax.ShapeDtypeStruct((cols, width), F32),
        ),
        scratch=[
            pltpu.VMEM((width, width), F32),
            pltpu.VMEM((cols, width), BF16),
            pltpu.VMEM((1, cols), F32),
            pltpu.SemaphoreType.DMA((4,)),
        ],
        flops=2 * rows * width * width,
        space=pltpu.HBM,
    )(*[pltpu.with_memory_space_constraint(x, pltpu.HBM) for x in (source, start_map, target, warm_potential.reshape(1, cols))])
    other = lax.ppermute(plain, "tgt", [(me, me ^ 1) for me in range(n_tgt)])
    lse = call(
        functools.partial(row_first, unit),
        "row_first",
        row_vec,
        scratch=[
            pltpu.VMEM((rows, cols), F32),
            pltpu.VMEM((rows, LANES), F32),
            pltpu.VMEM((rows, LANES), F32),
            pltpu.VMEM(row_vec.shape, F32),
        ],
        flops=4 * mac,
    )(left, right)
    block, targets, row_pot, peak, lse = call(
        functools.partial(col_first, n_tgt, unit, log_rows),
        "col_first",
        (
            jax.ShapeDtypeStruct((2 * cols, rows), BF16),
            jax.ShapeDtypeStruct((2 * cols, width), BF16),
            row_vec,
            pair_vec,
            pair_vec,
        ),
        scratch=[
            pltpu.VMEM((width + LANES, rows), BF16),
            pltpu.VMEM((2 * cols, width + LANES), BF16),
            pltpu.VMEM((CHUNK, rows), F32),
            pltpu.VMEM((CHUNK, rows), F32),
        ],
        flops=8 * mac,
    )(turned, right, other, over_tgt(lse))
    col_pot, col_scale, sums = call(
        functools.partial(row_second, n_src, unit, log_cols), "row_second", (pair_vec, pair_vec, row_vec), flops=4 * mac
    )(block, peak, *over_src(lse))
    col_later_call = call(
        functools.partial(col_later, n_pairs, ratio),
        "col_later",
        pair_vec,
        flops=4 * mac,
    )
    sums = col_later_call(block, col_scale, *over_pairs(sums))
    sums = call(functools.partial(row_later, n_src), "row_later", row_vec, flops=4 * mac)(
        block, col_scale, *over_src(sums)
    )
    sums = col_later_call(block, col_scale, *over_pairs(sums))
    col_totals, factor, sums = call(
        functools.partial(row_last, n_src), "row_last", (pair_vec, pair_vec, row_vec), flops=4 * mac
    )(block, col_scale, *over_src(sums))
    bary, col_out = call(
        functools.partial(barycentre, unit),
        "barycentre",
        (jax.ShapeDtypeStruct((width, rows), F32), jax.ShapeDtypeStruct((1, cols), F32)),
        flops=4 * mac,
    )(block, factor, targets, col_pot, col_totals)
    square = jax.ShapeDtypeStruct((width, width), F32)
    share_shape = jax.ShapeDtypeStruct((width // n_src, width), F32)
    row_totals, *shares = call(
        functools.partial(cross_local, n_pairs),
        "cross_local",
        (row_vec,) + (share_shape,) * n_src,
        scratch=[pltpu.VMEM((width, width), F32)],
        flops=2 * rows * width * width,
    )(source, bary, *over_pairs(sums))
    row_out = call(functools.partial(row_potential, unit, ratio), "row_potential", row_vec, flops=mac)(row_pot, row_totals)
    share = call(share_sum, "share_sum", share_shape)(*partners(shares[::-1], "src", range(n_src - 1, -1, -1)))
    share = call(share_sum, "share_sum", share_shape)(*over_pairs(share))
    new_map = call(polar, "polar", square, scratch=[pltpu.VMEM((width, width), F32)], flops=1 << 27)(*over_src(share))
    return row_out.reshape(rows), col_out.reshape(cols), new_map


def solution(mesh):
    placed = (P("src", None), P("tgt", None), P(), P("tgt"))
    return jax.shard_map(
        shards, mesh=mesh, in_specs=placed, out_specs=(P("src"), P("tgt"), P()), check_vma=False
    )
```

```python
import functools
import math

import jax
import jax.numpy as jnp
from jax import lax
from jax.experimental import pallas as pl
from jax.experimental.pallas import tpu as pltpu
from jax.sharding import PartitionSpec as P

NEWTON = 10
EPS = 0.05
LANES = 128
CHUNK = 256
VMEM_LIMIT = 40 * 1024 * 1024

F32 = jnp.float32
BF16 = jnp.bfloat16


def call(body, name, out_shape, scratch=(), flops=0, space=pltpu.VMEM):
    return lambda *args: pl.pallas_call(
        body,
        name=name,
        out_shape=out_shape,
        in_specs=[pl.BlockSpec(memory_space=space)] * len(args),
        out_specs=jax.tree.map(lambda _: pl.BlockSpec(memory_space=pltpu.VMEM), out_shape),
        scratch_shapes=scratch,
        compiler_params=pltpu.CompilerParams(vmem_limit_bytes=VMEM_LIMIT),
        cost_estimate=pl.CostEstimate(flops=flops, bytes_accessed=8 << 20, transcendentals=0),
    )(*args)


def eye_mask():
    row, lane = (lax.broadcasted_iota(jnp.int32, (LANES, LANES), k) for k in range(2))
    return row == lane


def to_lanes(column):
    wide = jnp.broadcast_to(column, (LANES, LANES))
    return jnp.sum(jnp.where(eye_mask(), wide, 0.0), axis=0, keepdims=True)


def to_column(row):
    wide = jnp.broadcast_to(row, (LANES, LANES))
    return jnp.broadcast_to(jnp.sum(jnp.where(eye_mask(), wide, 0.0), axis=1, keepdims=True), (LANES, LANES))


def split(x):
    high = x.astype(BF16)
    return high, (x - high.astype(F32)).astype(BF16)


def lane_parts(wide):
    lane = lax.broadcasted_iota(jnp.int32, wide.shape, 1)
    rest = wide
    out = jnp.zeros_like(wide)
    for k in range(3):
        part = rest.astype(BF16).astype(F32)
        out = jnp.where(lane == k, part, out)
        rest = rest - part
    return out.astype(BF16)


def tree(combine, values):
    values = list(values)
    while len(values) > 1:
        values = [combine(a, b) for a, b in zip(values[::2], values[1::2])]
    return values[0]


def tree_sum(parts):
    return tree(jnp.add, parts)


def tree_lse(unit, parts):
    peak = tree(jnp.maximum, parts)
    total = tree(jnp.add, [jnp.exp2(unit * (part - peak)) for part in parts])
    return peak + jnp.log(total) * (1.0 / (unit * math.log(2.0)))


def received(refs, group):
    if len(refs[0].shape) == 3:
        return [refs[0][k] for k in range(group)], refs[1:]
    return [ref[...] for ref in refs[:group]], refs[group:]


def dot_t(a, b):
    return lax.dot_general(a, b, (((1,), (1,)), ((), ())), preferred_element_type=F32)


def prepare(
    scale, source_hbm, map_hbm, target_hbm, pot_hbm, source, left_out, right_out, plain_out,
    start_map, target, pot, sems,
):
    copies = [
        pltpu.make_async_copy(src, dst, sems.at[k])
        for k, (src, dst) in enumerate(
            [(source_hbm, source), (map_hbm, start_map), (target_hbm, target), (pot_hbm, pot)]
        )
    ]
    for copy in copies:
        copy.start()
    for copy in copies:
        copy.wait()
    width = source.shape[1]
    plain_out[...] = target[...].astype(F32)
    for part in range(target.shape[0] // LANES):
        at = pl.ds(part * LANES, LANES)
        right_out[at, :width] = target[at, :]
        right_out[at, width:] = lane_parts(to_column(pot[:, at] * (1.0 / scale)))
    left_out[...] = jnp.dot(source[...], start_map[...].astype(BF16), preferred_element_type=F32).astype(BF16)


def row_first(unit, left_in, right, lse_out, turned_out, work, peaks, totals, sums):
    rows = left_in.shape[0]
    lane = lax.broadcasted_iota(jnp.int32, (CHUNK, LANES), 1)
    ones = jnp.where(lane < 3, 1.0, 0.0).astype(BF16)
    group = 16
    for start in range(0, rows, CHUNK):
        left = jnp.concatenate([left_in[start : start + CHUNK, :], ones], axis=1)
        work[start : start + CHUNK, :] = dot_t(left, right[...])
        for at in range(start, start + CHUNK, group):
            tiles = [work[at : at + group, k : k + LANES] for k in range(0, work.shape[1], LANES)]
            peak = functools.reduce(jnp.maximum, tiles)
            peaks[at : at + group, :] = peak
            totals[at : at + group, :] = functools.reduce(jnp.add, [jnp.exp2((tile - peak) * unit) for tile in tiles])
        for at in range(start, start + CHUNK, LANES):
            turned_out[:, at : at + LANES] = left_in[at : at + LANES, :].T
    for part in range(rows // LANES):
        here = slice(part * LANES, (part + 1) * LANES)
        lane_peak = peaks[here, :]
        peak = jnp.max(lane_peak, axis=1, keepdims=True)
        total = jnp.sum(totals[here, :] * jnp.exp2((lane_peak - peak) * unit), axis=1, keepdims=True)
        lse_out[part : part + 1, :] = to_lanes(peak)
        sums[part : part + 1, :] = to_lanes(total)
    lse_out[...] = lse_out[...] + jnp.log(sums[...]) * (1.0 / (unit * math.log(2.0)))


def in_row(parts):
    return jnp.concatenate([parts[k : k + 1, :] for k in range(parts.shape[0])], axis=1)


def col_first(group, unit, log_rows, turned, own, other, *refs):
    parts, (block_out, target_out, pot_out, peak_out, lse_out, left, right, *work) = received(refs, group)
    row_pot = -log_rows - tree_lse(unit, parts)
    pot_out[...] = row_pot
    width, rows = turned.shape
    half = own.shape[0]
    cols = 2 * half
    odd = lax.axis_index("tgt") & 1
    right[pl.ds(pl.multiple_of(odd * half, half), half), :width] = own[:, :width]
    right[pl.ds(pl.multiple_of((1 - odd) * half, half), half), :width] = other[...].astype(BF16)
    target_out[...] = right[:, :width]
    lane = lax.broadcasted_iota(jnp.int32, (cols, LANES), 1)
    right[:, width:] = jnp.where(lane < 3, 1.0, 0.0).astype(BF16)
    left[:width, :] = turned[...]
    rest = in_row(row_pot)
    pieces = []
    for _ in range(3):
        pieces.append(rest.astype(BF16).astype(F32))
        rest = rest - pieces[-1]
    left[width:, :] = jnp.concatenate([*pieces, jnp.zeros((LANES - 3, rows), F32)], axis=0).astype(BF16)
    for start in range(0, cols, CHUNK):
        scores = work[start // CHUNK % 2]
        scores[...] = jnp.dot(right[start : start + CHUNK, :], left[...], preferred_element_type=F32)
        peaks, sums = [], []
        for at in range(0, CHUNK, 16):
            tiles = [scores[at : at + 16, k : k + LANES] for k in range(0, rows, LANES)]
            peaks.append(functools.reduce(jnp.maximum, tiles))
        peak = jnp.max(jnp.concatenate(peaks, axis=0), axis=1, keepdims=True)
        peak = jnp.broadcast_to(peak, (CHUNK, LANES))
        for at in range(0, CHUNK, 16):
            top = peak[at : at + 16]
            total = None
            for k in range(0, rows, LANES):
                value = jnp.exp2((scores[at : at + 16, k : k + LANES] - top) * unit)
                block_out[start + at : start + at + 16, k : k + LANES] = value.astype(BF16)
                total = value if total is None else total + value
            sums.append(total)
        total = jnp.sum(jnp.concatenate(sums, axis=0), axis=1, keepdims=True)
        for part in range(0, CHUNK, LANES):
            here = slice(start + part, start + part + LANES)
            peak_out[:, here] = to_lanes(peak[part : part + LANES])
            lse_out[:, here] = to_lanes(total[part : part + LANES])
    lse_out[...] = peak_out[...] + jnp.log(lse_out[...]) * (1.0 / (unit * math.log(2.0)))


def two_rows(row):
    high, low = split(row)
    zeros = jnp.zeros((14, row.shape[1]), F32)
    return jnp.concatenate([high.astype(F32), low.astype(F32), zeros], axis=0).astype(BF16)


def put_rows(out, start, row):
    for part in range(row.shape[1] // LANES):
        at = start // LANES + part
        out[at : at + 1, :] = row[:, part * LANES : (part + 1) * LANES]


def sums_down(block, row, out):
    rows, cols = block.shape
    cut = cols * 3 // 4 // LANES * LANES
    pair = two_rows(row)
    product = jnp.zeros((16, cut), F32)
    total = jnp.zeros((8, cols - cut), F32)
    for start in range(0, rows, CHUNK):
        product += jnp.dot(pair[:, start : start + CHUNK], block[start : start + CHUNK, :cut], preferred_element_type=F32)
        for part in range(start, start + CHUNK, LANES):
            column = to_column(row[:, part : part + LANES])
            for at in range(0, LANES, 16):
                factor = jnp.concatenate([column[at : at + 16]] * ((cols - cut) // LANES), axis=1)
                value = block[part + at : part + at + 16, cut:].astype(F32) * factor
                total = total + value[:8] + value[8:]
    put_rows(out, 0, jnp.concatenate([product[0:1] + product[1:2], jnp.sum(total, axis=0, keepdims=True)], axis=1))


def sums_across(block, row, out):
    rows, cols = block.shape
    cut = cols // 4 // LANES * LANES
    first = lax.broadcasted_iota(jnp.int32, (16, 2 * LANES), 0) == 0
    pair = jnp.concatenate([two_rows(row[:, :cut]), jnp.where(first, 1.0, 0.0).astype(BF16)], axis=1)
    tiles = [(at, jnp.broadcast_to(row[:, at : at + LANES], (16, LANES))) for at in range(cut, cols, LANES)]
    for start in range(0, rows, CHUNK):
        folded = []
        for here in range(start, start + CHUNK, 16):
            terms = [block[here : here + 16, at : at + LANES].astype(F32) * factor for at, factor in tiles]
            folded.append(functools.reduce(jnp.add, terms))
        folded = split(jnp.concatenate(folded, axis=0))
        both = dot_t(pair, jnp.concatenate([block[start : start + CHUNK, :cut], *folded], axis=1))
        out[:, start : start + CHUNK] = both[0:1] + both[1:2]


def row_second(group, unit, log_cols, block, peak, *refs):
    parts, (pot_out, scale_out, sums_out) = received(refs, group)
    lse = tree_lse(unit, parts)
    pot_out[...] = -log_cols - lse
    scale = jnp.exp2(unit * (peak[...] - lse))
    scale_out[...] = scale
    sums_down(block, scale, sums_out)


def col_later(group, ratio, block, scale, *refs):
    parts, (sums_out,) = received(refs, group)
    sums_across(block, in_row(ratio / tree_sum(parts)), sums_out)
    sums_out[...] *= scale[...]


def row_later(group, block, scale, *refs):
    parts, (sums_out,) = received(refs, group)
    sums_down(block, scale[...] / tree_sum(parts), sums_out)


def row_last(group, block, scale, *refs):
    parts, (totals_out, factor_out, sums_out) = received(refs, group)
    totals = tree_sum(parts)
    totals_out[...] = totals
    row = scale[...] / totals
    factor_out[...] = row
    sums_down(block, row, sums_out)


def barycentre(unit, block, factor, target, pot, totals, bary_out, col_out):
    pots = (EPS * math.log(2.0)) * (unit * pot[...] - jnp.log(totals[...]) * (1.0 / math.log(2.0)))
    half = col_out.shape[1]
    col_out[...] = jnp.where((lax.axis_index("tgt") & 1) == 0, pots[:, :half], pots[:, half:])
    pieces = []
    for at in range(0, target.shape[0], LANES):
        pieces.append((target[at : at + LANES, :].T.astype(F32) * factor[:, at : at + LANES]).astype(BF16))
    left = jnp.concatenate(pieces, axis=1)
    for start in range(0, block.shape[1], CHUNK):
        bary_out[:, start : start + CHUNK] = jnp.dot(
            left, block[:, start : start + CHUNK], preferred_element_type=F32
        )


def row_potential(unit, ratio, pot, totals, out):
    out[...] = (EPS * math.log(2.0)) * (unit * pot[...] + jnp.log(ratio / totals[...]) * (1.0 / math.log(2.0)))


def cross_local(group, source, bary, *refs):
    parts, (totals_out, *share_outs, square) = received(refs, group)
    totals = tree_sum(parts)
    totals_out[...] = totals
    inverse = in_row(1.0 / totals)
    both = jnp.concatenate(split(bary[...] * inverse), axis=0)
    cross = jnp.dot(both, source[...], preferred_element_type=F32)
    width = square.shape[0]
    square[...] = (cross[:width, :] + cross[width:, :]).T
    index = lax.axis_index("src")
    count = len(share_outs)
    height = width // count
    for k, out in zip(range(count - 1, -1, -1), share_outs):
        out[...] = square[pl.ds(pl.multiple_of((index ^ k) * height, height), height), :]


def share_sum(*refs):
    refs[-1][...] = tree_sum([ref[...] for ref in refs[:-1]])


def precise(a, b, axis=1):
    ah, al = split(a)
    bh, bl = split(b)
    return lax.dot_general(
        jnp.concatenate([ah, ah, al], axis=axis),
        jnp.concatenate([bh, bl, bh], axis=0),
        (((axis,), (0,)), ((), ())),
        preferred_element_type=F32,
    )


def polar(*refs):
    shares, (out, square) = refs[:-2], refs[-2:]
    index = lax.axis_index("src")
    height = shares[0].shape[0]
    for k, share in enumerate(shares):
        square[pl.ds(pl.multiple_of((index ^ k) * height, height), height), :] = share[...]
    cross = square[...]
    unity = jnp.where(eye_mask(), 1.0, 0.0)
    square_sum = jnp.sum(cross * cross) + 1e-06
    error = unity - precise(cross, cross, 0) / square_sum
    iterate = cross / jnp.sqrt(square_sum)
    size = error.shape[0]
    for step in range(NEWTON - 1):
        both = precise(jnp.concatenate([error, iterate], axis=0), error)
        iterate = iterate + 0.5 * both[size:]
        error = precise(both[:size], 0.75 * unity + 0.25 * error)
    out[...] = iterate + 0.5 * precise(iterate, error)


def partners(values, axis, order):
    size = lax.axis_size(axis)
    return [lax.ppermute(values[k], axis, [(me, me ^ k) for me in range(size)]) if k else values[0] for k in order]


def over_src(x):
    size = lax.axis_size("src")
    return partners([x] * size, "src", range(size))


def over_pairs(x):
    size = lax.axis_size("tgt")
    return partners([x] * size, "tgt", range(0, size, 2))


def over_tgt(x):
    return lax.all_to_all(jnp.broadcast_to(x, (lax.axis_size("tgt"),) + x.shape), "tgt", 0, 0)


def shards(source, target, start_map, warm_potential):
    rows, width = source.shape
    cols = target.shape[0]
    n_src, n_tgt = lax.axis_size("src"), lax.axis_size("tgt")
    ratio = (cols * n_tgt) / (rows * n_src)
    scale = 1.0 / (math.sqrt(width) * EPS)
    unit = scale / math.log(2.0)
    log_rows, log_cols = math.log(rows * n_src) / scale, math.log(cols * n_tgt) / scale
    n_pairs = n_tgt // 2
    row_vec = jax.ShapeDtypeStruct((rows // LANES, LANES), F32)
    pair_vec = jax.ShapeDtypeStruct((1, 2 * cols), F32)
    mac = rows * cols * width

    source, left, right, plain = call(
        functools.partial(prepare, scale),
        "prepare",
        (
            jax.ShapeDtypeStruct((rows, width), BF16),
            jax.ShapeDtypeStruct((rows, width), BF16),
            jax.ShapeDtypeStruct((cols, width + LANES), BF16),
            jax.ShapeDtypeStruct((cols, width), F32),
        ),
        scratch=[
            pltpu.VMEM((width, width), F32),
            pltpu.VMEM((cols, width), BF16),
            pltpu.VMEM((1, cols), F32),
            pltpu.SemaphoreType.DMA((4,)),
        ],
        flops=2 * rows * width * width,
        space=pltpu.HBM,
    )(*[pltpu.with_memory_space_constraint(x, pltpu.HBM) for x in (source, start_map, target, warm_potential.reshape(1, cols))])
    other = lax.ppermute(plain, "tgt", [(me, me ^ 1) for me in range(n_tgt)])
    lse, turned = call(
        functools.partial(row_first, unit),
        "row_first",
        (row_vec, jax.ShapeDtypeStruct((width, rows), BF16)),
        scratch=[
            pltpu.VMEM((rows, cols), F32),
            pltpu.VMEM((rows, LANES), F32),
            pltpu.VMEM((rows, LANES), F32),
            pltpu.VMEM(row_vec.shape, F32),
        ],
        flops=4 * mac,
    )(left, right)
    block, targets, row_pot, peak, lse = call(
        functools.partial(col_first, n_tgt, unit, log_rows),
        "col_first",
        (
            jax.ShapeDtypeStruct((2 * cols, rows), BF16),
            jax.ShapeDtypeStruct((2 * cols, width), BF16),
            row_vec,
            pair_vec,
            pair_vec,
        ),
        scratch=[
            pltpu.VMEM((width + LANES, rows), BF16),
            pltpu.VMEM((2 * cols, width + LANES), BF16),
            pltpu.VMEM((CHUNK, rows), F32),
            pltpu.VMEM((CHUNK, rows), F32),
        ],
        flops=8 * mac,
    )(turned, right, other, over_tgt(lse))
    col_pot, col_scale, sums = call(
        functools.partial(row_second, n_src, unit, log_cols), "row_second", (pair_vec, pair_vec, row_vec), flops=4 * mac
    )(block, peak, *over_src(lse))
    col_later_call = call(
        functools.partial(col_later, n_pairs, ratio),
        "col_later",
        pair_vec,
        flops=4 * mac,
    )
    sums = col_later_call(block, col_scale, *over_pairs(sums))
    sums = call(functools.partial(row_later, n_src), "row_later", row_vec, flops=4 * mac)(
        block, col_scale, *over_src(sums)
    )
    sums = col_later_call(block, col_scale, *over_pairs(sums))
    col_totals, factor, sums = call(
        functools.partial(row_last, n_src), "row_last", (pair_vec, pair_vec, row_vec), flops=4 * mac
    )(block, col_scale, *over_src(sums))
    bary, col_out = call(
        functools.partial(barycentre, unit),
        "barycentre",
        (jax.ShapeDtypeStruct((width, rows), F32), jax.ShapeDtypeStruct((1, cols), F32)),
        flops=4 * mac,
    )(block, factor, targets, col_pot, col_totals)
    square = jax.ShapeDtypeStruct((width, width), F32)
    share_shape = jax.ShapeDtypeStruct((width // n_src, width), F32)
    row_totals, *shares = call(
        functools.partial(cross_local, n_pairs),
        "cross_local",
        (row_vec,) + (share_shape,) * n_src,
        scratch=[pltpu.VMEM((width, width), F32)],
        flops=2 * rows * width * width,
    )(source, bary, *over_pairs(sums))
    row_out = call(functools.partial(row_potential, unit, ratio), "row_potential", row_vec, flops=mac)(row_pot, row_totals)
    share = call(share_sum, "share_sum", share_shape)(*partners(shares[::-1], "src", range(n_src - 1, -1, -1)))
    share = call(share_sum, "share_sum", share_shape)(*over_pairs(share))
    new_map = call(polar, "polar", square, scratch=[pltpu.VMEM((width, width), F32)], flops=1 << 27)(*over_src(share))
    return row_out.reshape(rows), col_out.reshape(cols), new_map


def solution(mesh):
    placed = (P("src", None), P("tgt", None), P(), P("tgt"))
    return jax.shard_map(
        shards, mesh=mesh, in_specs=placed, out_specs=(P("src"), P("tgt"), P()), check_vma=False
    )
```

```python
import functools
import math

import jax
import jax.numpy as jnp
from jax import lax
from jax.experimental import pallas as pl
from jax.experimental.pallas import tpu as pltpu
from jax.sharding import PartitionSpec as P

NEWTON = 10
EPS = 0.05
LANES = 128
CHUNK = 256
VMEM_LIMIT = 40 * 1024 * 1024

F32 = jnp.float32
BF16 = jnp.bfloat16


def call(body, name, out_shape, scratch=(), flops=0, space=pltpu.VMEM):
    return lambda *args: pl.pallas_call(
        body,
        name=name,
        out_shape=out_shape,
        in_specs=[pl.BlockSpec(memory_space=space)] * len(args),
        out_specs=jax.tree.map(lambda _: pl.BlockSpec(memory_space=pltpu.VMEM), out_shape),
        scratch_shapes=scratch,
        compiler_params=pltpu.CompilerParams(vmem_limit_bytes=VMEM_LIMIT),
        cost_estimate=pl.CostEstimate(flops=flops, bytes_accessed=8 << 20, transcendentals=0),
    )(*args)


def eye_mask():
    row, lane = (lax.broadcasted_iota(jnp.int32, (LANES, LANES), k) for k in range(2))
    return row == lane


def to_lanes(column):
    wide = jnp.broadcast_to(column, (LANES, LANES))
    return jnp.sum(jnp.where(eye_mask(), wide, 0.0), axis=0, keepdims=True)


def to_column(row):
    wide = jnp.broadcast_to(row, (LANES, LANES))
    return jnp.broadcast_to(jnp.sum(jnp.where(eye_mask(), wide, 0.0), axis=1, keepdims=True), (LANES, LANES))


def split(x):
    high = x.astype(BF16)
    return high, (x - high.astype(F32)).astype(BF16)


def lane_parts(wide):
    lane = lax.broadcasted_iota(jnp.int32, wide.shape, 1)
    rest = wide
    out = jnp.zeros_like(wide)
    for k in range(3):
        part = rest.astype(BF16).astype(F32)
        out = jnp.where(lane == k, part, out)
        rest = rest - part
    return out.astype(BF16)


def tree(combine, values):
    values = list(values)
    while len(values) > 1:
        values = [combine(a, b) for a, b in zip(values[::2], values[1::2])]
    return values[0]


def tree_sum(parts):
    return tree(jnp.add, parts)


def tree_lse(unit, parts):
    peak = tree(jnp.maximum, parts)
    total = tree(jnp.add, [jnp.exp2(unit * (part - peak)) for part in parts])
    return peak + jnp.log(total) * (1.0 / (unit * math.log(2.0)))


def received(refs, group):
    if len(refs[0].shape) == 3:
        return [refs[0][k] for k in range(group)], refs[1:]
    return [ref[...] for ref in refs[:group]], refs[group:]


def dot_t(a, b):
    return lax.dot_general(a, b, (((1,), (1,)), ((), ())), preferred_element_type=F32)


def prepare(
    scale, source_hbm, map_hbm, target_hbm, pot_hbm, source, left_out, right_out, plain_out,
    start_map, target, pot, sems,
):
    copies = [
        pltpu.make_async_copy(src, dst, sems.at[k])
        for k, (src, dst) in enumerate(
            [(source_hbm, source), (map_hbm, start_map), (target_hbm, target), (pot_hbm, pot)]
        )
    ]
    for copy in copies:
        copy.start()
    for copy in copies:
        copy.wait()
    width = source.shape[1]
    plain_out[...] = target[...].astype(F32)
    for part in range(target.shape[0] // LANES):
        at = pl.ds(part * LANES, LANES)
        right_out[at, :width] = target[at, :]
        right_out[at, width:] = lane_parts(to_column(pot[:, at] * (1.0 / scale)))
    left_out[...] = jnp.dot(source[...], start_map[...].astype(BF16), preferred_element_type=F32).astype(BF16)


def row_first(unit, left_in, right, lse_out, turned_out, work, peaks, totals, sums):
    rows = left_in.shape[0]
    lane = lax.broadcasted_iota(jnp.int32, (CHUNK, LANES), 1)
    ones = jnp.where(lane < 3, 1.0, 0.0).astype(BF16)
    group = 16
    for start in range(0, rows, CHUNK):
        left = jnp.concatenate([left_in[start : start + CHUNK, :], ones], axis=1)
        work[start : start + CHUNK, :] = dot_t(left, right[...])
        for at in range(start, start + CHUNK, group):
            tiles = [work[at : at + group, k : k + LANES] for k in range(0, work.shape[1], LANES)]
            peak = functools.reduce(jnp.maximum, tiles)
            peaks[at : at + group, :] = peak
            totals[at : at + group, :] = functools.reduce(jnp.add, [jnp.exp2((tile - peak) * unit) for tile in tiles])
        for at in range(start, start + CHUNK, LANES):
            turned_out[:, at : at + LANES] = left_in[at : at + LANES, :].T
    for part in range(rows // LANES):
        here = slice(part * LANES, (part + 1) * LANES)
        lane_peak = peaks[here, :]
        peak = jnp.max(lane_peak, axis=1, keepdims=True)
        total = jnp.sum(totals[here, :] * jnp.exp2((lane_peak - peak) * unit), axis=1, keepdims=True)
        lse_out[part : part + 1, :] = to_lanes(peak)
        sums[part : part + 1, :] = to_lanes(total)
    lse_out[...] = lse_out[...] + jnp.log(sums[...]) * (1.0 / (unit * math.log(2.0)))


def in_row(parts):
    return jnp.concatenate([parts[k : k + 1, :] for k in range(parts.shape[0])], axis=1)


def col_first(group, unit, log_rows, turned, own, other, *refs):
    parts, (block_out, target_out, pot_out, peak_out, lse_out, left, right, *work) = received(refs, group)
    row_pot = -log_rows - tree_lse(unit, parts)
    pot_out[...] = row_pot
    width, rows = turned.shape
    half = own.shape[0]
    cols = 2 * half
    odd = lax.axis_index("tgt") & 1
    right[pl.ds(pl.multiple_of(odd * half, half), half), :width] = own[:, :width]
    right[pl.ds(pl.multiple_of((1 - odd) * half, half), half), :width] = other[...].astype(BF16)
    target_out[...] = right[:, :width]
    lane = lax.broadcasted_iota(jnp.int32, (cols, LANES), 1)
    right[:, width:] = jnp.where(lane < 3, 1.0, 0.0).astype(BF16)
    left[:width, :] = turned[...]
    rest = in_row(row_pot)
    pieces = []
    for _ in range(3):
        pieces.append(rest.astype(BF16).astype(F32))
        rest = rest - pieces[-1]
    left[width:, :] = jnp.concatenate([*pieces, jnp.zeros((LANES - 3, rows), F32)], axis=0).astype(BF16)
    for start in range(0, cols, CHUNK):
        scores = work[start // CHUNK % 2]
        scores[...] = jnp.dot(right[start : start + CHUNK, :], left[...], preferred_element_type=F32)
        peaks, sums = [], []
        for at in range(0, CHUNK, 16):
            tiles = [scores[at : at + 16, k : k + LANES] for k in range(0, rows, LANES)]
            peaks.append(functools.reduce(jnp.maximum, tiles))
        peak = jnp.max(jnp.concatenate(peaks, axis=0), axis=1, keepdims=True)
        peak = jnp.broadcast_to(peak, (CHUNK, LANES))
        for at in range(0, CHUNK, 16):
            top = peak[at : at + 16]
            total = None
            for k in range(0, rows, LANES):
                value = jnp.exp2((scores[at : at + 16, k : k + LANES] - top) * unit)
                block_out[start + at : start + at + 16, k : k + LANES] = value.astype(BF16)
                total = value if total is None else total + value
            sums.append(total)
        total = jnp.sum(jnp.concatenate(sums, axis=0), axis=1, keepdims=True)
        for part in range(0, CHUNK, LANES):
            here = slice(start + part, start + part + LANES)
            peak_out[:, here] = to_lanes(peak[part : part + LANES])
            lse_out[:, here] = to_lanes(total[part : part + LANES])
    lse_out[...] = peak_out[...] + jnp.log(lse_out[...]) * (1.0 / (unit * math.log(2.0)))


def two_rows(row):
    high, low = split(row)
    zeros = jnp.zeros((14, row.shape[1]), F32)
    return jnp.concatenate([high.astype(F32), low.astype(F32), zeros], axis=0).astype(BF16)


def put_rows(out, start, row):
    for part in range(row.shape[1] // LANES):
        at = start // LANES + part
        out[at : at + 1, :] = row[:, part * LANES : (part + 1) * LANES]


def sums_down(block, row, out):
    rows, cols = block.shape
    cut = cols * 5 // 8 // LANES * LANES
    pair = two_rows(row)
    product = jnp.zeros((16, cut), F32)
    total = jnp.zeros((8, cols - cut), F32)
    for start in range(0, rows, CHUNK):
        product += jnp.dot(pair[:, start : start + CHUNK], block[start : start + CHUNK, :cut], preferred_element_type=F32)
        for part in range(start, start + CHUNK, LANES):
            column = to_column(row[:, part : part + LANES])
            for at in range(0, LANES, 16):
                factor = jnp.concatenate([column[at : at + 16]] * ((cols - cut) // LANES), axis=1)
                value = block[part + at : part + at + 16, cut:].astype(F32) * factor
                total = total + value[:8] + value[8:]
    put_rows(out, 0, jnp.concatenate([product[0:1] + product[1:2], jnp.sum(total, axis=0, keepdims=True)], axis=1))


def sums_across(block, row, out):
    rows, cols = block.shape
    cut = cols * 3 // 8 // LANES * LANES
    first = lax.broadcasted_iota(jnp.int32, (16, 2 * LANES), 0) == 0
    pair = jnp.concatenate([two_rows(row[:, :cut]), jnp.where(first, 1.0, 0.0).astype(BF16)], axis=1)
    tiles = [(at, jnp.broadcast_to(row[:, at : at + LANES], (16, LANES))) for at in range(cut, cols, LANES)]
    for start in range(0, rows, CHUNK):
        folded = []
        for here in range(start, start + CHUNK, 16):
            terms = [block[here : here + 16, at : at + LANES].astype(F32) * factor for at, factor in tiles]
            folded.append(functools.reduce(jnp.add, terms))
        folded = split(jnp.concatenate(folded, axis=0))
        both = dot_t(pair, jnp.concatenate([block[start : start + CHUNK, :cut], *folded], axis=1))
        out[:, start : start + CHUNK] = both[0:1] + both[1:2]


def row_second(group, unit, log_cols, block, peak, *refs):
    parts, (pot_out, scale_out, sums_out) = received(refs, group)
    lse = tree_lse(unit, parts)
    pot_out[...] = -log_cols - lse
    scale = jnp.exp2(unit * (peak[...] - lse))
    scale_out[...] = scale
    sums_down(block, scale, sums_out)


def col_later(group, ratio, block, scale, *refs):
    parts, (sums_out,) = received(refs, group)
    sums_across(block, in_row(ratio / tree_sum(parts)), sums_out)
    sums_out[...] *= scale[...]


def row_later(group, block, scale, *refs):
    parts, (sums_out,) = received(refs, group)
    sums_down(block, scale[...] / tree_sum(parts), sums_out)


def row_last(group, block, scale, *refs):
    parts, (totals_out, factor_out, sums_out) = received(refs, group)
    totals = tree_sum(parts)
    totals_out[...] = totals
    row = scale[...] / totals
    factor_out[...] = row
    sums_down(block, row, sums_out)


def barycentre(unit, block, factor, target, pot, totals, bary_out, col_out):
    pots = (EPS * math.log(2.0)) * (unit * pot[...] - jnp.log(totals[...]) * (1.0 / math.log(2.0)))
    half = col_out.shape[1]
    col_out[...] = jnp.where((lax.axis_index("tgt") & 1) == 0, pots[:, :half], pots[:, half:])
    pieces = []
    for at in range(0, target.shape[0], LANES):
        pieces.append((target[at : at + LANES, :].T.astype(F32) * factor[:, at : at + LANES]).astype(BF16))
    left = jnp.concatenate(pieces, axis=1)
    for start in range(0, block.shape[1], CHUNK):
        bary_out[:, start : start + CHUNK] = jnp.dot(
            left, block[:, start : start + CHUNK], preferred_element_type=F32
        )


def row_potential(unit, ratio, pot, totals, out):
    out[...] = (EPS * math.log(2.0)) * (unit * pot[...] + jnp.log(ratio / totals[...]) * (1.0 / math.log(2.0)))


def cross_local(group, source, bary, *refs):
    parts, (totals_out, *share_outs, square) = received(refs, group)
    totals = tree_sum(parts)
    totals_out[...] = totals
    inverse = in_row(1.0 / totals)
    both = jnp.concatenate(split(bary[...] * inverse), axis=0)
    cross = jnp.dot(both, source[...], preferred_element_type=F32)
    width = square.shape[0]
    square[...] = (cross[:width, :] + cross[width:, :]).T
    index = lax.axis_index("src")
    count = len(share_outs)
    height = width // count
    for k, out in zip(range(count - 1, -1, -1), share_outs):
        out[...] = square[pl.ds(pl.multiple_of((index ^ k) * height, height), height), :]


def share_sum(*refs):
    refs[-1][...] = tree_sum([ref[...] for ref in refs[:-1]])


def precise(a, b, axis=1):
    ah, al = split(a)
    bh, bl = split(b)
    return lax.dot_general(
        jnp.concatenate([ah, ah, al], axis=axis),
        jnp.concatenate([bh, bl, bh], axis=0),
        (((axis,), (0,)), ((), ())),
        preferred_element_type=F32,
    )


def polar(*refs):
    shares, (out, square) = refs[:-2], refs[-2:]
    index = lax.axis_index("src")
    height = shares[0].shape[0]
    for k, share in enumerate(shares):
        square[pl.ds(pl.multiple_of((index ^ k) * height, height), height), :] = share[...]
    cross = square[...]
    unity = jnp.where(eye_mask(), 1.0, 0.0)
    square_sum = jnp.sum(cross * cross) + 1e-06
    error = unity - precise(cross, cross, 0) / square_sum
    iterate = cross / jnp.sqrt(square_sum)
    size = error.shape[0]
    for step in range(NEWTON - 1):
        both = precise(jnp.concatenate([error, iterate], axis=0), error)
        iterate = iterate + 0.5 * both[size:]
        error = precise(both[:size], 0.75 * unity + 0.25 * error)
    out[...] = iterate + 0.5 * precise(iterate, error)


def partners(values, axis, order):
    size = lax.axis_size(axis)
    return [lax.ppermute(values[k], axis, [(me, me ^ k) for me in range(size)]) if k else values[0] for k in order]


def over_src(x):
    size = lax.axis_size("src")
    return partners([x] * size, "src", range(size))


def over_pairs(x):
    size = lax.axis_size("tgt")
    return partners([x] * size, "tgt", range(0, size, 2))


def over_tgt(x):
    return lax.all_to_all(jnp.broadcast_to(x, (lax.axis_size("tgt"),) + x.shape), "tgt", 0, 0)


def shards(source, target, start_map, warm_potential):
    rows, width = source.shape
    cols = target.shape[0]
    n_src, n_tgt = lax.axis_size("src"), lax.axis_size("tgt")
    ratio = (cols * n_tgt) / (rows * n_src)
    scale = 1.0 / (math.sqrt(width) * EPS)
    unit = scale / math.log(2.0)
    log_rows, log_cols = math.log(rows * n_src) / scale, math.log(cols * n_tgt) / scale
    n_pairs = n_tgt // 2
    row_vec = jax.ShapeDtypeStruct((rows // LANES, LANES), F32)
    pair_vec = jax.ShapeDtypeStruct((1, 2 * cols), F32)
    mac = rows * cols * width

    source, left, right, plain = call(
        functools.partial(prepare, scale),
        "prepare",
        (
            jax.ShapeDtypeStruct((rows, width), BF16),
            jax.ShapeDtypeStruct((rows, width), BF16),
            jax.ShapeDtypeStruct((cols, width + LANES), BF16),
            jax.ShapeDtypeStruct((cols, width), F32),
        ),
        scratch=[
            pltpu.VMEM((width, width), F32),
            pltpu.VMEM((cols, width), BF16),
            pltpu.VMEM((1, cols), F32),
            pltpu.SemaphoreType.DMA((4,)),
        ],
        flops=2 * rows * width * width,
        space=pltpu.HBM,
    )(*[pltpu.with_memory_space_constraint(x, pltpu.HBM) for x in (source, start_map, target, warm_potential.reshape(1, cols))])
    other = lax.ppermute(plain, "tgt", [(me, me ^ 1) for me in range(n_tgt)])
    lse, turned = call(
        functools.partial(row_first, unit),
        "row_first",
        (row_vec, jax.ShapeDtypeStruct((width, rows), BF16)),
        scratch=[
            pltpu.VMEM((rows, cols), F32),
            pltpu.VMEM((rows, LANES), F32),
            pltpu.VMEM((rows, LANES), F32),
            pltpu.VMEM(row_vec.shape, F32),
        ],
        flops=4 * mac,
    )(left, right)
    block, targets, row_pot, peak, lse = call(
        functools.partial(col_first, n_tgt, unit, log_rows),
        "col_first",
        (
            jax.ShapeDtypeStruct((2 * cols, rows), BF16),
            jax.ShapeDtypeStruct((2 * cols, width), BF16),
            row_vec,
            pair_vec,
            pair_vec,
        ),
        scratch=[
            pltpu.VMEM((width + LANES, rows), BF16),
            pltpu.VMEM((2 * cols, width + LANES), BF16),
            pltpu.VMEM((CHUNK, rows), F32),
            pltpu.VMEM((CHUNK, rows), F32),
        ],
        flops=8 * mac,
    )(turned, right, other, over_tgt(lse))
    col_pot, col_scale, sums = call(
        functools.partial(row_second, n_src, unit, log_cols), "row_second", (pair_vec, pair_vec, row_vec), flops=4 * mac
    )(block, peak, *over_src(lse))
    col_later_call = call(
        functools.partial(col_later, n_pairs, ratio),
        "col_later",
        pair_vec,
        flops=4 * mac,
    )
    sums = col_later_call(block, col_scale, *over_pairs(sums))
    sums = call(functools.partial(row_later, n_src), "row_later", row_vec, flops=4 * mac)(
        block, col_scale, *over_src(sums)
    )
    sums = col_later_call(block, col_scale, *over_pairs(sums))
    col_totals, factor, sums = call(
        functools.partial(row_last, n_src), "row_last", (pair_vec, pair_vec, row_vec), flops=4 * mac
    )(block, col_scale, *over_src(sums))
    bary, col_out = call(
        functools.partial(barycentre, unit),
        "barycentre",
        (jax.ShapeDtypeStruct((width, rows), F32), jax.ShapeDtypeStruct((1, cols), F32)),
        flops=4 * mac,
    )(block, factor, targets, col_pot, col_totals)
    square = jax.ShapeDtypeStruct((width, width), F32)
    share_shape = jax.ShapeDtypeStruct((width // n_src, width), F32)
    row_totals, *shares = call(
        functools.partial(cross_local, n_pairs),
        "cross_local",
        (row_vec,) + (share_shape,) * n_src,
        scratch=[pltpu.VMEM((width, width), F32)],
        flops=2 * rows * width * width,
    )(source, bary, *over_pairs(sums))
    row_out = call(functools.partial(row_potential, unit, ratio), "row_potential", row_vec, flops=mac)(row_pot, row_totals)
    share = call(share_sum, "share_sum", share_shape)(*partners(shares[::-1], "src", range(n_src - 1, -1, -1)))
    share = call(share_sum, "share_sum", share_shape)(*over_pairs(share))
    new_map = call(polar, "polar", square, scratch=[pltpu.VMEM((width, width), F32)], flops=1 << 27)(*over_src(share))
    return row_out.reshape(rows), col_out.reshape(cols), new_map


def solution(mesh):
    placed = (P("src", None), P("tgt", None), P(), P("tgt"))
    return jax.shard_map(
        shards, mesh=mesh, in_specs=placed, out_specs=(P("src"), P("tgt"), P()), check_vma=False
    )
```
